32 devices in a mesh: dp: 8 (over z, x), group: 4 (over y, core).
Axes of the slice: x: 2, y: 2, z: 4, core: 2. Of those that a mesh axis runs over, the one named last changes fastest.
Arguments:
- hidden_in: bfloat16 [16, 1024, 1024], P('dp', 'group'), may hold values from -6 to 6
- out_grad: bfloat16 [16, 1024, 1024], P('dp', 'group'), may hold values from -6 to 6
- stretch_order: int32 [8], replicated, may hold values from 0 to 7, as said below
- positions: int32 [16, 1024], P('dp', 'group'), may hold values from 0 to 5118, as said below
- qkv_weight: float32 [1024, 4096], P('group'), may hold values from -0.1875 to 0.1875
- qkv_moment: float32 [1024, 4096], P('group'), may hold values from -128 to 128
- qkv_square: float32 [1024, 4096], P('group'), may hold values from 861.7984 to 13762.56
- out_weight: float32 [2048, 1024], P('group'), may hold values from -1.5 to 1.5
- out_moment: float32 [2048, 1024], P('group'), may hold values from -6 to 6
- out_square: float32 [2048, 1024], P('group'), may hold values from 2.944 to 47.2
- gateup_weight: float32 [1024, 6144], P('group'), may hold values from -0.1875 to 0.1875
- gateup_moment: float32 [1024, 6144], P('group'), may hold values from -48 to 48
- gateup_square: float32 [1024, 6144], P('group'), may hold values from 129.4336 to 2064.384
- down_weight: float32 [3072, 1024], P('group'), may hold values from -0.109375 to 0.109375
- down_moment: float32 [3072, 1024], P('group'), may hold values from -48 to 48
- down_square: float32 [3072, 1024], P('group'), may hold values from 155.648 to 2490.368
- gain_weight: float32 [2304], P('group'), may hold values from 0.5 to 1.5
- gain_moment: float32 [2304], P('group'), may hold values from -246.1863 to 246.1863
- gain_square: float32 [2304], P('group'), may hold values from 655.36 to 221184
Outputs:
- layer_out: bfloat16 [16, 1024, 1024], P('dp', 'group')
- input_grad: bfloat16 [16, 1024, 1024], P('dp', 'group')
- qkv_new: float32 [1024, 4096], P('group')
- qkv_moment_new: float32 [1024, 4096], P('group')
- qkv_square_new: float32 [1024, 4096], P('group')
- out_new: float32 [2048, 1024], P('group')
- out_moment_new: float32 [2048, 1024], P('group')
- out_square_new: float32 [2048, 1024], P('group')
- gateup_new: float32 [1024, 6144], P('group')
- gateup_moment_new: float32 [1024, 6144], P('group')
- gateup_square_new: float32 [1024, 6144], P('group')
- down_new: float32 [3072, 1024], P('group')
- down_moment_new: float32 [3072, 1024], P('group')
- down_square_new: float32 [3072, 1024], P('group')
- gain_new: float32 [2304], P('group')
- gain_moment_new: float32 [2304], P('group')
- gain_square_new: float32 [2304], P('group')
The draws below stay inside these ranges and needn't reach their ends.
Inputs may be any that keep to these rules, and one draw needn't show every extreme that they name: `stretch_order`: A permutation in which stored pieces 2 i and 2 i + 1 hold pieces that add up to 7. positions[b, p] = start of sequence b plus the place of stored token p; starts are below 4096, one sequence starts at 0 and one at 4095.
All inputs are finite; a program needn't handle non-finite values.
Results may differ from the reference program's by a relative error of at most 0.02.
Values may be sent and summed in bfloat16 or wider, within the bound.
No kernel may reach another device: no remote copies, remote signals or barrier semaphores. Data moves between devices by JAX's collectives and lax.ppermute only.
A program may use at most 256 MiB of HBM per device.

```python
import math
import jax
import jax.numpy as jnp
from jax import lax

D = 1024
H = 16
KV = 8
HD = 128
FF = 3072
STEP = 10
POS_SPAN = 4096
LEN = 1024
STRETCHES = 8
CH = 128
BATCH = 16
TOKENS = 16384
QKV = 4096
HQD = 2048
GAINS = 2304
OUT_FAN = 16


def stretch_pairs(key):
    pairs = STRETCHES // 2
    picked = jax.random.permutation(jax.random.fold_in(key, 101), pairs).astype(jnp.int32)
    flips = jax.random.randint(jax.random.fold_in(key, 102), (pairs,), 0, 2)
    first = jnp.where(flips == 1, picked, STRETCHES - 1 - picked)
    second = STRETCHES - 1 - first
    return jnp.stack([first, second], axis=1).reshape(STRETCHES).astype(jnp.int32)


def draw_stretch_order(key, part):
    return stretch_pairs(key)


def draw_positions(key, part):
    stretch_list = stretch_pairs(key)
    key = jax.random.fold_in(key, 7)
    stored = jnp.arange(LEN, dtype=jnp.int32)
    places = stretch_list[stored // CH] * CH + stored % CH
    ordering = jax.random.permutation(jax.random.fold_in(key, 1), BATCH).astype(jnp.int32)
    starts = jax.random.randint(jax.random.fold_in(key, 2), (BATCH,), 0, POS_SPAN)
    starts = jnp.where(ordering == 0, 0, jnp.where(ordering == 1, POS_SPAN - 1, starts))
    return (starts[:, None] + places[None, :]).astype(jnp.int32)


def gain_scales():
    pieces = [jnp.full((D,), 9.0), jnp.full((D,), 1.8), jnp.full((HD,), 16.0), jnp.full((HD,), 32.0)]
    return jnp.concatenate(pieces).astype(jnp.float32) * TOKENS


def draw_gain_moment(key, part):
    key = jax.random.fold_in(key, 31)
    noise = jax.random.truncated_normal(key, -3.0, 3.0, (GAINS,), jnp.float32)
    return (0.111 * jnp.sqrt(gain_scales()) * noise).astype(jnp.float32)


def draw_gain_square(key, part):
    key = jax.random.fold_in(key, 41)
    spread = jax.random.uniform(key, (GAINS,), jnp.float32, jnp.log(0.5), jnp.log(8.0))
    return (0.0526 * gain_scales() * jnp.exp(spread)).astype(jnp.float32)


def block_levels(key, shape, cuts, least, largest):
    level = 1.0
    for position, shards_of in cuts:
        steps = jax.random.uniform(jax.random.fold_in(jax.random.fold_in(key, 6), position), (shards_of,), jnp.float32, least / len(cuts), largest / len(cuts))
        level = level * jnp.repeat(jnp.exp(steps), shape[position] // shards_of).reshape((-1,) + (1,) * (len(shape) - 1 - position))
    return level


def bell_draw(rng, extent, scale, most, split=(), kind=jnp.bfloat16):
    drawn = scale * jax.random.normal(rng, extent, jnp.float32)
    if split:
        drawn = drawn * block_levels(rng, extent, split, -0.22, 0.18)
    return jnp.clip(drawn, -most, most).astype(kind)


def setup_inputs(seed: int = 0) -> dict:
    key_of = jax.random.split(jax.random.key(seed), 20)
    hidden_in = bell_draw(key_of[0], (BATCH, LEN, D), 1.0, 6.0, ((0, 8), (1, 4)))
    out_grad = bell_draw(key_of[1], (BATCH, LEN, D), 1.0, 6.0, ((0, 8), (1, 4)))
    stretch_order = draw_stretch_order(jax.random.fold_in(key_of[19], 71), 0)
    positions = draw_positions(jax.random.fold_in(key_of[19], 71), 0)
    qkv_weight = bell_draw(key_of[4], (D, QKV), D ** -0.5, 0.1875, ((0, 4),), jnp.float32)
    qkv_moment = bell_draw(key_of[5], (D, QKV), (0.157 * TOKENS ** 0.5), 128.0, ((0, 4),), jnp.float32)
    qkv_square = jnp.clip(jnp.exp(math.log(13762.56) - 2.7706857 * jax.random.uniform(key_of[6], (D, QKV), jnp.float32) ** block_levels(key_of[6], (D, QKV), ((0, 4),), -0.2, 0.2)), 861.7984, 13762.56)
    out_weight = bell_draw(key_of[7], (HQD, D), OUT_FAN ** -0.5, 1.5, ((0, 4),), jnp.float32)
    out_moment = bell_draw(key_of[8], (HQD, D), (0.294 * BATCH ** 0.5), 6.0, ((0, 4),), jnp.float32)
    out_square = jnp.clip(jnp.exp(math.log(47.2) - 2.77462471 * jax.random.uniform(key_of[9], (HQD, D), jnp.float32) ** block_levels(key_of[9], (HQD, D), ((0, 4),), -0.2, 0.2)), 2.944, 47.2)
    gateup_weight = bell_draw(key_of[10], (D, 2 * FF), D ** -0.5, 0.1875, ((0, 4),), jnp.float32)
    gateup_moment = bell_draw(key_of[11], (D, 2 * FF), (0.061 * TOKENS ** 0.5), 48.0, ((0, 4),), jnp.float32)
    gateup_square = jnp.clip(jnp.exp(math.log(2064.384) - 2.7694192 * jax.random.uniform(key_of[12], (D, 2 * FF), jnp.float32) ** block_levels(key_of[12], (D, 2 * FF), ((0, 4),), -0.2, 0.2)), 129.4336, 2064.384)
    down_weight = bell_draw(key_of[13], (FF, D), FF ** -0.5, 0.109375, ((0, 4),), jnp.float32)
    down_moment = bell_draw(key_of[14], (FF, D), (0.067 * TOKENS ** 0.5), 48.0, ((0, 4),), jnp.float32)
    down_square = jnp.clip(jnp.exp(math.log(2490.368) - 2.7725887 * jax.random.uniform(key_of[15], (FF, D), jnp.float32) ** block_levels(key_of[15], (FF, D), ((0, 4),), -0.2, 0.2)), 155.648, 2490.368)
    gain_weight = jnp.clip(1.0 + 0.1 * jax.random.normal(key_of[16], (GAINS,), jnp.float32), 0.5, 1.5)
    gain_moment = draw_gain_moment(jax.random.fold_in(key_of[19], 71), 0)
    gain_square = draw_gain_square(jax.random.fold_in(key_of[19], 71), 0)
    return {"hidden_in": hidden_in, "out_grad": out_grad, "stretch_order": stretch_order, "positions": positions, "qkv_weight": qkv_weight, "qkv_moment": qkv_moment, "qkv_square": qkv_square, "out_weight": out_weight, "out_moment": out_moment, "out_square": out_square, "gateup_weight": gateup_weight, "gateup_moment": gateup_moment, "gateup_square": gateup_square, "down_weight": down_weight, "down_moment": down_moment, "down_square": down_square, "gain_weight": gain_weight, "gain_moment": gain_moment, "gain_square": gain_square}


@jax.custom_vjp
def low(v):
    return lax.optimization_barrier(v.astype(jnp.bfloat16)).astype(jnp.float32)

@jax.custom_vjp
def low_back(v):
    return v

def low_keep(v):
    return (low(v), None)

def low_pass(kept, grad):
    return (grad,)

def back_keep(v):
    return (v, None)

def back_low(kept, grad):
    return (low(grad),)
low.defvjp(low_keep, low_pass)
low_back.defvjp(back_keep, back_low)
EPSILON = 1e-06
ROPE_BASE = 1000000.0
BETA_ONE = 0.9
BETA_TWO = 0.95
ADAM_EPSILON = 1e-08
DECAY = 0.1
LR_MULT = 3.0
GAIN_RATE = 0.3
MASKED = -1e+30
HIGHEST = lax.Precision.HIGHEST

def product(left, right):
    return jnp.dot(left, right, precision=HIGHEST, preferred_element_type=jnp.float32)

def rms_scale(values, gain):
    mean_square = lax.optimization_barrier(jnp.mean(values * values, axis=-1, keepdims=True))
    return values * lax.rsqrt(mean_square + EPSILON) * gain

def rotate(values, cosine, sine):
    half = values.shape[-1] // 2
    turned = jnp.concatenate([-values[..., half:], values[..., :half]], axis=-1)
    return values * cosine + turned * sine

def rope_tables(places):
    exponent = jnp.arange(HD // 2, dtype=jnp.float32) * (2.0 / HD)
    inverse = jnp.power(jnp.float32(ROPE_BASE), -exponent)
    angle = places.astype(jnp.float32)[:, None] * inverse[None, :]
    angle = jnp.concatenate([angle, angle], axis=-1)
    return (jnp.cos(angle), jnp.sin(angle))

def split_heads(mixed, query_gain, key_gain, cosine, sine):
    row_count = mixed.shape[0]
    query = mixed[:, :H * HD].reshape(row_count, H, HD)
    keys = mixed[:, H * HD:(H + KV) * HD].reshape(row_count, KV, HD)
    values = mixed[:, (H + KV) * HD:].reshape(row_count, KV, HD)
    query = rotate(rms_scale(query, query_gain), cosine[:, None, :], sine[:, None, :])
    keys = rotate(rms_scale(keys, key_gain), cosine[:, None, :], sine[:, None, :])
    return (query, keys, values)

def gated(gate_up):
    half = gate_up.shape[1] // 2
    return jax.nn.silu(gate_up[:, :half]) * gate_up[:, half:]

def attend(query, keys, values, places):
    length = query.shape[0]
    block = min(512, length)
    scale = HD ** (-0.5)
    starts = jnp.arange(length // block, dtype=jnp.int32) * block

    def one_block(start):
        rows_here = lax.dynamic_slice_in_dim(query, start, block, 0)
        row_places = lax.dynamic_slice_in_dim(places, start, block, 0)
        scores = jnp.einsum('qkrd,pkd->krqp', rows_here, keys, precision=HIGHEST) * scale
        scores = low_back(scores)
        allowed = places[None, :] <= row_places[:, None]
        scores = jnp.where(allowed, scores, MASKED)
        top = lax.optimization_barrier(jnp.max(scores, axis=-1, keepdims=True))
        total = jnp.log(lax.optimization_barrier(jnp.sum(jnp.exp(scores - top), axis=-1, keepdims=True))) + top
        weights = low(jnp.exp(scores - total))
        return jnp.einsum('krqp,pkd->qkrd', weights, values, precision=HIGHEST)
    outputs = lax.map(jax.checkpoint(one_block), starts)
    return outputs.reshape(length, H * HD)

def layer(params, hidden, cosine, sine, places):
    w_qkv, w_out, w_gateup, w_down, gains = params
    length = hidden.shape[0]
    gain_one = gains[:D]
    gain_two = gains[D:2 * D]
    gain_query = gains[2 * D:2 * D + HD]
    gain_key = gains[2 * D + HD:]
    normed = low(rms_scale(hidden, gain_one))
    mixed = low_back(product(normed, w_qkv))
    query, keys, values = split_heads(mixed, gain_query, gain_key, cosine, sine)
    query = low(query).reshape(length, KV, H // KV, HD)
    keys = low(keys)
    values = low(values)
    attended = low_back(low(attend(query, keys, values, places)))
    middle = hidden + low_back(product(attended, w_out))
    second = low(rms_scale(middle, gain_two))
    gate_up = low_back(product(second, w_gateup))
    inner = low(gated(gate_up))
    return middle + low_back(product(inner, w_down))

def adam_step(weight, moment, square, grad, rate, decay):
    moment_new = BETA_ONE * moment + (1.0 - BETA_ONE) * grad
    square_new = BETA_TWO * square + (1.0 - BETA_TWO) * grad * grad
    ratio = moment_new / (1.0 - BETA_ONE ** STEP) / (jnp.sqrt(square_new / (1.0 - BETA_TWO ** STEP)) + ADAM_EPSILON)
    return (weight - rate * (ratio + decay * weight), moment_new, square_new)

def reference(hidden_in, out_grad, stretch_order, positions, qkv_weight, qkv_moment, qkv_square, out_weight, out_moment, out_square, gateup_weight, gateup_moment, gateup_square, down_weight, down_moment, down_square, gain_weight, gain_moment, gain_square):
    masters = (qkv_weight, out_weight, gateup_weight, down_weight, gain_weight)
    params = tuple((master.astype(jnp.bfloat16).astype(jnp.float32) for master in masters))
    stored = jnp.arange(LEN, dtype=jnp.int32)
    places = (stretch_order[stored // CH] * CH + stored % CH).astype(jnp.int32)

    def per_sequence(sums, inputs):
        hidden, cotangent, where_at = inputs
        cosine, sine = rope_tables(where_at)

        def forward(weights, values):
            return layer(weights, values, cosine, sine, places)
        result, pullback = jax.vjp(forward, params, hidden.astype(jnp.float32))
        grads, grad_hidden = pullback(cotangent.astype(jnp.float32))
        sums = jax.tree.map(lambda first, second: first + second, sums, grads)
        return (sums, (result.astype(jnp.bfloat16), grad_hidden.astype(jnp.bfloat16)))
    zeros = tuple((jnp.zeros_like(param) for param in params))
    sums, (layer_out, input_grad) = lax.scan(per_sequence, zeros, (hidden_in, out_grad, positions))
    grad_qkv, grad_out, grad_gateup, grad_down, grad_gain = sums
    qkv_new = adam_step(qkv_weight, qkv_moment, qkv_square, grad_qkv, LR_MULT * D ** (-0.5), DECAY)
    out_new = adam_step(out_weight, out_moment, out_square, grad_out, LR_MULT * OUT_FAN ** (-0.5), DECAY)
    gateup_new = adam_step(gateup_weight, gateup_moment, gateup_square, grad_gateup, LR_MULT * D ** (-0.5), DECAY)
    down_new = adam_step(down_weight, down_moment, down_square, grad_down, LR_MULT * FF ** (-0.5), DECAY)
    gain_new = adam_step(gain_weight, gain_moment, gain_square, grad_gain, GAIN_RATE, 0.0)
    return (layer_out, input_grad, qkv_new[0], qkv_new[1], qkv_new[2], out_new[0], out_new[1], out_new[2], gateup_new[0], gateup_new[1], gateup_new[2], down_new[0], down_new[1], down_new[2], gain_new[0], gain_new[1], gain_new[2])
```

```python
import jax
import jax.numpy as jnp
from jax import lax
from jax.experimental import pallas as pl
from jax.experimental.pallas import tpu as pltpu
from jax.sharding import PartitionSpec as P

D = 1024
H = 16
KV = 8
HD = 128
FF = 3072
STEP = 10


EPSILON = 1e-06
ROPE_BASE = 1000000.0
BETA_ONE = 0.9
BETA_TWO = 0.95
ADAM_EPSILON = 1e-08
DECAY = 0.1
LR_MULT = 3.0
GAIN_RATE = 0.3
MASKED = -1e30
START_TOP = -1e29


def rms_scale(values, gain):
    mean_square = jnp.mean(values * values, axis=-1, keepdims=True)
    return values * lax.rsqrt(mean_square + EPSILON) * gain


def rotate(values, cosine, sine):
    half = values.shape[-1] // 2
    turned = jnp.concatenate([-values[..., half:], values[..., :half]], axis=-1)
    return values * cosine + turned * sine


def rope_tables(places):
    exponent = jnp.arange(HD // 2, dtype=jnp.float32) * (2.0 / HD)
    inverse = jnp.power(jnp.float32(ROPE_BASE), -exponent)
    angle = places.astype(jnp.float32)[:, None] * inverse[None, :]
    angle = jnp.concatenate([angle, angle], axis=-1)
    return (jnp.cos(angle), jnp.sin(angle))


def split_heads(mixed, query_gain, key_gain, cosine, sine):
    row_count = mixed.shape[0]
    query = mixed[:, : H * HD].reshape(row_count, H, HD)
    keys = mixed[:, H * HD : (H + KV) * HD].reshape(row_count, KV, HD)
    values = mixed[:, (H + KV) * HD :].reshape(row_count, KV, HD)
    query = rotate(rms_scale(query, query_gain), cosine[:, None, :], sine[:, None, :])
    keys = rotate(rms_scale(keys, key_gain), cosine[:, None, :], sine[:, None, :])
    return (query, keys, values)


def gated(gate_up):
    half = gate_up.shape[1] // 2
    return jax.nn.silu(gate_up[:, :half]) * gate_up[:, half:]


def real_places(stretch_list, start, count, half_stretch):
    stored = start + jnp.arange(count, dtype=jnp.int32)
    piece_index = stored // half_stretch
    table = jnp.arange(stretch_list.shape[0], dtype=jnp.int32)
    picked = jnp.sum(
        jnp.where(piece_index[:, None] == table[None, :], stretch_list[None, :], 0), axis=1
    )
    return picked * half_stretch + stored % half_stretch


def by_blocks(block_fn, carry, piece, width):
    count = piece[0].shape[1]

    def advance(state, number):
        sliced = tuple(
            (lax.dynamic_slice_in_dim(member, number * width, width, 1) for member in piece)
        )
        return (block_fn(state, sliced, number * width), None)

    state, unused = lax.scan(advance, carry, jnp.arange(count // width, dtype=jnp.int32))
    return state


def adam_step(weight, moment, square, grad, rate, decay):
    moment_new = BETA_ONE * moment + (1.0 - BETA_ONE) * grad
    square_new = BETA_TWO * square + (1.0 - BETA_TWO) * grad * grad
    ratio = (
        moment_new
        / (1.0 - BETA_ONE**STEP)
        / (jnp.sqrt(square_new / (1.0 - BETA_TWO**STEP)) + ADAM_EPSILON)
    )
    return (weight - rate * (ratio + decay * weight), moment_new, square_new)


def general_shards(
    hidden_in,
    out_grad,
    stretch_order,
    positions,
    qkv_weight,
    qkv_moment,
    qkv_square,
    out_weight,
    out_moment,
    out_square,
    gateup_weight,
    gateup_moment,
    gateup_square,
    down_weight,
    down_moment,
    down_square,
    gain_weight,
    gain_moment,
    gain_square,
):
    groups = lax.axis_size("group")
    sequences, local_len, width = hidden_in.shape
    half_stretch = local_len // 2
    seq_len = local_len * groups
    ratio = H // KV
    row_count = sequences * local_len
    scale = HD ** (-0.5)
    bf16 = jnp.bfloat16
    f32 = jnp.float32
    w_qkv, w_out, w_gateup, w_down, gains_low = (
        lax.all_gather(qkv_weight.astype(bf16), "group", axis=0, tiled=True),
        lax.all_gather(out_weight.astype(bf16), "group", axis=0, tiled=True),
        lax.all_gather(gateup_weight.astype(bf16), "group", axis=0, tiled=True),
        lax.all_gather(down_weight.astype(bf16), "group", axis=0, tiled=True),
        lax.all_gather(gain_weight.astype(bf16), "group", axis=0, tiled=True),
    )
    gains = gains_low.astype(f32)
    gain_one = gains[:D]
    gain_two = gains[D : 2 * D]
    gain_query = gains[2 * D : 2 * D + HD]
    gain_key = gains[2 * D + HD :]
    member = lax.axis_index("group")
    query_places = real_places(stretch_order, member * local_len, local_len, half_stretch)
    cosine, sine = rope_tables(positions.reshape(row_count))
    tokens = hidden_in.reshape(row_count, width).astype(f32)
    normed, pull_one = jax.vjp(rms_scale, tokens, gain_one)
    normed_low = normed.astype(bf16)
    mixed = jnp.dot(normed_low, w_qkv, preferred_element_type=f32)

    def heads_of(mixed_rows, query_gain, key_gain):
        return split_heads(mixed_rows, query_gain, key_gain, cosine, sine)

    (query, keys, values), pull_heads = jax.vjp(heads_of, mixed, gain_query, gain_key)
    query_low = query.astype(bf16).reshape(sequences, local_len, KV, ratio, HD)
    keys_low = keys.astype(bf16).reshape(sequences, local_len, KV, HD)
    values_low = values.astype(bf16).reshape(sequences, local_len, KV, HD)

    def scores_for(keys_piece, start):
        count = keys_piece.shape[1]
        key_places = real_places(stretch_order, start, count, half_stretch)
        allowed = key_places[None, :] <= query_places[:, None]
        raw_scores = (
            jnp.einsum("sqkrd,spkd->skrqp", query_low, keys_piece, preferred_element_type=f32)
            * scale
        )
        return jnp.where(allowed, raw_scores, MASKED)

    def forward_block(carry, piece, start):
        top_old, total_old, accum_old = carry
        scores = scores_for(piece[0], start)
        top_new = jnp.maximum(top_old, jnp.max(scores, axis=-1))
        factor = jnp.exp(top_old - top_new)
        exp_terms = jnp.exp(scores - top_new[..., None])
        total_new = total_old * factor + jnp.sum(exp_terms, axis=-1)
        update = jnp.einsum(
            "skrqp,spkd->skrqd", exp_terms.astype(bf16), piece[1], preferred_element_type=f32
        )
        return (top_new, total_new, accum_old * factor[..., None] + update)

    start_state = (
        jnp.full((sequences, KV, ratio, local_len), START_TOP, f32),
        jnp.zeros((sequences, KV, ratio, local_len), f32),
        jnp.zeros((sequences, KV, ratio, local_len, HD), f32),
    )
    top, total, accum = by_blocks(
        forward_block,
        start_state,
        (
            lax.all_gather(keys_low, "group", axis=1, tiled=True),
            lax.all_gather(values_low, "group", axis=1, tiled=True),
        ),
        local_len,
    )
    attended = accum / total[..., None]
    log_total = top + jnp.log(total)
    attended_low = jnp.transpose(attended, (0, 3, 1, 2, 4)).reshape(row_count, H * HD).astype(bf16)
    middle = tokens + jnp.dot(attended_low, w_out, preferred_element_type=f32)
    second, pull_two = jax.vjp(rms_scale, middle, gain_two)
    second_low = second.astype(bf16)
    gate_up = jnp.dot(second_low, w_gateup, preferred_element_type=f32)
    inner, pull_gate = jax.vjp(gated, gate_up)
    inner_low = inner.astype(bf16)
    result = middle + jnp.dot(inner_low, w_down, preferred_element_type=f32)
    layer_out = result.astype(bf16).reshape(sequences, local_len, width)
    grad_result_low = out_grad.reshape(row_count, width)
    grad_down = jnp.einsum("ti,to->io", inner_low, grad_result_low, preferred_element_type=f32)
    grad_inner = jnp.einsum("to,io->ti", grad_result_low, w_down, preferred_element_type=f32)
    (grad_gate_up,) = pull_gate(grad_inner)
    grad_gate_low = grad_gate_up.astype(bf16)
    grad_gateup = jnp.einsum("td,tf->df", second_low, grad_gate_low, preferred_element_type=f32)
    grad_second = jnp.einsum("tf,df->td", grad_gate_low, w_gateup, preferred_element_type=f32)
    grad_mid_part, grad_gain_two = pull_two(grad_second)
    grad_middle = grad_result_low.astype(f32) + grad_mid_part
    grad_branch_low = grad_middle.astype(bf16)
    grad_out = jnp.einsum("ta,td->ad", attended_low, grad_branch_low, preferred_element_type=f32)
    grad_att = jnp.einsum("td,ad->ta", grad_branch_low, w_out, preferred_element_type=f32).astype(
        bf16
    )
    grad_att_heads = jnp.transpose(
        grad_att.reshape(sequences, local_len, KV, ratio, HD), (0, 2, 3, 1, 4)
    )
    delta = jnp.sum(grad_att_heads.astype(f32) * attended, axis=-1)

    def backward_block(carry, piece, start):
        grad_query, grad_pairs = carry
        keys_piece, values_piece = piece
        count = keys_piece.shape[1]
        scores = scores_for(keys_piece, start)
        probs = jnp.exp(scores - log_total[..., None])
        grad_values = jnp.einsum(
            "skrqp,skrqd->spkd", probs.astype(bf16), grad_att_heads, preferred_element_type=f32
        )
        grad_probs = jnp.einsum(
            "skrqd,spkd->skrqp", grad_att_heads, values_piece, preferred_element_type=f32
        )
        grad_scores = (probs * (grad_probs - delta[..., None])).astype(bf16)
        grad_query = (
            grad_query
            + jnp.einsum("skrqp,spkd->skrqd", grad_scores, keys_piece, preferred_element_type=f32)
            * scale
        )
        grad_keys = (
            jnp.einsum("skrqp,sqkrd->spkd", grad_scores, query_low, preferred_element_type=f32)
            * scale
        )
        current = lax.dynamic_slice_in_dim(grad_pairs, start, count, 1)
        joined = current + jnp.concatenate([grad_keys, grad_values], axis=-1)
        return (grad_query, lax.dynamic_update_slice_in_dim(grad_pairs, joined, start, 1))

    back_state = (
        jnp.zeros((sequences, KV, ratio, local_len, HD), f32),
        jnp.zeros((sequences, seq_len, KV, 2 * HD), f32),
    )
    grad_query, grad_pairs = by_blocks(
        backward_block,
        back_state,
        (
            lax.all_gather(keys_low, "group", axis=1, tiled=True),
            lax.all_gather(values_low, "group", axis=1, tiled=True),
        ),
        local_len,
    )
    grad_local = lax.psum_scatter(
        grad_pairs.astype(jnp.bfloat16), "group", scatter_dimension=1, tiled=True
    ).astype(jnp.float32)
    grad_keys = grad_local[..., :HD].reshape(row_count, KV, HD)
    grad_values = grad_local[..., HD:].reshape(row_count, KV, HD)
    grad_query = jnp.transpose(grad_query, (0, 3, 1, 2, 4)).reshape(row_count, H, HD)
    grad_mixed, grad_gain_query, grad_gain_key = pull_heads((grad_query, grad_keys, grad_values))
    grad_mixed_low = grad_mixed.astype(bf16)
    grad_qkv = jnp.einsum("td,tc->dc", normed_low, grad_mixed_low, preferred_element_type=f32)
    grad_normed = jnp.einsum("tc,dc->td", grad_mixed_low, w_qkv, preferred_element_type=f32)
    grad_token_part, grad_gain_one = pull_one(grad_normed)
    input_grad = (grad_middle + grad_token_part).astype(bf16).reshape(sequences, local_len, width)
    grad_gains = jnp.concatenate([grad_gain_one, grad_gain_two, grad_gain_query, grad_gain_key])
    part_qkv, part_out, part_gateup, part_down, part_gain = (
        lax.psum_scatter(
            grad_qkv.astype(jnp.bfloat16), "group", scatter_dimension=0, tiled=True
        ).astype(jnp.float32),
        lax.psum_scatter(
            grad_out.astype(jnp.bfloat16), "group", scatter_dimension=0, tiled=True
        ).astype(jnp.float32),
        lax.psum_scatter(
            grad_gateup.astype(jnp.bfloat16), "group", scatter_dimension=0, tiled=True
        ).astype(jnp.float32),
        lax.psum_scatter(
            grad_down.astype(jnp.bfloat16), "group", scatter_dimension=0, tiled=True
        ).astype(jnp.float32),
        lax.psum_scatter(
            grad_gains.astype(jnp.bfloat16), "group", scatter_dimension=0, tiled=True
        ).astype(jnp.float32),
    )
    total_qkv, total_out, total_gateup, total_down, total_gain = (
        lax.psum(part_qkv.astype(jnp.bfloat16), "dp").astype(jnp.float32),
        lax.psum(part_out.astype(jnp.bfloat16), "dp").astype(jnp.float32),
        lax.psum(part_gateup.astype(jnp.bfloat16), "dp").astype(jnp.float32),
        lax.psum(part_down.astype(jnp.bfloat16), "dp").astype(jnp.float32),
        lax.psum(part_gain.astype(jnp.bfloat16), "dp").astype(jnp.float32),
    )
    out_fan = H * HD * 8 // seq_len
    qkv_new = adam_step(qkv_weight, qkv_moment, qkv_square, total_qkv, LR_MULT * D ** (-0.5), DECAY)
    out_new = adam_step(
        out_weight, out_moment, out_square, total_out, LR_MULT * out_fan ** (-0.5), DECAY
    )
    gateup_new = adam_step(
        gateup_weight, gateup_moment, gateup_square, total_gateup, LR_MULT * D ** (-0.5), DECAY
    )
    down_new = adam_step(
        down_weight, down_moment, down_square, total_down, LR_MULT * FF ** (-0.5), DECAY
    )
    gain_new = adam_step(gain_weight, gain_moment, gain_square, total_gain, GAIN_RATE, 0.0)
    return (
        layer_out,
        input_grad,
        qkv_new[0],
        qkv_new[1],
        qkv_new[2],
        out_new[0],
        out_new[1],
        out_new[2],
        gateup_new[0],
        gateup_new[1],
        gateup_new[2],
        down_new[0],
        down_new[1],
        down_new[2],
        gain_new[0],
        gain_new[1],
        gain_new[2],
    )


ALL = ("dp", "group")
LOG2E = 1.4426950408889634


def tie(value, *others):
    return lax.optimization_barrier((value, *others))[0]


def split_product(left, right, left_dim, right_dim):
    return lax.dot_general(
        left, right, (((left_dim,), (right_dim,)), ((), ())), preferred_element_type=jnp.float32
    )


def place_rows(pieces, targets, chunk):
    count = targets.shape[0]
    per_piece = count // len(pieces)
    width = pieces[0].shape[1]

    def kernel(targets_ref, *refs):
        sources = refs[: len(pieces)]
        placed, sems = refs[len(pieces) :]
        copies = []
        for number in range(count):
            row = pl.multiple_of(targets_ref[number] * chunk, chunk)
            copies.append(
                pltpu.make_async_copy(
                    sources[number // per_piece].at[pl.ds((number % per_piece) * chunk, chunk)],
                    placed.at[pl.ds(row, chunk)],
                    sems.at[number],
                )
            )
        for copy in copies:
            copy.start()
        for copy in copies:
            copy.wait()

    return pl.pallas_call(
        kernel,
        out_shape=jax.ShapeDtypeStruct((count * chunk, width), pieces[0].dtype),
        grid_spec=pltpu.PrefetchScalarGridSpec(
            num_scalar_prefetch=1,
            grid=(1,),
            in_specs=[pl.BlockSpec(memory_space=pl.ANY)] * len(pieces),
            out_specs=pl.BlockSpec(memory_space=pl.ANY),
            scratch_shapes=[pltpu.SemaphoreType.DMA((count,))],
        ),
        cost_estimate=pl.CostEstimate(
            flops=0, bytes_accessed=4 * count * chunk * width, transcendentals=0
        ),
        name="place_rows",
    )(targets, *pieces)


def take_rows(rows, sources, chunk):
    return jnp.concatenate(
        [
            lax.dynamic_slice_in_dim(rows, sources[number] * chunk, chunk, 0)
            for number in range(sources.shape[0])
        ],
        axis=0,
    )


def normal_rope(raw, gain, cosine, sine):
    inverse = lax.rsqrt(jnp.mean(raw * raw, axis=-1, keepdims=True) + EPSILON)
    scaled = raw * inverse * gain
    return scaled * cosine + pltpu.roll(scaled, HD // 2, 1) * sine, inverse


def normal_rope_back(grad, raw, inverse, gain, cosine, sine):
    grad_scaled = grad * cosine + pltpu.roll(grad * sine, HD // 2, 1)
    unit = raw * inverse
    grad_gain = jnp.sum(grad_scaled * unit, axis=0, keepdims=True)
    weighted = grad_scaled * gain
    shift = jnp.mean(weighted * unit, axis=-1, keepdims=True)
    return inverse * (weighted - unit * shift), grad_gain


def causal_mask(block, ratio):
    row = lax.broadcasted_iota(jnp.int32, (ratio * block, block), 0) % block
    column = lax.broadcasted_iota(jnp.int32, (ratio * block, block), 1)
    return column <= row


def attend_forward(mixed, cosine, sine, gain_query, gain_key, heads, ratio, block):
    rows = mixed.shape[0]
    wide = (ratio + 2) * HD
    factor = HD ** (-0.5) * LOG2E
    bf16 = jnp.bfloat16
    f32 = jnp.float32

    def kernel(mixed_ref, cos_ref, sin_ref, gq_ref, gk_ref, att_ref, total_ref):
        cos = cos_ref[...]
        sin = sin_ref[...]
        query = [
            normal_rope(mixed_ref[:, r * HD : (r + 1) * HD], gq_ref[...], cos, sin)[0].astype(bf16)
            for r in range(ratio)
        ]
        keys = normal_rope(mixed_ref[:, ratio * HD : (ratio + 1) * HD], gk_ref[...], cos, sin)[0]
        keys = keys.astype(bf16)
        values = mixed_ref[:, (ratio + 1) * HD :].astype(bf16)
        values = jnp.concatenate([values, jnp.ones((rows, HD), bf16)], axis=1)
        allowed = causal_mask(block, ratio)
        lane = lax.broadcasted_iota(jnp.int32, (block, HD), 1)
        for number in range(rows // block):
            low, high = number * block, (number + 1) * block
            stacked = jnp.concatenate([part[low:high] for part in query], axis=0)
            scores = split_product(stacked, keys[low:high], 1, 1)
            terms = jnp.where(allowed, jnp.exp2(scores * factor), 0.0).astype(bf16)
            joined = split_product(terms, values[low:high], 1, 0)
            if low:
                scores = split_product(stacked, keys[:low], 1, 1)
                terms = jnp.exp2(scores * factor).astype(bf16)
                joined = joined + split_product(terms, values[:low], 1, 0)
            total = joined[:, HD:]
            result = (joined[:, :HD] / total).astype(bf16)
            kept = total[:block]
            for r in range(ratio):
                att_ref[low:high, r * HD : (r + 1) * HD] = result[r * block : (r + 1) * block]
                if r:
                    kept = jnp.where(
                        lane >= r * (HD // ratio), total[r * block : (r + 1) * block], kept
                    )
            total_ref[low:high, :] = kept

    work = heads * ratio * rows * rows * HD * 4 * 5 // 8
    return pl.pallas_call(
        kernel,
        grid=(heads,),
        in_specs=[
            pl.BlockSpec((rows, wide), lambda i: (0, i)),
            pl.BlockSpec((rows, HD), lambda i: (0, 0)),
            pl.BlockSpec((rows, HD), lambda i: (0, 0)),
            pl.BlockSpec((1, HD), lambda i: (0, 0)),
            pl.BlockSpec((1, HD), lambda i: (0, 0)),
        ],
        out_specs=[
            pl.BlockSpec((rows, ratio * HD), lambda i: (0, i)),
            pl.BlockSpec((rows, HD), lambda i: (0, i)),
        ],
        out_shape=[
            jax.ShapeDtypeStruct((rows, heads * ratio * HD), bf16),
            jax.ShapeDtypeStruct((rows, heads * HD), f32),
        ],
        compiler_params=pltpu.CompilerParams(vmem_limit_bytes=48 * 1024 * 1024),
        cost_estimate=pl.CostEstimate(
            flops=work,
            bytes_accessed=heads * rows * (wide * 4 + ratio * HD * 2 + HD * 4),
            transcendentals=heads * ratio * rows * rows * 5 // 8,
        ),
        name="attend_forward",
    )(mixed, cosine, sine, gain_query, gain_key)


def attend_backward(
    mixed, cosine, sine, gain_query, gain_key, attended, totals, grad_att, heads, ratio, block
):
    rows = mixed.shape[0]
    wide = (ratio + 2) * HD
    scale = HD ** (-0.5)
    factor = scale * LOG2E
    bf16 = jnp.bfloat16
    f32 = jnp.float32

    def kernel(
        mixed_ref, cos_ref, sin_ref, gq_ref, gk_ref, att_ref, total_ref, grad_ref,
        out_ref, dgq_ref, dgk_ref, key_sum, value_sum,
    ):
        cos = cos_ref[...]
        sin = sin_ref[...]
        gain_q = gq_ref[...]
        query = []
        query_inverse = []
        for r in range(ratio):
            turned, inverse = normal_rope(mixed_ref[:, r * HD : (r + 1) * HD], gain_q, cos, sin)
            query.append(turned.astype(bf16))
            query_inverse.append(inverse)
        raw_keys = mixed_ref[:, ratio * HD : (ratio + 1) * HD]
        keys, key_inverse = normal_rope(raw_keys, gk_ref[...], cos, sin)
        keys = keys.astype(bf16)
        values = mixed_ref[:, (ratio + 1) * HD :].astype(bf16)
        allowed = causal_mask(block, ratio)
        grad_gain = jnp.zeros((1, HD), f32)

        @pl.when(pl.program_id(0) == 0)
        def _():
            dgq_ref[...] = jnp.zeros_like(dgq_ref)
            dgk_ref[...] = jnp.zeros_like(dgk_ref)

        for number in reversed(range(rows // block)):
            low, high = number * block, (number + 1) * block
            stacked = jnp.concatenate([part[low:high] for part in query], axis=0)
            grads = []
            deltas = []
            for r in range(ratio):
                lane = r * (HD // ratio)
                inverse = 1.0 / total_ref[low:high, lane : lane + 1]
                columns = slice(r * HD, (r + 1) * HD)
                part = (grad_ref[low:high, columns].astype(f32) * inverse).astype(bf16)
                grads.append(part)
                deltas.append(
                    jnp.sum(
                        part.astype(f32) * att_ref[low:high, columns].astype(f32),
                        axis=-1,
                        keepdims=True,
                    )
                )
            grad = jnp.concatenate(grads, axis=0)
            delta = jnp.concatenate(deltas, axis=0)
            grad_query = None
            for start, end, masked in ((low, high, True), (0, low, False)):
                if end == start:
                    continue
                scores = split_product(stacked, keys[start:end], 1, 1)
                terms = jnp.exp2(scores * factor)
                if masked:
                    terms = jnp.where(allowed, terms, 0.0)
                grad_terms = split_product(grad, values[start:end], 1, 1)
                grad_scores = (terms * (grad_terms - delta)).astype(bf16)
                grad_values = split_product(terms.astype(bf16), grad, 0, 0)
                grad_keys = split_product(grad_scores, stacked, 0, 0)
                part = split_product(grad_scores, keys[start:end], 1, 0)
                grad_query = part if grad_query is None else grad_query + part
                if number == rows // block - 1:
                    value_sum[start:end, :] = grad_values
                    key_sum[start:end, :] = grad_keys
                else:
                    value_sum[start:end, :] += grad_values
                    key_sum[start:end, :] += grad_keys
            for r in range(ratio):
                columns = slice(r * HD, (r + 1) * HD)
                back, gain_part = normal_rope_back(
                    grad_query[r * block : (r + 1) * block] * scale,
                    mixed_ref[low:high, columns],
                    query_inverse[r][low:high],
                    gain_q,
                    cos[low:high],
                    sin[low:high],
                )
                out_ref[low:high, columns] = back.astype(bf16)
                grad_gain = grad_gain + gain_part
        dgq_ref[...] += grad_gain
        back, gain_part = normal_rope_back(
            key_sum[...] * scale, raw_keys, key_inverse, gk_ref[...], cos, sin
        )
        dgk_ref[...] += gain_part
        out_ref[:, ratio * HD : (ratio + 1) * HD] = back.astype(bf16)
        out_ref[:, (ratio + 1) * HD :] = value_sum[...].astype(bf16)

    work = heads * ratio * rows * rows * HD * 10 * 5 // 8
    return pl.pallas_call(
        kernel,
        grid=(heads,),
        in_specs=[
            pl.BlockSpec((rows, wide), lambda i: (0, i)),
            pl.BlockSpec((rows, HD), lambda i: (0, 0)),
            pl.BlockSpec((rows, HD), lambda i: (0, 0)),
            pl.BlockSpec((1, HD), lambda i: (0, 0)),
            pl.BlockSpec((1, HD), lambda i: (0, 0)),
            pl.BlockSpec((rows, ratio * HD), lambda i: (0, i)),
            pl.BlockSpec((rows, HD), lambda i: (0, i)),
            pl.BlockSpec((rows, ratio * HD), lambda i: (0, i)),
        ],
        out_specs=[
            pl.BlockSpec((rows, wide), lambda i: (0, i)),
            pl.BlockSpec((1, HD), lambda i: (0, 0)),
            pl.BlockSpec((1, HD), lambda i: (0, 0)),
        ],
        out_shape=[
            jax.ShapeDtypeStruct((rows, heads * wide), bf16),
            jax.ShapeDtypeStruct((1, HD), f32),
            jax.ShapeDtypeStruct((1, HD), f32),
        ],
        scratch_shapes=[pltpu.VMEM((rows, HD), f32), pltpu.VMEM((rows, HD), f32)],
        compiler_params=pltpu.CompilerParams(vmem_limit_bytes=48 * 1024 * 1024),
        cost_estimate=pl.CostEstimate(
            flops=work,
            bytes_accessed=heads * rows * (wide * 6 + ratio * HD * 4 + HD * 4),
            transcendentals=heads * ratio * rows * rows * 5 // 8,
        ),
        name="attend_backward",
    )(mixed, cosine, sine, gain_query, gain_key, attended, totals, grad_att)


def paired_shards(
    hidden_in,
    out_grad,
    stretch_order,
    positions,
    qkv_weight,
    qkv_moment,
    qkv_square,
    out_weight,
    out_moment,
    out_square,
    gateup_weight,
    gateup_moment,
    gateup_square,
    down_weight,
    down_moment,
    down_square,
    gain_weight,
    gain_moment,
    gain_square,
):
    groups = lax.axis_size("group")
    copies = lax.axis_size("dp")
    sequences, local_len, width = hidden_in.shape
    seq_len = local_len * groups
    pieces = stretch_order.shape[0]
    chunk = seq_len // pieces
    held = pieces // groups
    ratio = H // KV
    heads = 2 * KV // groups
    ff = FF // groups
    bf16 = jnp.bfloat16
    f32 = jnp.float32
    member = lax.axis_index("group")
    copy = lax.axis_index("dp")
    half = member // 2
    rank = member % 2
    side = copy % 2

    def permute(value, target):
        pairs = []
        for d in range(copies):
            for g in range(groups):
                to_d, to_g = target(d, g)
                pairs.append((d * groups + g, to_d * groups + to_g))
        return lax.ppermute(value, ALL, pairs)

    def over_core(value):
        return permute(value, lambda d, g: (d, g ^ 1))

    def over_chip(value):
        return permute(value, lambda d, g: (d, g ^ 2))

    def over_side(value):
        return permute(value, lambda d, g: (d ^ 1, g))

    def block_of(far, other_rank):
        at = half if not far else 1 - half
        return at * 2 + (rank if not other_rank else 1 - rank)

    def pick(array, index):
        return lax.dynamic_index_in_dim(array, index, 0, keepdims=False)

    gains = lax.all_gather(gain_weight.astype(bf16), "group", axis=0, tiled=True).astype(f32)
    gain_one = gains[:D]
    gain_two = gains[D : 2 * D]
    gain_query = gains[2 * D : 2 * D + HD].reshape(1, HD)
    gain_key = gains[2 * D + HD :].reshape(1, HD)

    first_piece = pick(stretch_order, member * held)
    start = pick(positions, half)[0] - first_piece * chunk
    exponent = jnp.arange(HD // 2, dtype=f32) * (2.0 / HD)
    inverse = jnp.power(jnp.float32(ROPE_BASE), -exponent)
    places = (start + jnp.arange(seq_len, dtype=jnp.int32)).astype(f32)
    angle = places[:, None] * inverse[None, :]
    cosine_half, sine_half = jnp.cos(angle), jnp.sin(angle)
    cosine = jnp.concatenate([cosine_half, cosine_half], axis=-1)
    sine = jnp.concatenate([-sine_half, sine_half], axis=-1)

    def piece_targets(other_rank):
        return [
            stretch_order[block_of(far, other_rank) * held + number]
            for far in (False, True)
            for number in range(held)
        ]

    own_targets = jnp.stack(piece_targets(False))
    peer_targets = jnp.stack(piece_targets(True))
    all_targets = jnp.concatenate([own_targets, peer_targets])

    def whole_sequence(array, far_part):
        near_part = pick(array, half)
        mine = jnp.concatenate([near_part, far_part], axis=0)
        theirs = over_core(mine)
        return place_rows([mine, theirs], all_targets, chunk)

    def by_heads(array):
        lead = array.shape[0]
        query = array[:, : H * HD].reshape(lead, KV, ratio * HD)
        keys = array[:, H * HD : (H + KV) * HD].reshape(lead, KV, HD)
        values = array[:, (H + KV) * HD :].reshape(lead, KV, HD)
        return jnp.concatenate([query, keys, values], axis=2).reshape(lead, groups, -1)

    def by_units(array):
        lead = array.shape[0]
        gate = array[:, :FF].reshape(lead, groups, ff)
        up = array[:, FF:].reshape(lead, groups, ff)
        return jnp.concatenate([gate, up], axis=2)

    def column_blocks(blocked, other_rank):
        parts = []
        for far in (False, True):
            parts.append(
                lax.dynamic_index_in_dim(blocked, block_of(far, other_rank), 1, keepdims=False)
            )
        return jnp.concatenate(parts, axis=1)

    def chip_columns(blocked):
        mine = column_blocks(blocked, False)
        theirs = over_core(column_blocks(blocked, True))
        lead, cols = mine.shape
        chip = jnp.zeros((2 * lead, cols), bf16)
        chip = lax.dynamic_update_slice(chip, mine, (rank * lead, 0))
        return lax.dynamic_update_slice(chip, theirs, ((1 - rank) * lead, 0))

    def columns_payload(chip):
        lead, cols = chip.shape
        return lax.dynamic_slice(chip, (0, (1 - side) * (cols // 2)), (lead, cols // 2))

    def columns_join(chip, from_chip, from_side):
        lead, cols = chip.shape
        whole = jnp.zeros((2 * lead, cols), bf16)
        whole = lax.dynamic_update_slice(whole, chip, (half * lead, 0))
        whole = lax.dynamic_update_slice(
            whole, from_chip, ((1 - half) * lead, side * (cols // 2))
        )
        return lax.dynamic_update_slice(
            whole, from_side, ((1 - half) * lead, (1 - side) * (cols // 2))
        )

    def rows_payload(own):
        return lax.dynamic_slice_in_dim(own, side * (own.shape[0] // 2), own.shape[0] // 2, 0)

    def rows_join(own, from_chip, from_side):
        lead, cols = own.shape
        whole = jnp.zeros((2 * lead, cols), bf16)
        whole = lax.dynamic_update_slice(whole, own, (0, 0))
        whole = lax.dynamic_update_slice(whole, from_chip, (lead + side * (lead // 2), 0))
        return lax.dynamic_update_slice(whole, from_side, (lead + (1 - side) * (lead // 2), 0))

    hidden_far = over_chip(pick(hidden_in, 1 - half))
    qkv_chip = chip_columns(by_heads(qkv_weight.astype(bf16)))
    qkv_y = over_chip(columns_payload(qkv_chip))
    qkv_x = over_side(qkv_y)
    out_own = out_weight.astype(bf16)
    out_y = over_chip(tie(rows_payload(out_own), hidden_far))
    out_x = over_side(out_y)
    gateup_chip = chip_columns(by_units(gateup_weight.astype(bf16)))
    gateup_y = over_chip(tie(columns_payload(gateup_chip), qkv_y))
    gateup_x = over_side(gateup_y)
    down_own = down_weight.astype(bf16)
    down_y = over_chip(tie(rows_payload(down_own), out_y))
    down_x = over_side(down_y)
    grad_far = over_chip(tie(pick(out_grad, 1 - half), gateup_y))

    hidden = whole_sequence(hidden_in, hidden_far)
    tokens = hidden.astype(f32)
    normed_low = rms_scale(tokens, gain_one).astype(bf16)
    w_qkv = columns_join(qkv_chip, qkv_y, qkv_x)
    mixed = split_product(normed_low, w_qkv, 1, 0)
    block = min(256, seq_len)
    attended, totals = attend_forward(
        mixed, cosine, sine, gain_query, gain_key, heads, ratio, block
    )
    w_out = rows_join(out_own, out_y, out_x)
    branch = split_product(attended, w_out, 1, 0).astype(bf16)
    middle = tokens + (branch.astype(f32) + over_core(branch).astype(f32))
    second, pull_two = jax.vjp(rms_scale, middle, gain_two)
    second_low = second.astype(bf16)
    w_gateup = columns_join(gateup_chip, gateup_y, gateup_x)
    gate_up = split_product(second_low, w_gateup, 1, 0)

    def gated_pairs(values):
        return jnp.concatenate(
            [
                jax.nn.silu(values[:, far * 2 * ff : far * 2 * ff + ff])
                * values[:, far * 2 * ff + ff : (far + 1) * 2 * ff]
                for far in range(2)
            ],
            axis=1,
        )

    inner, pull_gate = jax.vjp(gated_pairs, gate_up)
    inner_low = inner.astype(bf16)
    grad_result = whole_sequence(out_grad, grad_far)

    def near_far(grad_fn, swapped=False):
        far = grad_fn(True)
        from_far = over_chip(far)
        near = grad_fn(False)
        if swapped:
            size = from_far.shape[1] // 2
            from_far = jnp.concatenate([from_far[:, size:], from_far[:, :size]], axis=1)
        return (near.astype(f32) + from_far.astype(f32)).astype(bf16)

    def unit_rows(array, far):
        size = array.shape[1] // 2
        return array[:, size:] if far else array[:, :size]

    def chip_rows(array, far):
        size = array.shape[1] // 2
        at = (1 - half) if far else half
        return lax.dynamic_slice_in_dim(array, at * size, size, 1)

    sum_down = near_far(
        lambda far: split_product(unit_rows(inner_low, far), grad_result, 0, 0).astype(bf16)
    )
    w_down = rows_join(down_own, down_y, down_x)
    result_part = split_product(inner_low, w_down, 1, 0).astype(bf16)
    grad_inner = split_product(grad_result, w_down, 1, 1)
    (grad_gate_up,) = pull_gate(grad_inner)
    grad_gate_low = grad_gate_up.astype(bf16)
    sum_gateup = near_far(
        lambda far: split_product(chip_rows(second_low, far), grad_gate_low, 0, 0).astype(bf16),
        True,
    )
    second_part = split_product(grad_gate_low, w_gateup, 1, 1).astype(bf16)
    grad_second = second_part.astype(f32) + over_core(second_part).astype(f32)
    grad_mid_part, grad_gain_two = pull_two(grad_second)
    grad_middle = grad_result.astype(f32) + grad_mid_part
    grad_branch_low = grad_middle.astype(bf16)
    sum_out = near_far(
        lambda far: split_product(unit_rows(attended, far), grad_branch_low, 0, 0).astype(bf16)
    )
    grad_att = split_product(grad_branch_low, w_out, 1, 1).astype(bf16)
    grad_mixed_low, grad_gain_query, grad_gain_key = attend_backward(
        mixed, cosine, sine, gain_query, gain_key, attended, totals, grad_att, heads, ratio, block
    )
    sum_qkv = near_far(
        lambda far: split_product(chip_rows(normed_low, far), grad_mixed_low, 0, 0).astype(bf16),
        True,
    )
    normed_part = split_product(grad_mixed_low, w_qkv, 1, 1).astype(bf16)

    def share_rows(part):
        return take_rows(part, own_targets, chunk).astype(f32) + over_core(
            take_rows(part, peer_targets, chunk)
        ).astype(f32)

    def to_stored(rows_here):
        stored = rows_here.astype(bf16).reshape(2, local_len, width)
        from_far = over_chip(stored[1])
        first = jnp.where(half == 0, stored[0], from_far)
        last = jnp.where(half == 0, from_far, stored[0])
        return jnp.stack([first, last])

    layer_out = to_stored(take_rows(middle, own_targets, chunk) + share_rows(result_part))
    grad_normed = share_rows(normed_part)
    own_tokens = take_rows(hidden, own_targets, chunk).astype(f32)
    unused, pull_one = jax.vjp(rms_scale, own_tokens, gain_one)
    grad_token_part, grad_gain_one = pull_one(grad_normed)
    input_grad = to_stored(take_rows(grad_middle, own_targets, chunk) + grad_token_part)

    def swap_rows(chip_sum):
        lead = chip_sum.shape[0] // 2
        mine = lax.dynamic_slice_in_dim(chip_sum, rank * lead, lead, 0)
        theirs = lax.dynamic_slice_in_dim(chip_sum, (1 - rank) * lead, lead, 0)
        return jnp.concatenate([mine, over_core(theirs)], axis=0)

    bits = []
    step = 1
    while step < copies:
        bits.append(step)
        step *= 2

    def dp_sum(value):
        for bit in bits:
            size = value.shape[0] // 2
            at = (copy // bit) % 2
            sent = lax.dynamic_slice_in_dim(value, (1 - at) * size, size, 0)
            kept = lax.dynamic_slice_in_dim(value, at * size, size, 0)
            received = permute(sent, lambda d, g: (d ^ bit, g))
            value = (kept.astype(f32) + received.astype(f32)).astype(bf16)
        for bit in reversed(bits):
            size = value.shape[0]
            at = (copy // bit) % 2
            received = permute(value, lambda d, g: (d ^ bit, g))
            whole = jnp.zeros((2 * size, value.shape[1]), bf16)
            whole = lax.dynamic_update_slice(whole, value, (at * size, 0))
            value = lax.dynamic_update_slice(whole, received, ((1 - at) * size, 0))
        return value

    total_down = dp_sum(sum_down).astype(f32)
    total_gateup = dp_sum(swap_rows(sum_gateup))
    total_out = dp_sum(sum_out).astype(f32)
    total_qkv = dp_sum(swap_rows(sum_qkv))

    def owner_blocks(total):
        lead = total.shape[0] // 2
        cols = total.shape[1] // 2
        blocks = []
        for block_number in range(groups):
            far = (block_number // 2) ^ half
            peer = (block_number % 2) ^ rank
            blocks.append(lax.dynamic_slice(total, (peer * lead, far * cols), (lead, cols)))
        return blocks

    gateup_blocks = owner_blocks(total_gateup)
    total_gateup = jnp.concatenate(
        [blocked[:, :ff] for blocked in gateup_blocks]
        + [blocked[:, ff:] for blocked in gateup_blocks],
        axis=1,
    ).astype(f32)
    wide = (ratio + 2) * HD
    head_blocks = [
        blocked[:, number * wide : (number + 1) * wide]
        for blocked in owner_blocks(total_qkv)
        for number in range(blocked.shape[1] // wide)
    ]
    total_qkv = jnp.concatenate(
        [blocked[:, : ratio * HD] for blocked in head_blocks]
        + [blocked[:, ratio * HD : (ratio + 1) * HD] for blocked in head_blocks]
        + [blocked[:, (ratio + 1) * HD :] for blocked in head_blocks],
        axis=1,
    ).astype(f32)
    counted = jnp.where(rank == 0, 1.0, 0.0).astype(f32)
    grad_gains = jnp.concatenate(
        [grad_gain_one, grad_gain_two * counted, grad_gain_query[0], grad_gain_key[0]]
    )
    total_gains = lax.psum(grad_gains, ALL)
    gain_rows = gain_weight.shape[0]
    total_gain = lax.dynamic_slice_in_dim(total_gains, member * gain_rows, gain_rows, 0)

    out_fan = H * HD * 8 // seq_len
    qkv_new = adam_step(qkv_weight, qkv_moment, qkv_square, total_qkv, LR_MULT * D ** (-0.5), DECAY)
    out_new = adam_step(
        out_weight, out_moment, out_square, total_out, LR_MULT * out_fan ** (-0.5), DECAY
    )
    gateup_new = adam_step(
        gateup_weight, gateup_moment, gateup_square, total_gateup, LR_MULT * D ** (-0.5), DECAY
    )
    down_new = adam_step(
        down_weight, down_moment, down_square, total_down, LR_MULT * FF ** (-0.5), DECAY
    )
    gain_new = adam_step(gain_weight, gain_moment, gain_square, total_gain, GAIN_RATE, 0.0)
    return (layer_out, input_grad, *qkv_new, *out_new, *gateup_new, *down_new, *gain_new)


def shards(hidden_in, *others):
    groups = lax.axis_size("group")
    copies = lax.axis_size("dp")
    two_ranks = hidden_in.shape[0] == 2 and groups == 4
    if two_ranks and copies % 2 == 0 and copies & (copies - 1) == 0:
        return paired_shards(hidden_in, *others)
    return general_shards(hidden_in, *others)


def solution(mesh):
    return jax.shard_map(
        shards,
        mesh=mesh,
        in_specs=(
            P("dp", "group", None),
            P("dp", "group", None),
            P(),
            P("dp", "group"),
            P("group", None),
            P("group", None),
            P("group", None),
            P("group", None),
            P("group", None),
            P("group", None),
            P("group", None),
            P("group", None),
            P("group", None),
            P("group", None),
            P("group", None),
            P("group", None),
            P("group"),
            P("group"),
            P("group"),
        ),
        out_specs=(
            P("dp", "group", None),
            P("dp", "group", None),
            P("group", None),
            P("group", None),
            P("group", None),
            P("group", None),
            P("group", None),
            P("group", None),
            P("group", None),
            P("group", None),
            P("group", None),
            P("group", None),
            P("group", None),
            P("group", None),
            P("group"),
            P("group"),
            P("group"),
        ),
        check_vma=False,
    )
```

```python
import jax
import jax.numpy as jnp
from jax import lax
from jax.experimental import pallas as pl
from jax.experimental.pallas import tpu as pltpu
from jax.sharding import PartitionSpec as P

D = 1024
H = 16
KV = 8
HD = 128
FF = 3072
STEP = 10


EPSILON = 1e-06
ROPE_BASE = 1000000.0
BETA_ONE = 0.9
BETA_TWO = 0.95
ADAM_EPSILON = 1e-08
DECAY = 0.1
LR_MULT = 3.0
GAIN_RATE = 0.3
MASKED = -1e30
START_TOP = -1e29


def rms_scale(values, gain):
    mean_square = jnp.mean(values * values, axis=-1, keepdims=True)
    return values * lax.rsqrt(mean_square + EPSILON) * gain


def rotate(values, cosine, sine):
    half = values.shape[-1] // 2
    turned = jnp.concatenate([-values[..., half:], values[..., :half]], axis=-1)
    return values * cosine + turned * sine


def rope_tables(places):
    exponent = jnp.arange(HD // 2, dtype=jnp.float32) * (2.0 / HD)
    inverse = jnp.power(jnp.float32(ROPE_BASE), -exponent)
    angle = places.astype(jnp.float32)[:, None] * inverse[None, :]
    angle = jnp.concatenate([angle, angle], axis=-1)
    return (jnp.cos(angle), jnp.sin(angle))


def split_heads(mixed, query_gain, key_gain, cosine, sine):
    row_count = mixed.shape[0]
    query = mixed[:, : H * HD].reshape(row_count, H, HD)
    keys = mixed[:, H * HD : (H + KV) * HD].reshape(row_count, KV, HD)
    values = mixed[:, (H + KV) * HD :].reshape(row_count, KV, HD)
    query = rotate(rms_scale(query, query_gain), cosine[:, None, :], sine[:, None, :])
    keys = rotate(rms_scale(keys, key_gain), cosine[:, None, :], sine[:, None, :])
    return (query, keys, values)


def gated(gate_up):
    half = gate_up.shape[1] // 2
    return jax.nn.silu(gate_up[:, :half]) * gate_up[:, half:]


def real_places(stretch_list, start, count, half_stretch):
    stored = start + jnp.arange(count, dtype=jnp.int32)
    piece_index = stored // half_stretch
    table = jnp.arange(stretch_list.shape[0], dtype=jnp.int32)
    picked = jnp.sum(
        jnp.where(piece_index[:, None] == table[None, :], stretch_list[None, :], 0), axis=1
    )
    return picked * half_stretch + stored % half_stretch


def by_blocks(block_fn, carry, piece, width):
    count = piece[0].shape[1]

    def advance(state, number):
        sliced = tuple(
            (lax.dynamic_slice_in_dim(member, number * width, width, 1) for member in piece)
        )
        return (block_fn(state, sliced, number * width), None)

    state, unused = lax.scan(advance, carry, jnp.arange(count // width, dtype=jnp.int32))
    return state


def adam_step(weight, moment, square, grad, rate, decay):
    moment_new = BETA_ONE * moment + (1.0 - BETA_ONE) * grad
    square_new = BETA_TWO * square + (1.0 - BETA_TWO) * grad * grad
    ratio = (
        moment_new
        / (1.0 - BETA_ONE**STEP)
        / (jnp.sqrt(square_new / (1.0 - BETA_TWO**STEP)) + ADAM_EPSILON)
    )
    return (weight - rate * (ratio + decay * weight), moment_new, square_new)


def general_shards(
    hidden_in,
    out_grad,
    stretch_order,
    positions,
    qkv_weight,
    qkv_moment,
    qkv_square,
    out_weight,
    out_moment,
    out_square,
    gateup_weight,
    gateup_moment,
    gateup_square,
    down_weight,
    down_moment,
    down_square,
    gain_weight,
    gain_moment,
    gain_square,
):
    groups = lax.axis_size("group")
    sequences, local_len, width = hidden_in.shape
    half_stretch = local_len // 2
    seq_len = local_len * groups
    ratio = H // KV
    row_count = sequences * local_len
    scale = HD ** (-0.5)
    bf16 = jnp.bfloat16
    f32 = jnp.float32
    w_qkv, w_out, w_gateup, w_down, gains_low = (
        lax.all_gather(qkv_weight.astype(bf16), "group", axis=0, tiled=True),
        lax.all_gather(out_weight.astype(bf16), "group", axis=0, tiled=True),
        lax.all_gather(gateup_weight.astype(bf16), "group", axis=0, tiled=True),
        lax.all_gather(down_weight.astype(bf16), "group", axis=0, tiled=True),
        lax.all_gather(gain_weight.astype(bf16), "group", axis=0, tiled=True),
    )
    gains = gains_low.astype(f32)
    gain_one = gains[:D]
    gain_two = gains[D : 2 * D]
    gain_query = gains[2 * D : 2 * D + HD]
    gain_key = gains[2 * D + HD :]
    member = lax.axis_index("group")
    query_places = real_places(stretch_order, member * local_len, local_len, half_stretch)
    cosine, sine = rope_tables(positions.reshape(row_count))
    tokens = hidden_in.reshape(row_count, width).astype(f32)
    normed, pull_one = jax.vjp(rms_scale, tokens, gain_one)
    normed_low = normed.astype(bf16)
    mixed = jnp.dot(normed_low, w_qkv, preferred_element_type=f32)

    def heads_of(mixed_rows, query_gain, key_gain):
        return split_heads(mixed_rows, query_gain, key_gain, cosine, sine)

    (query, keys, values), pull_heads = jax.vjp(heads_of, mixed, gain_query, gain_key)
    query_low = query.astype(bf16).reshape(sequences, local_len, KV, ratio, HD)
    keys_low = keys.astype(bf16).reshape(sequences, local_len, KV, HD)
    values_low = values.astype(bf16).reshape(sequences, local_len, KV, HD)

    def scores_for(keys_piece, start):
        count = keys_piece.shape[1]
        key_places = real_places(stretch_order, start, count, half_stretch)
        allowed = key_places[None, :] <= query_places[:, None]
        raw_scores = (
            jnp.einsum("sqkrd,spkd->skrqp", query_low, keys_piece, preferred_element_type=f32)
            * scale
        )
        return jnp.where(allowed, raw_scores, MASKED)

    def forward_block(carry, piece, start):
        top_old, total_old, accum_old = carry
        scores = scores_for(piece[0], start)
        top_new = jnp.maximum(top_old, jnp.max(scores, axis=-1))
        factor = jnp.exp(top_old - top_new)
        exp_terms = jnp.exp(scores - top_new[..., None])
        total_new = total_old * factor + jnp.sum(exp_terms, axis=-1)
        update = jnp.einsum(
            "skrqp,spkd->skrqd", exp_terms.astype(bf16), piece[1], preferred_element_type=f32
        )
        return (top_new, total_new, accum_old * factor[..., None] + update)

    start_state = (
        jnp.full((sequences, KV, ratio, local_len), START_TOP, f32),
        jnp.zeros((sequences, KV, ratio, local_len), f32),
        jnp.zeros((sequences, KV, ratio, local_len, HD), f32),
    )
    top, total, accum = by_blocks(
        forward_block,
        start_state,
        (
            lax.all_gather(keys_low, "group", axis=1, tiled=True),
            lax.all_gather(values_low, "group", axis=1, tiled=True),
        ),
        local_len,
    )
    attended = accum / total[..., None]
    log_total = top + jnp.log(total)
    attended_low = jnp.transpose(attended, (0, 3, 1, 2, 4)).reshape(row_count, H * HD).astype(bf16)
    middle = tokens + jnp.dot(attended_low, w_out, preferred_element_type=f32)
    second, pull_two = jax.vjp(rms_scale, middle, gain_two)
    second_low = second.astype(bf16)
    gate_up = jnp.dot(second_low, w_gateup, preferred_element_type=f32)
    inner, pull_gate = jax.vjp(gated, gate_up)
    inner_low = inner.astype(bf16)
    result = middle + jnp.dot(inner_low, w_down, preferred_element_type=f32)
    layer_out = result.astype(bf16).reshape(sequences, local_len, width)
    grad_result_low = out_grad.reshape(row_count, width)
    grad_down = jnp.einsum("ti,to->io", inner_low, grad_result_low, preferred_element_type=f32)
    grad_inner = jnp.einsum("to,io->ti", grad_result_low, w_down, preferred_element_type=f32)
    (grad_gate_up,) = pull_gate(grad_inner)
    grad_gate_low = grad_gate_up.astype(bf16)
    grad_gateup = jnp.einsum("td,tf->df", second_low, grad_gate_low, preferred_element_type=f32)
    grad_second = jnp.einsum("tf,df->td", grad_gate_low, w_gateup, preferred_element_type=f32)
    grad_mid_part, grad_gain_two = pull_two(grad_second)
    grad_middle = grad_result_low.astype(f32) + grad_mid_part
    grad_branch_low = grad_middle.astype(bf16)
    grad_out = jnp.einsum("ta,td->ad", attended_low, grad_branch_low, preferred_element_type=f32)
    grad_att = jnp.einsum("td,ad->ta", grad_branch_low, w_out, preferred_element_type=f32).astype(
        bf16
    )
    grad_att_heads = jnp.transpose(
        grad_att.reshape(sequences, local_len, KV, ratio, HD), (0, 2, 3, 1, 4)
    )
    delta = jnp.sum(grad_att_heads.astype(f32) * attended, axis=-1)

    def backward_block(carry, piece, start):
        grad_query, grad_pairs = carry
        keys_piece, values_piece = piece
        count = keys_piece.shape[1]
        scores = scores_for(keys_piece, start)
        probs = jnp.exp(scores - log_total[..., None])
        grad_values = jnp.einsum(
            "skrqp,skrqd->spkd", probs.astype(bf16), grad_att_heads, preferred_element_type=f32
        )
        grad_probs = jnp.einsum(
            "skrqd,spkd->skrqp", grad_att_heads, values_piece, preferred_element_type=f32
        )
        grad_scores = (probs * (grad_probs - delta[..., None])).astype(bf16)
        grad_query = (
            grad_query
            + jnp.einsum("skrqp,spkd->skrqd", grad_scores, keys_piece, preferred_element_type=f32)
            * scale
        )
        grad_keys = (
            jnp.einsum("skrqp,sqkrd->spkd", grad_scores, query_low, preferred_element_type=f32)
            * scale
        )
        current = lax.dynamic_slice_in_dim(grad_pairs, start, count, 1)
        joined = current + jnp.concatenate([grad_keys, grad_values], axis=-1)
        return (grad_query, lax.dynamic_update_slice_in_dim(grad_pairs, joined, start, 1))

    back_state = (
        jnp.zeros((sequences, KV, ratio, local_len, HD), f32),
        jnp.zeros((sequences, seq_len, KV, 2 * HD), f32),
    )
    grad_query, grad_pairs = by_blocks(
        backward_block,
        back_state,
        (
            lax.all_gather(keys_low, "group", axis=1, tiled=True),
            lax.all_gather(values_low, "group", axis=1, tiled=True),
        ),
        local_len,
    )
    grad_local = lax.psum_scatter(
        grad_pairs.astype(jnp.bfloat16), "group", scatter_dimension=1, tiled=True
    ).astype(jnp.float32)
    grad_keys = grad_local[..., :HD].reshape(row_count, KV, HD)
    grad_values = grad_local[..., HD:].reshape(row_count, KV, HD)
    grad_query = jnp.transpose(grad_query, (0, 3, 1, 2, 4)).reshape(row_count, H, HD)
    grad_mixed, grad_gain_query, grad_gain_key = pull_heads((grad_query, grad_keys, grad_values))
    grad_mixed_low = grad_mixed.astype(bf16)
    grad_qkv = jnp.einsum("td,tc->dc", normed_low, grad_mixed_low, preferred_element_type=f32)
    grad_normed = jnp.einsum("tc,dc->td", grad_mixed_low, w_qkv, preferred_element_type=f32)
    grad_token_part, grad_gain_one = pull_one(grad_normed)
    input_grad = (grad_middle + grad_token_part).astype(bf16).reshape(sequences, local_len, width)
    grad_gains = jnp.concatenate([grad_gain_one, grad_gain_two, grad_gain_query, grad_gain_key])
    part_qkv, part_out, part_gateup, part_down, part_gain = (
        lax.psum_scatter(
            grad_qkv.astype(jnp.bfloat16), "group", scatter_dimension=0, tiled=True
        ).astype(jnp.float32),
        lax.psum_scatter(
            grad_out.astype(jnp.bfloat16), "group", scatter_dimension=0, tiled=True
        ).astype(jnp.float32),
        lax.psum_scatter(
            grad_gateup.astype(jnp.bfloat16), "group", scatter_dimension=0, tiled=True
        ).astype(jnp.float32),
        lax.psum_scatter(
            grad_down.astype(jnp.bfloat16), "group", scatter_dimension=0, tiled=True
        ).astype(jnp.float32),
        lax.psum_scatter(
            grad_gains.astype(jnp.bfloat16), "group", scatter_dimension=0, tiled=True
        ).astype(jnp.float32),
    )
    total_qkv, total_out, total_gateup, total_down, total_gain = (
        lax.psum(part_qkv.astype(jnp.bfloat16), "dp").astype(jnp.float32),
        lax.psum(part_out.astype(jnp.bfloat16), "dp").astype(jnp.float32),
        lax.psum(part_gateup.astype(jnp.bfloat16), "dp").astype(jnp.float32),
        lax.psum(part_down.astype(jnp.bfloat16), "dp").astype(jnp.float32),
        lax.psum(part_gain.astype(jnp.bfloat16), "dp").astype(jnp.float32),
    )
    out_fan = H * HD * 8 // seq_len
    qkv_new = adam_step(qkv_weight, qkv_moment, qkv_square, total_qkv, LR_MULT * D ** (-0.5), DECAY)
    out_new = adam_step(
        out_weight, out_moment, out_square, total_out, LR_MULT * out_fan ** (-0.5), DECAY
    )
    gateup_new = adam_step(
        gateup_weight, gateup_moment, gateup_square, total_gateup, LR_MULT * D ** (-0.5), DECAY
    )
    down_new = adam_step(
        down_weight, down_moment, down_square, total_down, LR_MULT * FF ** (-0.5), DECAY
    )
    gain_new = adam_step(gain_weight, gain_moment, gain_square, total_gain, GAIN_RATE, 0.0)
    return (
        layer_out,
        input_grad,
        qkv_new[0],
        qkv_new[1],
        qkv_new[2],
        out_new[0],
        out_new[1],
        out_new[2],
        gateup_new[0],
        gateup_new[1],
        gateup_new[2],
        down_new[0],
        down_new[1],
        down_new[2],
        gain_new[0],
        gain_new[1],
        gain_new[2],
    )


ALL = ("dp", "group")
LOG2E = 1.4426950408889634


def tie(value, *others):
    return lax.optimization_barrier((value, *others))[0]


def split_product(left, right, left_dim, right_dim):
    return lax.dot_general(
        left, right, (((left_dim,), (right_dim,)), ((), ())), preferred_element_type=jnp.float32
    )


def place_rows(mine, theirs, targets, chunk, gain):
    count = targets.shape[0]
    width = mine.shape[1]
    near = mine.shape[0] // chunk
    with_norm = gain is not None

    def kernel(targets_ref, mine_ref, theirs_ref, *refs):
        step = pl.program_id(0)
        rows = jnp.where(step < near, mine_ref[...], theirs_ref[...])
        if with_norm:
            gain_ref, placed, normed = refs
            wide = rows.astype(jnp.float32)
            normed[...] = rms_scale(wide, gain_ref[...]).astype(jnp.bfloat16)
        else:
            (placed,) = refs
        placed[...] = rows

    def target_row(i, targets_ref):
        return (targets_ref[i], 0)

    in_specs = [
        pl.BlockSpec((chunk, width), lambda i, targets_ref: (jnp.minimum(i, near - 1), 0)),
        pl.BlockSpec((chunk, width), lambda i, targets_ref: (jnp.maximum(i - near, 0), 0)),
    ]
    operands = [mine, theirs]
    outputs = 1
    if with_norm:
        in_specs.append(pl.BlockSpec((1, width), lambda i, targets_ref: (0, 0)))
        operands.append(gain.reshape(1, width))
        outputs = 2
    shape = jax.ShapeDtypeStruct((count * chunk, width), mine.dtype)
    return pl.pallas_call(
        kernel,
        out_shape=[shape] * outputs,
        grid_spec=pltpu.PrefetchScalarGridSpec(
            num_scalar_prefetch=1,
            grid=(count,),
            in_specs=in_specs,
            out_specs=[pl.BlockSpec((chunk, width), target_row)] * outputs,
        ),
        cost_estimate=pl.CostEstimate(
            flops=0, bytes_accessed=4 * outputs * count * chunk * width, transcendentals=0
        ),
        name="place_rows",
    )(targets, *operands)


def join_columns(own_near, own_far, peer, chip, diagonal, chip_side, diagonal_side, where_at, parts):
    lead, cols = own_near.shape
    width = cols // parts

    def kernel(
        at_ref, near_ref, far_ref, peer_ref, chip_ref, diag_ref, chip_x_ref, diag_x_ref, out_ref
    ):
        step = pl.program_id(0)
        same_half = step // 2 == at_ref[0]
        same_rank = step % 2 == at_ref[1]
        even = at_ref[2] == 0

        def put(condition, first, second):
            @pl.when(condition)
            def _():
                for part in range(parts):
                    columns = slice(part * width, (part + 1) * width)
                    low = 2 * part * width
                    out_ref[:, low : low + width] = first[:, columns]
                    out_ref[:, low + width : low + 2 * width] = second[:, columns]

        put(same_half & same_rank, near_ref, far_ref)
        put(same_half & ~same_rank, peer_ref.at[0], peer_ref.at[1])
        put(~same_half & same_rank & even, chip_ref, chip_x_ref)
        put(~same_half & same_rank & ~even, chip_x_ref, chip_ref)
        put(~same_half & ~same_rank & even, diag_ref, diag_x_ref)
        put(~same_half & ~same_rank & ~even, diag_x_ref, diag_ref)

    flat = pl.BlockSpec((lead, cols), lambda i, at_ref: (0, 0))
    pair = pl.BlockSpec((2, lead, cols), lambda i, at_ref: (0, 0, 0))
    return pl.pallas_call(
        kernel,
        out_shape=jax.ShapeDtypeStruct((4 * lead, 2 * cols), own_near.dtype),
        grid_spec=pltpu.PrefetchScalarGridSpec(
            num_scalar_prefetch=1,
            grid=(4,),
            in_specs=[flat, flat, pair, flat, flat, flat, flat],
            out_specs=pl.BlockSpec((lead, 2 * cols), lambda i, at_ref: (i, 0)),
        ),
        compiler_params=pltpu.CompilerParams(vmem_limit_bytes=48 * 1024 * 1024),
        cost_estimate=pl.CostEstimate(
            flops=0, bytes_accessed=32 * lead * cols, transcendentals=0
        ),
        name="join_columns",
    )(where_at, own_near, own_far, peer, chip, diagonal, chip_side, diagonal_side)


def take_rows(rows, sources, chunk):
    return jnp.concatenate(
        [
            lax.dynamic_slice_in_dim(rows, sources[number] * chunk, chunk, 0)
            for number in range(sources.shape[0])
        ],
        axis=0,
    )


def normal_rope(raw, gain, cosine, sine):
    inverse = lax.rsqrt(jnp.mean(raw * raw, axis=-1, keepdims=True) + EPSILON)
    scaled = raw * inverse * gain
    return scaled * cosine + pltpu.roll(scaled, HD // 2, 1) * sine, inverse


def normal_rope_back(grad, raw, inverse, gain, cosine, sine):
    grad_scaled = grad * cosine + pltpu.roll(grad * sine, HD // 2, 1)
    unit = raw * inverse
    grad_gain = jnp.sum(grad_scaled * unit, axis=0, keepdims=True)
    weighted = grad_scaled * gain
    shift = jnp.mean(weighted * unit, axis=-1, keepdims=True)
    return inverse * (weighted - unit * shift), grad_gain


def causal_mask(block, ratio):
    row = lax.broadcasted_iota(jnp.int32, (ratio * block, block), 0) % block
    column = lax.broadcasted_iota(jnp.int32, (ratio * block, block), 1)
    return column <= row


def attend_forward(mixed, cosine, sine, gain_query, gain_key, heads, ratio, block):
    rows = mixed.shape[0]
    wide = (ratio + 2) * HD
    factor = HD ** (-0.5) * LOG2E
    bf16 = jnp.bfloat16
    f32 = jnp.float32

    def kernel(mixed_ref, cos_ref, sin_ref, gq_ref, gk_ref, att_ref, total_ref):
        cos = cos_ref[...]
        sin = sin_ref[...]
        query = [
            normal_rope(mixed_ref[:, r * HD : (r + 1) * HD], gq_ref[...], cos, sin)[0].astype(bf16)
            for r in range(ratio)
        ]
        keys = normal_rope(mixed_ref[:, ratio * HD : (ratio + 1) * HD], gk_ref[...], cos, sin)[0]
        keys = keys.astype(bf16)
        values = mixed_ref[:, (ratio + 1) * HD :].astype(bf16)
        values = jnp.concatenate([values, jnp.ones((rows, HD), bf16)], axis=1)
        allowed = causal_mask(block, ratio)
        lane = lax.broadcasted_iota(jnp.int32, (block, HD), 1)
        for number in range(rows // block):
            low, high = number * block, (number + 1) * block
            stacked = jnp.concatenate([part[low:high] for part in query], axis=0)
            scores = split_product(stacked, keys[low:high], 1, 1)
            terms = jnp.where(allowed, jnp.exp2(scores * factor), 0.0).astype(bf16)
            joined = split_product(terms, values[low:high], 1, 0)
            if low:
                scores = split_product(stacked, keys[:low], 1, 1)
                terms = jnp.exp2(scores * factor).astype(bf16)
                joined = joined + split_product(terms, values[:low], 1, 0)
            total = joined[:, HD:]
            result = (joined[:, :HD] / total).astype(bf16)
            kept = total[:block]
            for r in range(ratio):
                att_ref[low:high, r * HD : (r + 1) * HD] = result[r * block : (r + 1) * block]
                if r:
                    kept = jnp.where(
                        lane >= r * (HD // ratio), total[r * block : (r + 1) * block], kept
                    )
            total_ref[low:high, :] = kept

    work = heads * ratio * rows * rows * HD * 4 * 5 // 8
    return pl.pallas_call(
        kernel,
        grid=(heads,),
        in_specs=[
            pl.BlockSpec((rows, wide), lambda i: (0, i)),
            pl.BlockSpec((rows, HD), lambda i: (0, 0)),
            pl.BlockSpec((rows, HD), lambda i: (0, 0)),
            pl.BlockSpec((1, HD), lambda i: (0, 0)),
            pl.BlockSpec((1, HD), lambda i: (0, 0)),
        ],
        out_specs=[
            pl.BlockSpec((rows, ratio * HD), lambda i: (0, i % 2 * (heads // 2) + i // 2)),
            pl.BlockSpec((rows, HD), lambda i: (0, i)),
        ],
        out_shape=[
            jax.ShapeDtypeStruct((rows, heads * ratio * HD), bf16),
            jax.ShapeDtypeStruct((rows, heads * HD), f32),
        ],
        compiler_params=pltpu.CompilerParams(vmem_limit_bytes=48 * 1024 * 1024),
        cost_estimate=pl.CostEstimate(
            flops=work,
            bytes_accessed=heads * rows * (wide * 4 + ratio * HD * 2 + HD * 4),
            transcendentals=heads * ratio * rows * rows * 5 // 8,
        ),
        name="attend_forward",
    )(mixed, cosine, sine, gain_query, gain_key)


def attend_backward(
    mixed, cosine, sine, gain_query, gain_key, attended, totals, grad_att, part, parts, ratio, block
):
    heads = 2
    rows = mixed.shape[0]
    wide = (ratio + 2) * HD
    scale = HD ** (-0.5)
    factor = scale * LOG2E
    bf16 = jnp.bfloat16
    f32 = jnp.float32

    def kernel(
        mixed_ref, cos_ref, sin_ref, gq_ref, gk_ref, att_ref, total_ref, grad_ref,
        out_ref, dgq_ref, dgk_ref, key_sum, value_sum,
    ):
        cos = cos_ref[...]
        sin = sin_ref[...]
        gain_q = gq_ref[...]
        query = []
        query_inverse = []
        for r in range(ratio):
            turned, inverse = normal_rope(mixed_ref[:, r * HD : (r + 1) * HD], gain_q, cos, sin)
            query.append(turned.astype(bf16))
            query_inverse.append(inverse)
        raw_keys = mixed_ref[:, ratio * HD : (ratio + 1) * HD]
        keys, key_inverse = normal_rope(raw_keys, gk_ref[...], cos, sin)
        keys = keys.astype(bf16)
        values = mixed_ref[:, (ratio + 1) * HD :].astype(bf16)
        allowed = causal_mask(block, ratio)
        grad_gain = jnp.zeros((1, HD), f32)

        @pl.when(pl.program_id(0) == 0)
        def _():
            dgq_ref[...] = jnp.zeros_like(dgq_ref)
            dgk_ref[...] = jnp.zeros_like(dgk_ref)

        for number in reversed(range(rows // block)):
            low, high = number * block, (number + 1) * block
            stacked = jnp.concatenate([turned[low:high] for turned in query], axis=0)
            grads = []
            deltas = []
            for r in range(ratio):
                lane = r * (HD // ratio)
                inverse = 1.0 / total_ref[low:high, lane : lane + 1]
                columns = slice(r * HD, (r + 1) * HD)
                scaled = (grad_ref[low:high, columns].astype(f32) * inverse).astype(bf16)
                grads.append(scaled)
                deltas.append(
                    jnp.sum(
                        scaled.astype(f32) * att_ref[low:high, columns].astype(f32),
                        axis=-1,
                        keepdims=True,
                    )
                )
            grad = jnp.concatenate(grads, axis=0)
            delta = jnp.concatenate(deltas, axis=0)
            grad_query = None
            for start, end, masked in ((low, high, True), (0, low, False)):
                if end == start:
                    continue
                scores = split_product(stacked, keys[start:end], 1, 1)
                terms = jnp.exp2(scores * factor)
                if masked:
                    terms = jnp.where(allowed, terms, 0.0)
                grad_terms = split_product(grad, values[start:end], 1, 1)
                grad_scores = (terms * (grad_terms - delta)).astype(bf16)
                grad_values = split_product(terms.astype(bf16), grad, 0, 0)
                grad_keys = split_product(grad_scores, stacked, 0, 0)
                added = split_product(grad_scores, keys[start:end], 1, 0)
                grad_query = added if grad_query is None else grad_query + added
                if number == rows // block - 1:
                    value_sum[start:end, :] = grad_values
                    key_sum[start:end, :] = grad_keys
                else:
                    value_sum[start:end, :] += grad_values
                    key_sum[start:end, :] += grad_keys
            for r in range(ratio):
                columns = slice(r * HD, (r + 1) * HD)
                back, gain_part = normal_rope_back(
                    grad_query[r * block : (r + 1) * block] * scale,
                    mixed_ref[low:high, columns],
                    query_inverse[r][low:high],
                    gain_q,
                    cos[low:high],
                    sin[low:high],
                )
                out_ref[low:high, columns] = back.astype(bf16)
                grad_gain = grad_gain + gain_part
        dgq_ref[...] += grad_gain
        back, gain_part = normal_rope_back(
            key_sum[...] * scale, raw_keys, key_inverse, gk_ref[...], cos, sin
        )
        dgk_ref[...] += gain_part
        out_ref[:, ratio * HD : (ratio + 1) * HD] = back.astype(bf16)
        out_ref[:, (ratio + 1) * HD :] = value_sum[...].astype(bf16)

    work = heads * ratio * rows * rows * HD * 10 * 5 // 8
    return pl.pallas_call(
        kernel,
        grid=(heads,),
        in_specs=[
            pl.BlockSpec((rows, wide), lambda i: (0, part * 2 + i)),
            pl.BlockSpec((rows, HD), lambda i: (0, 0)),
            pl.BlockSpec((rows, HD), lambda i: (0, 0)),
            pl.BlockSpec((1, HD), lambda i: (0, 0)),
            pl.BlockSpec((1, HD), lambda i: (0, 0)),
            pl.BlockSpec((rows, ratio * HD), lambda i: (0, i * parts + part)),
            pl.BlockSpec((rows, HD), lambda i: (0, part * 2 + i)),
            pl.BlockSpec((rows, ratio * HD), lambda i: (0, i * parts + part)),
        ],
        out_specs=[
            pl.BlockSpec((rows, wide), lambda i: (0, i)),
            pl.BlockSpec((1, HD), lambda i: (0, 0)),
            pl.BlockSpec((1, HD), lambda i: (0, 0)),
        ],
        out_shape=[
            jax.ShapeDtypeStruct((rows, heads * wide), bf16),
            jax.ShapeDtypeStruct((1, HD), f32),
            jax.ShapeDtypeStruct((1, HD), f32),
        ],
        scratch_shapes=[pltpu.VMEM((rows, HD), f32), pltpu.VMEM((rows, HD), f32)],
        compiler_params=pltpu.CompilerParams(vmem_limit_bytes=48 * 1024 * 1024),
        cost_estimate=pl.CostEstimate(
            flops=work,
            bytes_accessed=heads * rows * (wide * 6 + ratio * HD * 4 + HD * 4),
            transcendentals=heads * ratio * rows * rows * 5 // 8,
        ),
        name="attend_backward",
    )(mixed, cosine, sine, gain_query, gain_key, attended, totals, grad_att)


def paired_shards(
    hidden_in,
    out_grad,
    stretch_order,
    positions,
    qkv_weight,
    qkv_moment,
    qkv_square,
    out_weight,
    out_moment,
    out_square,
    gateup_weight,
    gateup_moment,
    gateup_square,
    down_weight,
    down_moment,
    down_square,
    gain_weight,
    gain_moment,
    gain_square,
):
    groups = lax.axis_size("group")
    copies = lax.axis_size("dp")
    sequences, local_len, width = hidden_in.shape
    seq_len = local_len * groups
    pieces = stretch_order.shape[0]
    chunk = seq_len // pieces
    held = pieces // groups
    ratio = H // KV
    heads = 2 * KV // groups
    ff = FF // groups
    bf16 = jnp.bfloat16
    f32 = jnp.float32
    member = lax.axis_index("group")
    copy = lax.axis_index("dp")
    half = member // 2
    rank = member % 2
    side = copy % 2
    depth = copies // 2
    deep = copy // 2

    def permute(value, target):
        pairs = []
        for d in range(copies):
            for g in range(groups):
                to_d, to_g = target(d, g)
                pairs.append((d * groups + g, to_d * groups + to_g))
        return lax.ppermute(value, ALL, pairs)

    def over_core(value):
        return permute(value, lambda d, g: (d, g ^ 1))

    def over_chip(value):
        return permute(value, lambda d, g: (d, g ^ 2))

    def over_diagonal(value):
        return permute(value, lambda d, g: (d, g ^ 3))

    def over_side(value):
        return permute(value, lambda d, g: (d ^ 1, g))

    def over_depth(value, shift):
        return permute(value, lambda d, g: ((d // 2 + shift) % depth * 2 + d % 2, g))

    def block_of(far, other_rank):
        at = half if not far else 1 - half
        return at * 2 + (rank if not other_rank else 1 - rank)

    def pick(array, index):
        return lax.dynamic_index_in_dim(array, index, 0, keepdims=False)

    def ordered(first_side, mine, theirs):
        return jnp.concatenate(
            [jnp.where(first_side, mine, theirs), jnp.where(first_side, theirs, mine)]
        )

    gain_low = gain_weight.astype(bf16)
    gain_pair = ordered(rank == 0, gain_low, over_core(gain_low))
    gains = ordered(half == 0, gain_pair, over_chip(gain_pair)).astype(f32)
    gain_one = gains[:D]
    gain_two = gains[D : 2 * D]
    gain_query = gains[2 * D : 2 * D + HD].reshape(1, HD)
    gain_key = gains[2 * D + HD :].reshape(1, HD)

    first_piece = pick(stretch_order, member * held)
    start = pick(positions, half)[0] - first_piece * chunk
    exponent = jnp.arange(HD // 2, dtype=f32) * (2.0 / HD)
    inverse = jnp.power(jnp.float32(ROPE_BASE), -exponent)
    places = (start + jnp.arange(seq_len, dtype=jnp.int32)).astype(f32)
    angle = places[:, None] * inverse[None, :]
    cosine_half, sine_half = jnp.cos(angle), jnp.sin(angle)
    cosine = jnp.concatenate([cosine_half, cosine_half], axis=-1)
    sine = jnp.concatenate([-sine_half, sine_half], axis=-1)

    def piece_targets(other_rank):
        return [
            stretch_order[block_of(far, other_rank) * held + number]
            for far in (False, True)
            for number in range(held)
        ]

    own_targets = jnp.stack(piece_targets(False))
    peer_targets = jnp.stack(piece_targets(True))
    all_targets = jnp.concatenate([own_targets, peer_targets])

    def whole_sequence(array, far_part, gain):
        mine = jnp.concatenate([pick(array, half), far_part], axis=0)
        return place_rows(mine, over_core(mine), all_targets, chunk, gain)

    parts = 2
    wide = (ratio + 2) * HD
    some = ff // parts

    def by_heads(array):
        blocks = []
        for head in range(KV):
            blocks.append(array[:, head * ratio * HD : (head + 1) * ratio * HD])
            blocks.append(array[:, (H + head) * HD : (H + head + 1) * HD])
            blocks.append(array[:, (H + KV + head) * HD : (H + KV + head + 1) * HD])
        size = 3 * KV // groups
        return jnp.stack(
            [
                jnp.concatenate(blocks[number * size : (number + 1) * size], axis=1)
                for number in range(groups)
            ]
        )

    def by_units(array):
        stacked = []
        for number in range(groups):
            blocks = []
            for part in range(parts):
                low = number * ff + part * some
                blocks.append(array[:, low : low + some])
                blocks.append(array[:, FF + low : FF + low + some])
            stacked.append(jnp.concatenate(blocks, axis=1))
        return jnp.stack(stacked)

    where_at = jnp.stack([half, rank, side]).astype(jnp.int32)

    class Columns:
        def __init__(self, blocked):
            sent_half = jnp.where(side == 0, 1 - half, half)
            self.to_chip = pick(blocked, sent_half * 2 + rank)
            self.to_diagonal = pick(blocked, sent_half * 2 + 1 - rank)
            self.to_core = jnp.stack(
                [pick(blocked, block_of(False, True)), pick(blocked, block_of(True, True))]
            )
            self.near = pick(blocked, block_of(False, False))
            self.far = pick(blocked, block_of(True, False))

        def send(self):
            self.chip = over_chip(self.to_chip)
            self.diagonal = over_diagonal(self.to_diagonal)
            self.peer = over_core(self.to_core)
            self.chip_side = over_side(self.chip)
            self.diagonal_side = over_side(self.diagonal)

        def joined(self):
            return join_columns(
                self.near, self.far, self.peer, self.chip, self.diagonal,
                self.chip_side, self.diagonal_side, where_at, parts,
            )

    class Rows:
        def __init__(self, own):
            self.own = own
            self.payload = pick(own.reshape(2, own.shape[0] // 2, own.shape[1]), side)

        def send(self):
            self.chip = over_chip(self.payload)
            self.side = over_side(self.chip)

        def joined(self):
            return jnp.concatenate([self.own, ordered(side == 0, self.chip, self.side)], axis=0)

    hidden_far = over_chip(pick(hidden_in, 1 - half))
    qkv = Columns(by_heads(qkv_weight.astype(bf16)))
    qkv.send()
    out = Rows(tie(out_weight, qkv.to_chip, qkv.to_diagonal, qkv.to_core).astype(bf16))
    out.payload = tie(out.payload, hidden_far)
    out.send()
    gateup = Columns(by_units(tie(gateup_weight, qkv.to_chip, out.payload).astype(bf16)))
    gateup.to_chip = tie(gateup.to_chip, qkv.chip)
    gateup.to_diagonal = tie(gateup.to_diagonal, qkv.diagonal)
    gateup.send()
    down = Rows(tie(down_weight, gateup.to_chip, gateup.to_diagonal).astype(bf16))
    down.payload = tie(down.payload, out.chip, gateup.chip)
    down.send()
    grad_far = over_chip(tie(pick(out_grad, 1 - half), gateup.diagonal))

    hidden, normed_low = whole_sequence(hidden_in, hidden_far, gain_one)
    tokens = hidden.astype(f32)
    w_qkv = qkv.joined()
    mixed = split_product(normed_low, w_qkv, 1, 0)
    block = min(256, seq_len)
    attended, totals = attend_forward(
        mixed, cosine, sine, gain_query, gain_key, heads, ratio, block
    )
    w_out = out.joined()
    branch = split_product(attended, w_out, 1, 0).astype(bf16)
    middle = tokens + (branch.astype(f32) + over_core(branch).astype(f32))
    second, pull_two = jax.vjp(rms_scale, middle, gain_two)
    second_low = second.astype(bf16)
    w_gateup = gateup.joined()
    gate_up = split_product(second_low, w_gateup, 1, 0)

    def gated_part(values, part):
        pieces_here = []
        for far in range(2):
            low = (part * 2 + far) * 2 * some
            pieces_here.append(
                jax.nn.silu(values[:, low : low + some]) * values[:, low + some : low + 2 * some]
            )
        return pieces_here

    def gated_all(values):
        found = [gated_part(values, part) for part in range(parts)]
        return jnp.concatenate(
            [found[part][far] for far in range(2) for part in range(parts)], axis=1
        )

    inner, pull_gate = jax.vjp(gated_all, gate_up)
    inner_low = inner.astype(bf16)
    (grad_result,) = whole_sequence(out_grad, grad_far, None)

    def half_columns(array, far):
        size = array.shape[1] // 2
        near_side = half == (1 if far else 0)
        return jnp.where(near_side, array[:, :size], array[:, size:])

    def far_columns(array, far):
        size = array.shape[1] // 2
        return array[:, size:] if far else array[:, :size]

    def far_first(array):
        size = array.shape[1] // 2
        return jnp.concatenate([array[:, size:], array[:, :size]], axis=1)

    def exchange(left_far, left_near, right):
        far = split_product(left_far, right, 0, 0).astype(bf16)
        received = over_chip(far)
        near = split_product(left_near, right, 0, 0).astype(bf16)
        return near, received

    def add(first, *others):
        total = first.astype(f32)
        for other in others:
            total = total + other.astype(f32)
        return total.astype(bf16)

    def swap_rows(near, received):
        received = far_first(received)
        lead = near.shape[0] // 2
        near = near.reshape(2, lead, -1)
        received = received.reshape(2, lead, -1)
        theirs = add(pick(near, 1 - rank), pick(received, 1 - rank))
        mine = add(pick(near, rank), pick(received, rank))
        return jnp.stack([mine, over_core(theirs)])

    def side_sum(value):
        value = value.reshape(2, depth, -1, value.shape[-1])
        return add(pick(value, side), over_side(pick(value, 1 - side)))

    def depth_sum(value):
        received = [
            over_depth(pick(value, (deep + shift) % depth), shift) for shift in range(1, depth)
        ]
        return add(pick(value, deep), *received)

    def depth_gather(value):
        whole = jnp.zeros((depth, *value.shape), bf16)
        for shift in range(depth):
            piece = value if shift == 0 else over_depth(value, shift)
            whole = lax.dynamic_update_index_in_dim(whole, piece, (deep - shift) % depth, 0)
        return whole

    def side_gather(value):
        flat = value.reshape(-1, value.shape[-1])
        return ordered(side == 0, flat, over_side(flat))

    down_near, down_received = exchange(
        far_columns(inner_low, True), far_columns(inner_low, False), grad_result
    )
    w_down = down.joined()
    grad_inner = split_product(grad_result, w_down, 1, 1)
    (grad_gate_up,) = pull_gate(grad_inner)
    grad_gate_low = grad_gate_up.astype(bf16)
    second_near, second_far = half_columns(second_low, False), half_columns(second_low, True)
    part_cols = grad_gate_low.shape[1] // parts
    gateup_sent = [
        exchange(second_far, second_near, grad_gate_low[:, part * part_cols : (part + 1) * part_cols])
        for part in range(parts)
    ]
    second_part = split_product(grad_gate_low, w_gateup, 1, 1).astype(bf16)
    grad_second = second_part.astype(f32) + over_core(second_part).astype(f32)
    result_part = split_product(inner_low, w_down, 1, 0).astype(bf16)
    grad_mid_part, grad_gain_two = pull_two(grad_second)
    grad_middle = grad_result.astype(f32) + grad_mid_part
    grad_branch_low = grad_middle.astype(bf16)
    out_near, out_received = exchange(
        far_columns(attended, True), far_columns(attended, False), grad_branch_low
    )
    grad_att = split_product(grad_branch_low, w_out, 1, 1).astype(bf16)
    normed_near, normed_far = half_columns(normed_low, False), half_columns(normed_low, True)
    grad_parts = []
    qkv_sent = []
    gain_parts = []
    for part in range(parts):
        grad_part, grad_query_part, grad_key_part = attend_backward(
            mixed, cosine, sine, gain_query, gain_key, attended, totals, grad_att,
            part, parts, ratio, block,
        )
        grad_parts.append(grad_part)
        gain_parts.append((grad_query_part[0], grad_key_part[0]))
        qkv_sent.append(exchange(normed_far, normed_near, grad_part))
    normed_part = sum(
        split_product(grad_parts[part], w_qkv[:, part * 2 * wide : (part + 1) * 2 * wide], 1, 1)
        for part in range(parts)
    ).astype(bf16)

    down_sum = side_sum(add(down_near, tie(down_received, grad_att)))
    down_sum = depth_sum(tie(down_sum, grad_parts[0]))
    down_sum = side_gather(depth_gather(tie(down_sum, grad_parts[1])))
    gateup_swapped = []
    for part in range(parts):
        near, received = gateup_sent[part]
        gateup_swapped.append(swap_rows(near, tie(received, grad_parts[part])))

    def share_rows(part):
        return take_rows(part, own_targets, chunk).astype(f32) + over_core(
            take_rows(part, peer_targets, chunk)
        ).astype(f32)

    def to_stored(rows_here):
        stored = rows_here.astype(bf16).reshape(2, local_len, width)
        from_far = over_chip(stored[1])
        first = jnp.where(half == 0, stored[0], from_far)
        last = jnp.where(half == 0, from_far, stored[0])
        return jnp.stack([first, last])

    layer_out = to_stored(take_rows(middle, own_targets, chunk) + share_rows(result_part))
    grad_normed = share_rows(normed_part)
    own_tokens = take_rows(hidden, own_targets, chunk).astype(f32)
    unused, pull_one = jax.vjp(rms_scale, own_tokens, gain_one)
    grad_token_part, grad_gain_one = pull_one(grad_normed)
    input_grad = to_stored(take_rows(grad_middle, own_targets, chunk) + grad_token_part)

    def rest_of_sum(value):
        return side_gather(depth_gather(depth_sum(side_sum(value))))

    gateup_sums = [rest_of_sum(value) for value in gateup_swapped]
    out_sum = rest_of_sum(add(out_near, out_received))
    qkv_sums = [rest_of_sum(swap_rows(*sent)) for sent in qkv_sent]
    total_down = down_sum.astype(f32)
    total_out = out_sum.astype(f32)

    def owner_blocks(totals_of_parts):
        blocks = []
        for block_number in range(groups):
            far = (block_number // 2) ^ half
            peer = (block_number % 2) ^ rank
            for total in totals_of_parts:
                lead = total.shape[0] // 2
                cols = total.shape[1] // 2
                stacked = total.reshape(2, lead, 2 * cols)
                rows_here = pick(stacked, peer)
                blocks.append(jnp.where(far == 0, rows_here[:, :cols], rows_here[:, cols:]))
        return blocks

    gateup_blocks = owner_blocks(gateup_sums)
    total_gateup = jnp.concatenate(
        [blocked[:, :some] for blocked in gateup_blocks]
        + [blocked[:, some:] for blocked in gateup_blocks],
        axis=1,
    ).astype(f32)
    head_blocks = owner_blocks(qkv_sums)
    total_qkv = jnp.concatenate(
        [blocked[:, : ratio * HD] for blocked in head_blocks]
        + [blocked[:, ratio * HD : (ratio + 1) * HD] for blocked in head_blocks]
        + [blocked[:, (ratio + 1) * HD :] for blocked in head_blocks],
        axis=1,
    ).astype(f32)
    counted = jnp.where(rank == 0, 1.0, 0.0).astype(f32)
    total_gains = jnp.concatenate(
        [
            grad_gain_one,
            grad_gain_two * counted,
            sum(pair[0] for pair in gain_parts),
            sum(pair[1] for pair in gain_parts),
        ]
    )
    total_gains = total_gains + over_core(total_gains)
    total_gains = total_gains + over_chip(total_gains)
    total_gains = total_gains + over_side(total_gains)
    total_gains = total_gains + sum(over_depth(total_gains, shift) for shift in range(1, depth))
    gain_rows = gain_weight.shape[0]
    total_gain = lax.dynamic_slice_in_dim(total_gains, member * gain_rows, gain_rows, 0)

    out_fan = H * HD * 8 // seq_len
    qkv_new = adam_step(qkv_weight, qkv_moment, qkv_square, total_qkv, LR_MULT * D ** (-0.5), DECAY)
    out_new = adam_step(
        out_weight, out_moment, out_square, total_out, LR_MULT * out_fan ** (-0.5), DECAY
    )
    gateup_new = adam_step(
        gateup_weight, gateup_moment, gateup_square, total_gateup, LR_MULT * D ** (-0.5), DECAY
    )
    down_new = adam_step(
        down_weight, down_moment, down_square, total_down, LR_MULT * FF ** (-0.5), DECAY
    )
    gain_new = adam_step(gain_weight, gain_moment, gain_square, total_gain, GAIN_RATE, 0.0)
    return (layer_out, input_grad, *qkv_new, *out_new, *gateup_new, *down_new, *gain_new)


def shards(hidden_in, *others):
    groups = lax.axis_size("group")
    copies = lax.axis_size("dp")
    two_ranks = hidden_in.shape[0] == 2 and groups == 4
    if two_ranks and copies % 2 == 0:
        return paired_shards(hidden_in, *others)
    return general_shards(hidden_in, *others)


def solution(mesh):
    return jax.shard_map(
        shards,
        mesh=mesh,
        in_specs=(
            P("dp", "group", None),
            P("dp", "group", None),
            P(),
            P("dp", "group"),
            P("group", None),
            P("group", None),
            P("group", None),
            P("group", None),
            P("group", None),
            P("group", None),
            P("group", None),
            P("group", None),
            P("group", None),
            P("group", None),
            P("group", None),
            P("group", None),
            P("group"),
            P("group"),
            P("group"),
        ),
        out_specs=(
            P("dp", "group", None),
            P("dp", "group", None),
            P("group", None),
            P("group", None),
            P("group", None),
            P("group", None),
            P("group", None),
            P("group", None),
            P("group", None),
            P("group", None),
            P("group", None),
            P("group", None),
            P("group", None),
            P("group", None),
            P("group"),
            P("group"),
            P("group"),
        ),
        check_vma=False,
    )
```

```python
import jax
import jax.numpy as jnp
from jax import lax
from jax.experimental import pallas as pl
from jax.experimental.pallas import tpu as pltpu
from jax.sharding import PartitionSpec as P

D = 1024
H = 16
KV = 8
HD = 128
FF = 3072
STEP = 10


EPSILON = 1e-06
ROPE_BASE = 1000000.0
BETA_ONE = 0.9
BETA_TWO = 0.95
ADAM_EPSILON = 1e-08
DECAY = 0.1
LR_MULT = 3.0
GAIN_RATE = 0.3
MASKED = -1e30
START_TOP = -1e29


def rms_scale(values, gain):
    mean_square = jnp.mean(values * values, axis=-1, keepdims=True)
    return values * lax.rsqrt(mean_square + EPSILON) * gain


def rotate(values, cosine, sine):
    half = values.shape[-1] // 2
    turned = jnp.concatenate([-values[..., half:], values[..., :half]], axis=-1)
    return values * cosine + turned * sine


def rope_tables(places):
    exponent = jnp.arange(HD // 2, dtype=jnp.float32) * (2.0 / HD)
    inverse = jnp.power(jnp.float32(ROPE_BASE), -exponent)
    angle = places.astype(jnp.float32)[:, None] * inverse[None, :]
    angle = jnp.concatenate([angle, angle], axis=-1)
    return (jnp.cos(angle), jnp.sin(angle))


def split_heads(mixed, query_gain, key_gain, cosine, sine):
    row_count = mixed.shape[0]
    query = mixed[:, : H * HD].reshape(row_count, H, HD)
    keys = mixed[:, H * HD : (H + KV) * HD].reshape(row_count, KV, HD)
    values = mixed[:, (H + KV) * HD :].reshape(row_count, KV, HD)
    query = rotate(rms_scale(query, query_gain), cosine[:, None, :], sine[:, None, :])
    keys = rotate(rms_scale(keys, key_gain), cosine[:, None, :], sine[:, None, :])
    return (query, keys, values)


def gated(gate_up):
    half = gate_up.shape[1] // 2
    return jax.nn.silu(gate_up[:, :half]) * gate_up[:, half:]


def real_places(stretch_list, start, count, half_stretch):
    stored = start + jnp.arange(count, dtype=jnp.int32)
    piece_index = stored // half_stretch
    table = jnp.arange(stretch_list.shape[0], dtype=jnp.int32)
    picked = jnp.sum(
        jnp.where(piece_index[:, None] == table[None, :], stretch_list[None, :], 0), axis=1
    )
    return picked * half_stretch + stored % half_stretch


def by_blocks(block_fn, carry, piece, width):
    count = piece[0].shape[1]

    def advance(state, number):
        sliced = tuple(
            (lax.dynamic_slice_in_dim(member, number * width, width, 1) for member in piece)
        )
        return (block_fn(state, sliced, number * width), None)

    state, unused = lax.scan(advance, carry, jnp.arange(count // width, dtype=jnp.int32))
    return state


def adam_step(weight, moment, square, grad, rate, decay):
    moment_new = BETA_ONE * moment + (1.0 - BETA_ONE) * grad
    square_new = BETA_TWO * square + (1.0 - BETA_TWO) * grad * grad
    ratio = (
        moment_new
        / (1.0 - BETA_ONE**STEP)
        / (jnp.sqrt(square_new / (1.0 - BETA_TWO**STEP)) + ADAM_EPSILON)
    )
    return (weight - rate * (ratio + decay * weight), moment_new, square_new)


def general_shards(
    hidden_in,
    out_grad,
    stretch_order,
    positions,
    qkv_weight,
    qkv_moment,
    qkv_square,
    out_weight,
    out_moment,
    out_square,
    gateup_weight,
    gateup_moment,
    gateup_square,
    down_weight,
    down_moment,
    down_square,
    gain_weight,
    gain_moment,
    gain_square,
):
    groups = lax.axis_size("group")
    sequences, local_len, width = hidden_in.shape
    half_stretch = local_len // 2
    seq_len = local_len * groups
    ratio = H // KV
    row_count = sequences * local_len
    scale = HD ** (-0.5)
    bf16 = jnp.bfloat16
    f32 = jnp.float32
    w_qkv, w_out, w_gateup, w_down, gains_low = (
        lax.all_gather(qkv_weight.astype(bf16), "group", axis=0, tiled=True),
        lax.all_gather(out_weight.astype(bf16), "group", axis=0, tiled=True),
        lax.all_gather(gateup_weight.astype(bf16), "group", axis=0, tiled=True),
        lax.all_gather(down_weight.astype(bf16), "group", axis=0, tiled=True),
        lax.all_gather(gain_weight.astype(bf16), "group", axis=0, tiled=True),
    )
    gains = gains_low.astype(f32)
    gain_one = gains[:D]
    gain_two = gains[D : 2 * D]
    gain_query = gains[2 * D : 2 * D + HD]
    gain_key = gains[2 * D + HD :]
    member = lax.axis_index("group")
    query_places = real_places(stretch_order, member * local_len, local_len, half_stretch)
    cosine, sine = rope_tables(positions.reshape(row_count))
    tokens = hidden_in.reshape(row_count, width).astype(f32)
    normed, pull_one = jax.vjp(rms_scale, tokens, gain_one)
    normed_low = normed.astype(bf16)
    mixed = jnp.dot(normed_low, w_qkv, preferred_element_type=f32)

    def heads_of(mixed_rows, query_gain, key_gain):
        return split_heads(mixed_rows, query_gain, key_gain, cosine, sine)

    (query, keys, values), pull_heads = jax.vjp(heads_of, mixed, gain_query, gain_key)
    query_low = query.astype(bf16).reshape(sequences, local_len, KV, ratio, HD)
    keys_low = keys.astype(bf16).reshape(sequences, local_len, KV, HD)
    values_low = values.astype(bf16).reshape(sequences, local_len, KV, HD)

    def scores_for(keys_piece, start):
        count = keys_piece.shape[1]
        key_places = real_places(stretch_order, start, count, half_stretch)
        allowed = key_places[None, :] <= query_places[:, None]
        raw_scores = (
            jnp.einsum("sqkrd,spkd->skrqp", query_low, keys_piece, preferred_element_type=f32)
            * scale
        )
        return jnp.where(allowed, raw_scores, MASKED)

    def forward_block(carry, piece, start):
        top_old, total_old, accum_old = carry
        scores = scores_for(piece[0], start)
        top_new = jnp.maximum(top_old, jnp.max(scores, axis=-1))
        factor = jnp.exp(top_old - top_new)
        exp_terms = jnp.exp(scores - top_new[..., None])
        total_new = total_old * factor + jnp.sum(exp_terms, axis=-1)
        update = jnp.einsum(
            "skrqp,spkd->skrqd", exp_terms.astype(bf16), piece[1], preferred_element_type=f32
        )
        return (top_new, total_new, accum_old * factor[..., None] + update)

    start_state = (
        jnp.full((sequences, KV, ratio, local_len), START_TOP, f32),
        jnp.zeros((sequences, KV, ratio, local_len), f32),
        jnp.zeros((sequences, KV, ratio, local_len, HD), f32),
    )
    top, total, accum = by_blocks(
        forward_block,
        start_state,
        (
            lax.all_gather(keys_low, "group", axis=1, tiled=True),
            lax.all_gather(values_low, "group", axis=1, tiled=True),
        ),
        local_len,
    )
    attended = accum / total[..., None]
    log_total = top + jnp.log(total)
    attended_low = jnp.transpose(attended, (0, 3, 1, 2, 4)).reshape(row_count, H * HD).astype(bf16)
    middle = tokens + jnp.dot(attended_low, w_out, preferred_element_type=f32)
    second, pull_two = jax.vjp(rms_scale, middle, gain_two)
    second_low = second.astype(bf16)
    gate_up = jnp.dot(second_low, w_gateup, preferred_element_type=f32)
    inner, pull_gate = jax.vjp(gated, gate_up)
    inner_low = inner.astype(bf16)
    result = middle + jnp.dot(inner_low, w_down, preferred_element_type=f32)
    layer_out = result.astype(bf16).reshape(sequences, local_len, width)
    grad_result_low = out_grad.reshape(row_count, width)
    grad_down = jnp.einsum("ti,to->io", inner_low, grad_result_low, preferred_element_type=f32)
    grad_inner = jnp.einsum("to,io->ti", grad_result_low, w_down, preferred_element_type=f32)
    (grad_gate_up,) = pull_gate(grad_inner)
    grad_gate_low = grad_gate_up.astype(bf16)
    grad_gateup = jnp.einsum("td,tf->df", second_low, grad_gate_low, preferred_element_type=f32)
    grad_second = jnp.einsum("tf,df->td", grad_gate_low, w_gateup, preferred_element_type=f32)
    grad_mid_part, grad_gain_two = pull_two(grad_second)
    grad_middle = grad_result_low.astype(f32) + grad_mid_part
    grad_branch_low = grad_middle.astype(bf16)
    grad_out = jnp.einsum("ta,td->ad", attended_low, grad_branch_low, preferred_element_type=f32)
    grad_att = jnp.einsum("td,ad->ta", grad_branch_low, w_out, preferred_element_type=f32).astype(
        bf16
    )
    grad_att_heads = jnp.transpose(
        grad_att.reshape(sequences, local_len, KV, ratio, HD), (0, 2, 3, 1, 4)
    )
    delta = jnp.sum(grad_att_heads.astype(f32) * attended, axis=-1)

    def backward_block(carry, piece, start):
        grad_query, grad_pairs = carry
        keys_piece, values_piece = piece
        count = keys_piece.shape[1]
        scores = scores_for(keys_piece, start)
        probs = jnp.exp(scores - log_total[..., None])
        grad_values = jnp.einsum(
            "skrqp,skrqd->spkd", probs.astype(bf16), grad_att_heads, preferred_element_type=f32
        )
        grad_probs = jnp.einsum(
            "skrqd,spkd->skrqp", grad_att_heads, values_piece, preferred_element_type=f32
        )
        grad_scores = (probs * (grad_probs - delta[..., None])).astype(bf16)
        grad_query = (
            grad_query
            + jnp.einsum("skrqp,spkd->skrqd", grad_scores, keys_piece, preferred_element_type=f32)
            * scale
        )
        grad_keys = (
            jnp.einsum("skrqp,sqkrd->spkd", grad_scores, query_low, preferred_element_type=f32)
            * scale
        )
        current = lax.dynamic_slice_in_dim(grad_pairs, start, count, 1)
        joined = current + jnp.concatenate([grad_keys, grad_values], axis=-1)
        return (grad_query, lax.dynamic_update_slice_in_dim(grad_pairs, joined, start, 1))

    back_state = (
        jnp.zeros((sequences, KV, ratio, local_len, HD), f32),
        jnp.zeros((sequences, seq_len, KV, 2 * HD), f32),
    )
    grad_query, grad_pairs = by_blocks(
        backward_block,
        back_state,
        (
            lax.all_gather(keys_low, "group", axis=1, tiled=True),
            lax.all_gather(values_low, "group", axis=1, tiled=True),
        ),
        local_len,
    )
    grad_local = lax.psum_scatter(
        grad_pairs.astype(jnp.bfloat16), "group", scatter_dimension=1, tiled=True
    ).astype(jnp.float32)
    grad_keys = grad_local[..., :HD].reshape(row_count, KV, HD)
    grad_values = grad_local[..., HD:].reshape(row_count, KV, HD)
    grad_query = jnp.transpose(grad_query, (0, 3, 1, 2, 4)).reshape(row_count, H, HD)
    grad_mixed, grad_gain_query, grad_gain_key = pull_heads((grad_query, grad_keys, grad_values))
    grad_mixed_low = grad_mixed.astype(bf16)
    grad_qkv = jnp.einsum("td,tc->dc", normed_low, grad_mixed_low, preferred_element_type=f32)
    grad_normed = jnp.einsum("tc,dc->td", grad_mixed_low, w_qkv, preferred_element_type=f32)
    grad_token_part, grad_gain_one = pull_one(grad_normed)
    input_grad = (grad_middle + grad_token_part).astype(bf16).reshape(sequences, local_len, width)
    grad_gains = jnp.concatenate([grad_gain_one, grad_gain_two, grad_gain_query, grad_gain_key])
    part_qkv, part_out, part_gateup, part_down, part_gain = (
        lax.psum_scatter(
            grad_qkv.astype(jnp.bfloat16), "group", scatter_dimension=0, tiled=True
        ).astype(jnp.float32),
        lax.psum_scatter(
            grad_out.astype(jnp.bfloat16), "group", scatter_dimension=0, tiled=True
        ).astype(jnp.float32),
        lax.psum_scatter(
            grad_gateup.astype(jnp.bfloat16), "group", scatter_dimension=0, tiled=True
        ).astype(jnp.float32),
        lax.psum_scatter(
            grad_down.astype(jnp.bfloat16), "group", scatter_dimension=0, tiled=True
        ).astype(jnp.float32),
        lax.psum_scatter(
            grad_gains.astype(jnp.bfloat16), "group", scatter_dimension=0, tiled=True
        ).astype(jnp.float32),
    )
    total_qkv, total_out, total_gateup, total_down, total_gain = (
        lax.psum(part_qkv.astype(jnp.bfloat16), "dp").astype(jnp.float32),
        lax.psum(part_out.astype(jnp.bfloat16), "dp").astype(jnp.float32),
        lax.psum(part_gateup.astype(jnp.bfloat16), "dp").astype(jnp.float32),
        lax.psum(part_down.astype(jnp.bfloat16), "dp").astype(jnp.float32),
        lax.psum(part_gain.astype(jnp.bfloat16), "dp").astype(jnp.float32),
    )
    out_fan = H * HD * 8 // seq_len
    qkv_new = adam_step(qkv_weight, qkv_moment, qkv_square, total_qkv, LR_MULT * D ** (-0.5), DECAY)
    out_new = adam_step(
        out_weight, out_moment, out_square, total_out, LR_MULT * out_fan ** (-0.5), DECAY
    )
    gateup_new = adam_step(
        gateup_weight, gateup_moment, gateup_square, total_gateup, LR_MULT * D ** (-0.5), DECAY
    )
    down_new = adam_step(
        down_weight, down_moment, down_square, total_down, LR_MULT * FF ** (-0.5), DECAY
    )
    gain_new = adam_step(gain_weight, gain_moment, gain_square, total_gain, GAIN_RATE, 0.0)
    return (
        layer_out,
        input_grad,
        qkv_new[0],
        qkv_new[1],
        qkv_new[2],
        out_new[0],
        out_new[1],
        out_new[2],
        gateup_new[0],
        gateup_new[1],
        gateup_new[2],
        down_new[0],
        down_new[1],
        down_new[2],
        gain_new[0],
        gain_new[1],
        gain_new[2],
    )


ALL = ("dp", "group")
LOG2E = 1.4426950408889634
SMALL = pl.CostEstimate(flops=1000000, bytes_accessed=100000, transcendentals=0)


def tie(value, *others):
    return lax.optimization_barrier((value, *others))[0]


def split_product(left, right, left_dim, right_dim):
    return lax.dot_general(
        left, right, (((left_dim,), (right_dim,)), ((), ())), preferred_element_type=jnp.float32
    )


def place_rows(mine, theirs, targets, chunk, gain):
    count = targets.shape[0]
    width = mine.shape[1]
    near = mine.shape[0] // chunk
    with_norm = gain is not None

    def kernel(targets_ref, mine_ref, theirs_ref, *refs):
        step = pl.program_id(0)
        rows = jnp.where(step < near, mine_ref[...], theirs_ref[...])
        if with_norm:
            gain_ref, placed, normed = refs
            wide = rows.astype(jnp.float32)
            normed[...] = rms_scale(wide, gain_ref[...]).astype(jnp.bfloat16)
        else:
            (placed,) = refs
        placed[...] = rows

    def target_row(i, targets_ref):
        return (targets_ref[i], 0)

    in_specs = [
        pl.BlockSpec((chunk, width), lambda i, targets_ref: (jnp.minimum(i, near - 1), 0)),
        pl.BlockSpec((chunk, width), lambda i, targets_ref: (jnp.maximum(i - near, 0), 0)),
    ]
    operands = [mine, theirs]
    outputs = 1
    if with_norm:
        in_specs.append(pl.BlockSpec((1, width), lambda i, targets_ref: (0, 0)))
        operands.append(gain.reshape(1, width))
        outputs = 2
    shape = jax.ShapeDtypeStruct((count * chunk, width), mine.dtype)
    return pl.pallas_call(
        kernel,
        out_shape=[shape] * outputs,
        grid_spec=pltpu.PrefetchScalarGridSpec(
            num_scalar_prefetch=1,
            grid=(count,),
            in_specs=in_specs,
            out_specs=[pl.BlockSpec((chunk, width), target_row)] * outputs,
        ),
        cost_estimate=SMALL,
        name="place_rows",
    )(targets, *operands)


def cut_columns(array, rows_array, where_at, kinds, parts):
    lead, total = array.shape
    groups = 4
    kept = total // groups
    rows_lead, rows_width = rows_array.shape

    def kernel(at_ref, *refs):
        sources = refs[: len(kinds)]
        rows_ref = refs[len(kinds)]
        chip, diagonal, core, near, far, rows_out = refs[len(kinds) + 1 :]
        step = pl.program_id(0)
        for number, target in enumerate(
            (chip, diagonal, core.at[0], core.at[1], near, far)
        ):

            @pl.when(step == number)
            def _(target=target):
                low = 0
                for part in range(parts):
                    for source, (first, size) in zip(sources, kinds):
                        width = size // parts
                        target[:, low : low + width] = source[
                            :, part * width : (part + 1) * width
                        ].astype(jnp.bfloat16)
                        low += width

        @pl.when(step == 0)
        def _():
            rows_out[...] = rows_ref[...].astype(jnp.bfloat16)

    def block_at(step, at_ref):
        half, rank, side = at_ref[0], at_ref[1], at_ref[2]
        sent = jnp.where(side == 0, 1 - half, half)
        pair = jnp.where(
            step < 2, sent, jnp.where((step == 2) | (step == 4), half, 1 - half)
        )
        other = (step == 1) | (step == 2) | (step == 3)
        return pair * 2 + jnp.where(other, 1 - rank, rank)

    def source_spec(first, size):
        return pl.BlockSpec(
            (lead, size), lambda i, at_ref: (0, first // size + block_at(i, at_ref))
        )

    flat = pl.BlockSpec((lead, kept), lambda i, at_ref: (0, 0))
    pair = pl.BlockSpec((2, lead, kept), lambda i, at_ref: (0, 0, 0))
    half_rows = (rows_lead // 2, rows_width)
    single = jax.ShapeDtypeStruct((lead, kept), jnp.bfloat16)
    return pl.pallas_call(
        kernel,
        out_shape=[
            single,
            single,
            jax.ShapeDtypeStruct((2, lead, kept), jnp.bfloat16),
            single,
            single,
            jax.ShapeDtypeStruct(half_rows, jnp.bfloat16),
        ],
        grid_spec=pltpu.PrefetchScalarGridSpec(
            num_scalar_prefetch=1,
            grid=(6,),
            in_specs=[source_spec(first, size) for first, size in kinds]
            + [pl.BlockSpec(half_rows, lambda i, at_ref: (at_ref[2], 0))],
            out_specs=[flat, flat, pair, flat, flat]
            + [pl.BlockSpec(half_rows, lambda i, at_ref: (0, 0))],
        ),
        compiler_params=pltpu.CompilerParams(vmem_limit_bytes=48 * 1024 * 1024),
        cost_estimate=SMALL,
        name="cut_columns",
    )(where_at, *([array] * len(kinds)), rows_array)


def join_columns(own_near, own_far, peer, chip, diagonal, chip_side, diagonal_side, where_at, parts):
    lead, cols = own_near.shape
    width = cols // parts

    def kernel(
        at_ref, near_ref, far_ref, peer_ref, chip_ref, diag_ref, chip_x_ref, diag_x_ref, out_ref
    ):
        step = pl.program_id(0)
        same_half = step // 2 == at_ref[0]
        same_rank = step % 2 == at_ref[1]
        even = at_ref[2] == 0

        def put(condition, first, second):
            @pl.when(condition)
            def _():
                for part in range(parts):
                    columns = slice(part * width, (part + 1) * width)
                    low = 2 * part * width
                    out_ref[:, low : low + width] = first[:, columns]
                    out_ref[:, low + width : low + 2 * width] = second[:, columns]

        put(same_half & same_rank, near_ref, far_ref)
        put(same_half & ~same_rank, peer_ref.at[0], peer_ref.at[1])
        put(~same_half & same_rank & even, chip_ref, chip_x_ref)
        put(~same_half & same_rank & ~even, chip_x_ref, chip_ref)
        put(~same_half & ~same_rank & even, diag_ref, diag_x_ref)
        put(~same_half & ~same_rank & ~even, diag_x_ref, diag_ref)

    flat = pl.BlockSpec((lead, cols), lambda i, at_ref: (0, 0))
    pair = pl.BlockSpec((2, lead, cols), lambda i, at_ref: (0, 0, 0))
    return pl.pallas_call(
        kernel,
        out_shape=jax.ShapeDtypeStruct((4 * lead, 2 * cols), own_near.dtype),
        grid_spec=pltpu.PrefetchScalarGridSpec(
            num_scalar_prefetch=1,
            grid=(4,),
            in_specs=[flat, flat, pair, flat, flat, flat, flat],
            out_specs=pl.BlockSpec((lead, 2 * cols), lambda i, at_ref: (i, 0)),
        ),
        compiler_params=pltpu.CompilerParams(vmem_limit_bytes=48 * 1024 * 1024),
        cost_estimate=SMALL,
        name="join_columns",
    )(where_at, own_near, own_far, peer, chip, diagonal, chip_side, diagonal_side)


def take_rows(rows, sources, chunk):
    return jnp.concatenate(
        [
            lax.dynamic_slice_in_dim(rows, sources[number] * chunk, chunk, 0)
            for number in range(sources.shape[0])
        ],
        axis=0,
    )


def normal_rope(raw, gain, cosine, sine):
    inverse = lax.rsqrt(jnp.mean(raw * raw, axis=-1, keepdims=True) + EPSILON)
    scaled = raw * inverse * gain
    return scaled * cosine + pltpu.roll(scaled, HD // 2, 1) * sine, inverse


def normal_rope_back(grad, raw, inverse, gain, cosine, sine):
    grad_scaled = grad * cosine + pltpu.roll(grad * sine, HD // 2, 1)
    unit = raw * inverse
    grad_gain = jnp.sum(grad_scaled * unit, axis=0, keepdims=True)
    weighted = grad_scaled * gain
    shift = jnp.mean(weighted * unit, axis=-1, keepdims=True)
    return inverse * (weighted - unit * shift), grad_gain


def causal_mask(block, ratio):
    row = lax.broadcasted_iota(jnp.int32, (ratio * block, block), 0) % block
    column = lax.broadcasted_iota(jnp.int32, (ratio * block, block), 1)
    return column <= row


def attend_forward(mixed, cosine, sine, gain_query, gain_key, heads, ratio, block):
    rows = mixed.shape[0]
    wide = (ratio + 2) * HD
    factor = HD ** (-0.5) * LOG2E
    bf16 = jnp.bfloat16
    f32 = jnp.float32

    def kernel(mixed_ref, cos_ref, sin_ref, gq_ref, gk_ref, att_ref, total_ref):
        cos = cos_ref[...]
        sin = sin_ref[...]
        query = [
            normal_rope(mixed_ref[:, r * HD : (r + 1) * HD], gq_ref[...], cos, sin)[0].astype(bf16)
            for r in range(ratio)
        ]
        keys = normal_rope(mixed_ref[:, ratio * HD : (ratio + 1) * HD], gk_ref[...], cos, sin)[0]
        keys = keys.astype(bf16)
        values = mixed_ref[:, (ratio + 1) * HD :].astype(bf16)
        values = jnp.concatenate([values, jnp.ones((rows, HD), bf16)], axis=1)
        allowed = causal_mask(block, ratio)
        lane = lax.broadcasted_iota(jnp.int32, (block, HD), 1)
        for number in range(rows // block):
            low, high = number * block, (number + 1) * block
            stacked = jnp.concatenate([part[low:high] for part in query], axis=0)
            scores = split_product(stacked, keys[low:high], 1, 1)
            terms = jnp.where(allowed, jnp.exp2(scores * factor), 0.0).astype(bf16)
            joined = split_product(terms, values[low:high], 1, 0)
            if low:
                scores = split_product(stacked, keys[:low], 1, 1)
                terms = jnp.exp2(scores * factor).astype(bf16)
                joined = joined + split_product(terms, values[:low], 1, 0)
            total = joined[:, HD:]
            result = (joined[:, :HD] / total).astype(bf16)
            kept = total[:block]
            for r in range(ratio):
                att_ref[low:high, r * HD : (r + 1) * HD] = result[r * block : (r + 1) * block]
                if r:
                    kept = jnp.where(
                        lane >= r * (HD // ratio), total[r * block : (r + 1) * block], kept
                    )
            total_ref[low:high, :] = kept

    return pl.pallas_call(
        kernel,
        grid=(heads,),
        in_specs=[
            pl.BlockSpec((rows, wide), lambda i: (0, i)),
            pl.BlockSpec((rows, HD), lambda i: (0, 0)),
            pl.BlockSpec((rows, HD), lambda i: (0, 0)),
            pl.BlockSpec((1, HD), lambda i: (0, 0)),
            pl.BlockSpec((1, HD), lambda i: (0, 0)),
        ],
        out_specs=[
            pl.BlockSpec((rows, ratio * HD), lambda i: (0, i % 2 * (heads // 2) + i // 2)),
            pl.BlockSpec((rows, HD), lambda i: (0, i)),
        ],
        out_shape=[
            jax.ShapeDtypeStruct((rows, heads * ratio * HD), bf16),
            jax.ShapeDtypeStruct((rows, heads * HD), f32),
        ],
        compiler_params=pltpu.CompilerParams(vmem_limit_bytes=48 * 1024 * 1024),
        cost_estimate=SMALL,
        name="attend_forward",
    )(mixed, cosine, sine, gain_query, gain_key)


def attend_backward(
    mixed, cosine, sine, gain_query, gain_key, attended, totals, grad_att, part, parts, ratio, block
):
    heads = 2
    rows = mixed.shape[0]
    wide = (ratio + 2) * HD
    scale = HD ** (-0.5)
    factor = scale * LOG2E
    bf16 = jnp.bfloat16
    f32 = jnp.float32

    def kernel(
        mixed_ref, cos_ref, sin_ref, gq_ref, gk_ref, att_ref, total_ref, grad_ref,
        out_ref, dgq_ref, dgk_ref, key_sum, value_sum,
    ):
        cos = cos_ref[...]
        sin = sin_ref[...]
        gain_q = gq_ref[...]
        query = []
        query_inverse = []
        for r in range(ratio):
            turned, inverse = normal_rope(mixed_ref[:, r * HD : (r + 1) * HD], gain_q, cos, sin)
            query.append(turned.astype(bf16))
            query_inverse.append(inverse)
        raw_keys = mixed_ref[:, ratio * HD : (ratio + 1) * HD]
        keys, key_inverse = normal_rope(raw_keys, gk_ref[...], cos, sin)
        keys = keys.astype(bf16)
        values = mixed_ref[:, (ratio + 1) * HD :].astype(bf16)
        allowed = causal_mask(block, ratio)
        grad_gain = jnp.zeros((1, HD), f32)

        @pl.when(pl.program_id(0) == 0)
        def _():
            dgq_ref[...] = jnp.zeros_like(dgq_ref)
            dgk_ref[...] = jnp.zeros_like(dgk_ref)

        for number in reversed(range(rows // block)):
            low, high = number * block, (number + 1) * block
            stacked = jnp.concatenate([turned[low:high] for turned in query], axis=0)
            grads = []
            deltas = []
            for r in range(ratio):
                lane = r * (HD // ratio)
                inverse = 1.0 / total_ref[low:high, lane : lane + 1]
                columns = slice(r * HD, (r + 1) * HD)
                scaled = (grad_ref[low:high, columns].astype(f32) * inverse).astype(bf16)
                grads.append(scaled)
                deltas.append(
                    jnp.sum(
                        scaled.astype(f32) * att_ref[low:high, columns].astype(f32),
                        axis=-1,
                        keepdims=True,
                    )
                )
            grad = jnp.concatenate(grads, axis=0)
            delta = jnp.concatenate(deltas, axis=0)
            grad_query = None
            for start, end, masked in ((low, high, True), (0, low, False)):
                if end == start:
                    continue
                scores = split_product(stacked, keys[start:end], 1, 1)
                terms = jnp.exp2(scores * factor)
                if masked:
                    terms = jnp.where(allowed, terms, 0.0)
                grad_terms = split_product(grad, values[start:end], 1, 1)
                grad_scores = (terms * (grad_terms - delta)).astype(bf16)
                grad_values = split_product(terms.astype(bf16), grad, 0, 0)
                grad_keys = split_product(grad_scores, stacked, 0, 0)
                added = split_product(grad_scores, keys[start:end], 1, 0)
                grad_query = added if grad_query is None else grad_query + added
                if number == rows // block - 1:
                    value_sum[start:end, :] = grad_values
                    key_sum[start:end, :] = grad_keys
                else:
                    value_sum[start:end, :] += grad_values
                    key_sum[start:end, :] += grad_keys
            for r in range(ratio):
                columns = slice(r * HD, (r + 1) * HD)
                back, gain_part = normal_rope_back(
                    grad_query[r * block : (r + 1) * block] * scale,
                    mixed_ref[low:high, columns],
                    query_inverse[r][low:high],
                    gain_q,
                    cos[low:high],
                    sin[low:high],
                )
                out_ref[low:high, columns] = back.astype(bf16)
                grad_gain = grad_gain + gain_part
        dgq_ref[...] += grad_gain
        back, gain_part = normal_rope_back(
            key_sum[...] * scale, raw_keys, key_inverse, gk_ref[...], cos, sin
        )
        dgk_ref[...] += gain_part
        out_ref[:, ratio * HD : (ratio + 1) * HD] = back.astype(bf16)
        out_ref[:, (ratio + 1) * HD :] = value_sum[...].astype(bf16)

    return pl.pallas_call(
        kernel,
        grid=(heads,),
        in_specs=[
            pl.BlockSpec((rows, wide), lambda i: (0, part * 2 + i)),
            pl.BlockSpec((rows, HD), lambda i: (0, 0)),
            pl.BlockSpec((rows, HD), lambda i: (0, 0)),
            pl.BlockSpec((1, HD), lambda i: (0, 0)),
            pl.BlockSpec((1, HD), lambda i: (0, 0)),
            pl.BlockSpec((rows, ratio * HD), lambda i: (0, i * parts + part)),
            pl.BlockSpec((rows, HD), lambda i: (0, part * 2 + i)),
            pl.BlockSpec((rows, ratio * HD), lambda i: (0, i * parts + part)),
        ],
        out_specs=[
            pl.BlockSpec((rows, wide), lambda i: (0, i)),
            pl.BlockSpec((1, HD), lambda i: (0, 0)),
            pl.BlockSpec((1, HD), lambda i: (0, 0)),
        ],
        out_shape=[
            jax.ShapeDtypeStruct((rows, heads * wide), bf16),
            jax.ShapeDtypeStruct((1, HD), f32),
            jax.ShapeDtypeStruct((1, HD), f32),
        ],
        scratch_shapes=[pltpu.VMEM((rows, HD), f32), pltpu.VMEM((rows, HD), f32)],
        compiler_params=pltpu.CompilerParams(vmem_limit_bytes=48 * 1024 * 1024),
        cost_estimate=SMALL,
        name="attend_backward",
    )(mixed, cosine, sine, gain_query, gain_key, attended, totals, grad_att)


def paired_shards(
    hidden_in,
    out_grad,
    stretch_order,
    positions,
    qkv_weight,
    qkv_moment,
    qkv_square,
    out_weight,
    out_moment,
    out_square,
    gateup_weight,
    gateup_moment,
    gateup_square,
    down_weight,
    down_moment,
    down_square,
    gain_weight,
    gain_moment,
    gain_square,
):
    groups = lax.axis_size("group")
    copies = lax.axis_size("dp")
    sequences, local_len, width = hidden_in.shape
    seq_len = local_len * groups
    pieces = stretch_order.shape[0]
    chunk = seq_len // pieces
    held = pieces // groups
    ratio = H // KV
    heads = 2 * KV // groups
    ff = FF // groups
    bf16 = jnp.bfloat16
    f32 = jnp.float32
    member = lax.axis_index("group")
    copy = lax.axis_index("dp")
    half = member // 2
    rank = member % 2
    side = copy % 2
    depth = copies // 2

    def permute(value, target):
        pairs = []
        for d in range(copies):
            for g in range(groups):
                to_d, to_g = target(d, g)
                pairs.append((d * groups + g, to_d * groups + to_g))
        return lax.ppermute(value, ALL, pairs)

    def over_core(value):
        return permute(value, lambda d, g: (d, g ^ 1))

    def over_chip(value):
        return permute(value, lambda d, g: (d, g ^ 2))

    def over_diagonal(value):
        return permute(value, lambda d, g: (d, g ^ 3))

    def over_side(value):
        return permute(value, lambda d, g: (d ^ 1, g))

    def block_of(far, other_rank):
        at = half if not far else 1 - half
        return at * 2 + (rank if not other_rank else 1 - rank)

    def pick(array, index):
        return lax.dynamic_index_in_dim(array, index, 0, keepdims=False)

    def ordered(first_side, mine, theirs):
        return jnp.concatenate(
            [jnp.where(first_side, mine, theirs), jnp.where(first_side, theirs, mine)]
        )

    table = jnp.arange(pieces, dtype=jnp.int32)

    def places_of(stored):
        return jnp.sum(
            jnp.where(stored[:, None] == table[None, :], stretch_order[None, :], 0), axis=1
        )

    slots = jnp.arange(pieces, dtype=jnp.int32)
    slot_rank = jnp.where(slots < 2 * held, rank, 1 - rank)
    slot_half = jnp.where(slots // held % 2 == 0, half, 1 - half)
    all_targets = places_of((slot_half * 2 + slot_rank) * held + slots % held)
    own_targets, peer_targets = all_targets[: 2 * held], all_targets[2 * held :]
    start = pick(positions, half)[0] - all_targets[0] * chunk
    exponent = jnp.arange(HD // 2, dtype=f32) * (2.0 / HD)
    inverse = jnp.power(jnp.float32(ROPE_BASE), -exponent)
    places = (start + jnp.arange(seq_len, dtype=jnp.int32)).astype(f32)
    angle = places[:, None] * inverse[None, :]
    cosine_half, sine_half = jnp.cos(angle), jnp.sin(angle)
    cosine = jnp.concatenate([cosine_half, cosine_half], axis=-1)
    sine = jnp.concatenate([-sine_half, sine_half], axis=-1)

    parts = 2
    wide = (ratio + 2) * HD
    some = ff // parts
    where_at = jnp.stack([half, rank, side]).astype(jnp.int32)

    class Columns:
        def __init__(self, array, rows_array, kinds):
            self.to_chip, self.to_diagonal, self.to_core, self.near, self.far, self.rows = (
                cut_columns(array, rows_array, where_at, kinds, parts)
            )

        def joined(self):
            return join_columns(
                self.near, self.far, self.peer, self.chip, self.diagonal,
                self.chip_side, self.diagonal_side, where_at, parts,
            )

    def join_rows(own, chip, other_side):
        return jnp.concatenate([own.astype(bf16), ordered(side == 0, chip, other_side)], axis=0)

    gain_rows = gain_weight.shape[0]
    gain_pad = jnp.pad(gain_weight.astype(bf16), (0, 16 * width - gain_rows)).reshape(16, width)
    hidden_sent = jnp.concatenate([pick(hidden_in, 1 - half), gain_pad], axis=0)
    hidden_far = over_chip(hidden_sent)
    block_cols = H * HD // groups
    key_cols = KV * HD // groups
    qkv = Columns(
        tie(qkv_weight, hidden_sent),
        out_weight,
        [(0, block_cols), (H * HD, key_cols), ((H + KV) * HD, key_cols)],
    )
    qkv_chip = over_chip(jnp.stack([qkv.to_chip, qkv.rows]))
    qkv.diagonal = over_diagonal(qkv.to_diagonal)
    qkv.peer = over_core(qkv.to_core)
    gateup = Columns(
        tie(gateup_weight, qkv.to_chip, qkv.to_diagonal), down_weight, [(0, ff), (FF, ff)]
    )
    gateup.chip = over_chip(tie(gateup.to_chip, hidden_far))
    hidden_mine = jnp.concatenate(
        [pick(hidden_in, half), hidden_far[:local_len], gain_pad, hidden_far[local_len:]], axis=0
    )
    hidden_theirs = over_core(hidden_mine)
    gain_low = gain_pad.reshape(-1)[:gain_rows]
    gain_parts = [
        block.reshape(-1)[:gain_rows]
        for block in (
            hidden_theirs[2 * local_len : 2 * local_len + 16],
            hidden_far[local_len:],
            hidden_theirs[2 * local_len + 16 :],
        )
    ]
    gains = ordered(
        half == 0,
        ordered(rank == 0, gain_low, gain_parts[0]),
        ordered(rank == 0, gain_parts[1], gain_parts[2]),
    ).astype(f32)
    gain_one = gains[:D]
    gain_two = gains[D : 2 * D]
    gain_query = gains[2 * D : 2 * D + HD].reshape(1, HD)
    gain_key = gains[2 * D + HD :].reshape(1, HD)

    qkv_side = over_side(tie(qkv_chip, hidden_mine))
    gateup.diagonal = over_diagonal(tie(gateup.to_diagonal, qkv_chip))
    qkv.diagonal_side = over_side(qkv.diagonal)
    qkv.chip, qkv.chip_side = qkv_chip[0], qkv_side[0]
    w_out = join_rows(out_weight, qkv_chip[1], qkv_side[1])
    down_chip = over_chip(tie(gateup.rows, qkv.diagonal))
    gateup.chip_side = over_side(gateup.chip)
    gateup.diagonal_side = over_side(gateup.diagonal)
    grad_far = over_chip(tie(pick(out_grad, 1 - half), gateup.chip))
    gateup.peer = over_core(tie(gateup.to_core, qkv.peer))
    grad_mine = jnp.concatenate([pick(out_grad, half), grad_far], axis=0)
    grad_theirs = over_core(grad_mine)
    down_side = over_side(down_chip)

    hidden, normed_low = place_rows(hidden_mine, hidden_theirs, all_targets, chunk, gain_one)
    tokens = hidden.astype(f32)
    w_qkv = qkv.joined()
    mixed = split_product(normed_low, w_qkv, 1, 0)
    block = min(256, seq_len)
    attended, totals = attend_forward(
        mixed, cosine, sine, gain_query, gain_key, heads, ratio, block
    )
    branch = split_product(attended, w_out, 1, 0).astype(bf16)
    middle = tokens + (branch.astype(f32) + over_core(branch).astype(f32))
    second, pull_two = jax.vjp(rms_scale, middle, gain_two)
    second_low = second.astype(bf16)
    w_gateup = gateup.joined()
    gate_up = split_product(second_low, w_gateup, 1, 0)

    def gated_part(values, part):
        pieces_here = []
        for far in range(2):
            low = (part * 2 + far) * 2 * some
            pieces_here.append(
                jax.nn.silu(values[:, low : low + some]) * values[:, low + some : low + 2 * some]
            )
        return pieces_here

    def gated_all(values):
        found = [gated_part(values, part) for part in range(parts)]
        return jnp.concatenate(
            [found[part][far] for far in range(2) for part in range(parts)], axis=1
        )

    inner, pull_gate = jax.vjp(gated_all, gate_up)
    inner_low = inner.astype(bf16)
    (grad_result,) = place_rows(grad_mine, grad_theirs, all_targets, chunk, None)

    def half_columns(array, far):
        size = array.shape[1] // 2
        near_side = half == (1 if far else 0)
        return jnp.where(near_side, array[:, :size], array[:, size:])

    def far_columns(array, far):
        size = array.shape[1] // 2
        return array[:, size:] if far else array[:, :size]

    def far_first(array):
        size = array.shape[1] // 2
        return jnp.concatenate([array[:, size:], array[:, :size]], axis=1)

    def exchange(left_far, left_near, right):
        far = split_product(left_far, right, 0, 0).astype(bf16)
        received = over_chip(far)
        near = split_product(left_near, right, 0, 0).astype(bf16)
        return near, received

    def add(first, *others):
        total = first.astype(f32)
        for other in others:
            total = total + other.astype(f32)
        return total.astype(bf16)

    def swap_rows(near, received):
        received = far_first(received)
        lead = near.shape[0] // 2
        near = near.reshape(2, lead, -1)
        received = received.reshape(2, lead, -1)
        theirs = add(pick(near, 1 - rank), pick(received, 1 - rank))
        mine = add(pick(near, rank), pick(received, rank))
        return jnp.stack([mine, over_core(theirs)])

    def side_sum(value):
        value = value.reshape(2, depth, -1, value.shape[-1])
        return add(pick(value, side), over_side(pick(value, 1 - side)))

    deep_groups = [[d * 2 + x for d in range(depth)] for x in range(2)]

    def depth_all(value):
        return lax.psum(value, "dp", axis_index_groups=deep_groups)

    def side_gather(value):
        flat = value.reshape(-1, value.shape[-1])
        return ordered(side == 0, flat, over_side(flat))

    token = [None]

    def event(*values):
        if token[0] is None:
            return values
        return lax.optimization_barrier((*values, token[0]))[: len(values)]

    def passed(value):
        token[0] = value

    w_down = join_rows(down_weight, down_chip, down_side)
    down_near, down_received = exchange(
        far_columns(inner_low, True), far_columns(inner_low, False), grad_result
    )
    grad_inner = split_product(grad_result, w_down, 1, 1)
    (grad_gate_up,) = pull_gate(grad_inner)
    grad_gate_low = grad_gate_up.astype(bf16)
    second_near, second_far = half_columns(second_low, False), half_columns(second_low, True)
    part_cols = grad_gate_low.shape[1] // parts
    gateup_sent = [
        exchange(second_far, second_near, grad_gate_low[:, part * part_cols : (part + 1) * part_cols])
        for part in range(parts)
    ]
    second_part = split_product(grad_gate_low, w_gateup, 1, 1).astype(bf16)
    grad_second = second_part.astype(f32) + over_core(second_part).astype(f32)
    result_part = split_product(inner_low, w_down, 1, 0).astype(bf16)
    grad_mid_part, grad_gain_two = pull_two(grad_second)
    grad_middle = grad_result.astype(f32) + grad_mid_part
    grad_branch_low = grad_middle.astype(bf16)
    out_near, out_received = exchange(
        far_columns(attended, True), far_columns(attended, False), grad_branch_low
    )
    grad_att = split_product(grad_branch_low, w_out, 1, 1).astype(bf16)
    normed_near, normed_far = half_columns(normed_low, False), half_columns(normed_low, True)

    def share_rows(part):
        return take_rows(part, own_targets, chunk).astype(f32) + over_core(
            take_rows(part, peer_targets, chunk)
        ).astype(f32)

    def to_stored(rows_here):
        stored = rows_here.astype(bf16).reshape(2, local_len, width)
        from_far = over_chip(stored[1])
        first = jnp.where(half == 0, stored[0], from_far)
        last = jnp.where(half == 0, from_far, stored[0])
        return jnp.stack([first, last])

    def backward_part(part, grad_att):
        grad_part, grad_query_part, grad_key_part = attend_backward(
            mixed, cosine, sine, gain_query, gain_key, attended, totals, grad_att,
            part, parts, ratio, block,
        )
        return grad_part, grad_query_part[0], grad_key_part[0]

    def y_step(near, received):
        near, received = event(near, received)
        value = add(near, received)
        passed(value)
        return value

    def swap_step(near, received):
        near, received = event(near, received)
        value = swap_rows(near, received)
        passed(value)
        return value

    def x_parts(value):
        value = value.reshape(2, depth, -1, value.shape[-1])
        return pick(value, side), over_side(pick(value, 1 - side))

    def x_step(kept_received):
        value = add(*event(*kept_received))
        passed(value)
        return depth_all(value)

    def back_step(value):
        (value,) = event(value)
        flat = value.reshape(-1, value.shape[-1])
        received = over_side(flat)
        passed(flat)
        return flat, received

    def last_step(flat_received):
        flat, received = flat_received
        return ordered(side == 0, flat, received)

    down_x = x_parts(y_step(down_near, tie(down_received, grad_att)))
    grad_att = tie(grad_att, down_x[0])
    back_0 = backward_part(0, grad_att)
    qkv_0 = exchange(normed_far, normed_near, back_0[0])
    down_z = x_step((down_x[0], tie(down_x[1], qkv_0[0])))
    grad_att = tie(grad_att, token[0])
    back_1 = backward_part(1, grad_att)
    far_1 = split_product(normed_far, back_1[0], 0, 0).astype(bf16)
    near_1 = split_product(normed_near, back_1[0], 0, 0).astype(bf16)
    gateup_0 = swap_step(gateup_sent[0][0], tie(gateup_sent[0][1], near_1))
    gateup_0x = x_parts(gateup_0)
    normed_part = split_product(
        tie(back_0[0], token[0]), w_qkv[:, : 2 * wide], 1, 1
    ) + split_product(tie(back_1[0], token[0]), w_qkv[:, 2 * wide :], 1, 1)
    normed_part = normed_part.astype(bf16)
    down_b = back_step(tie(down_z, normed_part))
    gateup_0z = x_step(gateup_0x)
    gateup_1 = swap_step(*gateup_sent[1])
    received_1 = over_chip(tie(far_1, token[0]))
    gateup_1x = x_parts(gateup_1)
    grad_normed = share_rows(normed_part)
    own_tokens = take_rows(hidden, own_targets, chunk).astype(f32)
    unused, pull_one = jax.vjp(rms_scale, own_tokens, gain_one)
    grad_token_part, grad_gain_one = pull_one(grad_normed)
    input_rows = take_rows(grad_middle, own_targets, chunk) + grad_token_part
    down_sum = last_step(down_b)
    gateup_0b = back_step(gateup_0z)
    out_x = x_parts(y_step(out_near, out_received))
    gateup_1z = x_step(gateup_1x)
    gateup_0sum = last_step(gateup_0b)
    qkv_0x = x_parts(swap_step(*qkv_0))
    gateup_1b = back_step(gateup_1z)
    out_z = x_step(out_x)
    out_b = back_step(out_z)
    qkv_0z = x_step(qkv_0x)
    qkv_1x = x_parts(swap_step(near_1, received_1))
    layer_out = to_stored(
        take_rows(middle, own_targets, chunk) + share_rows(tie(result_part, token[0]))
    )
    input_grad = to_stored(tie(input_rows, token[0]))
    gateup_1sum = last_step(gateup_1b)
    qkv_0b = back_step(qkv_0z)
    qkv_1z = x_step(qkv_1x)
    out_sum = last_step(out_b)
    qkv_1b = back_step(qkv_1z)
    qkv_0sum = last_step(qkv_0b)
    qkv_1sum = last_step(qkv_1b)
    gateup_sums = [gateup_0sum, gateup_1sum]
    qkv_sums = [qkv_0sum, qkv_1sum]
    gain_parts = [back_0[1:], back_1[1:]]
    total_down = down_sum.astype(f32)
    total_out = out_sum.astype(f32)

    def owner_blocks(totals_of_parts):
        blocks = []
        for block_number in range(groups):
            far = (block_number // 2) ^ half
            peer = (block_number % 2) ^ rank
            for total in totals_of_parts:
                lead = total.shape[0] // 2
                cols = total.shape[1] // 2
                stacked = total.reshape(2, lead, 2 * cols)
                rows_here = pick(stacked, peer)
                blocks.append(jnp.where(far == 0, rows_here[:, :cols], rows_here[:, cols:]))
        return blocks

    gateup_blocks = owner_blocks(gateup_sums)
    total_gateup = jnp.concatenate(
        [blocked[:, :some] for blocked in gateup_blocks]
        + [blocked[:, some:] for blocked in gateup_blocks],
        axis=1,
    ).astype(f32)
    head_blocks = owner_blocks(qkv_sums)
    total_qkv = jnp.concatenate(
        [blocked[:, : ratio * HD] for blocked in head_blocks]
        + [blocked[:, ratio * HD : (ratio + 1) * HD] for blocked in head_blocks]
        + [blocked[:, (ratio + 1) * HD :] for blocked in head_blocks],
        axis=1,
    ).astype(f32)
    counted = jnp.where(rank == 0, 1.0, 0.0).astype(f32)
    total_gains = jnp.concatenate(
        [
            grad_gain_one,
            grad_gain_two * counted,
            sum(pair[0] for pair in gain_parts),
            sum(pair[1] for pair in gain_parts),
        ]
    )
    total_gains = total_gains + over_core(total_gains)
    total_gains = total_gains + over_chip(total_gains)
    total_gains = total_gains + over_side(total_gains)
    total_gains = lax.psum(tie(total_gains, token[0]), "dp", axis_index_groups=deep_groups)
    gain_rows = gain_weight.shape[0]
    total_gain = lax.dynamic_slice_in_dim(total_gains, member * gain_rows, gain_rows, 0)

    out_fan = H * HD * 8 // seq_len
    qkv_new = adam_step(qkv_weight, qkv_moment, qkv_square, total_qkv, LR_MULT * D ** (-0.5), DECAY)
    out_new = adam_step(
        out_weight, out_moment, out_square, total_out, LR_MULT * out_fan ** (-0.5), DECAY
    )
    gateup_new = adam_step(
        gateup_weight, gateup_moment, gateup_square, total_gateup, LR_MULT * D ** (-0.5), DECAY
    )
    down_new = adam_step(
        down_weight, down_moment, down_square, total_down, LR_MULT * FF ** (-0.5), DECAY
    )
    gain_new = adam_step(gain_weight, gain_moment, gain_square, total_gain, GAIN_RATE, 0.0)
    return (layer_out, input_grad, *qkv_new, *out_new, *gateup_new, *down_new, *gain_new)


def shards(hidden_in, *others):
    groups = lax.axis_size("group")
    copies = lax.axis_size("dp")
    two_ranks = hidden_in.shape[0] == 2 and groups == 4
    if two_ranks and copies % 2 == 0:
        return paired_shards(hidden_in, *others)
    return general_shards(hidden_in, *others)


def solution(mesh):
    return jax.shard_map(
        shards,
        mesh=mesh,
        in_specs=(
            P("dp", "group", None),
            P("dp", "group", None),
            P(),
            P("dp", "group"),
            P("group", None),
            P("group", None),
            P("group", None),
            P("group", None),
            P("group", None),
            P("group", None),
            P("group", None),
            P("group", None),
            P("group", None),
            P("group", None),
            P("group", None),
            P("group", None),
            P("group"),
            P("group"),
            P("group"),
        ),
        out_specs=(
            P("dp", "group", None),
            P("dp", "group", None),
            P("group", None),
            P("group", None),
            P("group", None),
            P("group", None),
            P("group", None),
            P("group", None),
            P("group", None),
            P("group", None),
            P("group", None),
            P("group", None),
            P("group", None),
            P("group", None),
            P("group"),
            P("group"),
            P("group"),
        ),
        check_vma=False,
    )
```

```python
import jax
import jax.numpy as jnp
from jax import lax
from jax.experimental import pallas as pl
from jax.experimental.pallas import tpu as pltpu
from jax.sharding import PartitionSpec as P

D = 1024
H = 16
KV = 8
HD = 128
FF = 3072
STEP = 10


EPSILON = 1e-06
ROPE_BASE = 1000000.0
BETA_ONE = 0.9
BETA_TWO = 0.95
ADAM_EPSILON = 1e-08
DECAY = 0.1
LR_MULT = 3.0
GAIN_RATE = 0.3
MASKED = -1e30
START_TOP = -1e29


def rms_scale(values, gain):
    mean_square = jnp.mean(values * values, axis=-1, keepdims=True)
    return values * lax.rsqrt(mean_square + EPSILON) * gain


def rotate(values, cosine, sine):
    half = values.shape[-1] // 2
    turned = jnp.concatenate([-values[..., half:], values[..., :half]], axis=-1)
    return values * cosine + turned * sine


def rope_tables(places):
    exponent = jnp.arange(HD // 2, dtype=jnp.float32) * (2.0 / HD)
    inverse = jnp.power(jnp.float32(ROPE_BASE), -exponent)
    angle = places.astype(jnp.float32)[:, None] * inverse[None, :]
    angle = jnp.concatenate([angle, angle], axis=-1)
    return (jnp.cos(angle), jnp.sin(angle))


def split_heads(mixed, query_gain, key_gain, cosine, sine):
    row_count = mixed.shape[0]
    query = mixed[:, : H * HD].reshape(row_count, H, HD)
    keys = mixed[:, H * HD : (H + KV) * HD].reshape(row_count, KV, HD)
    values = mixed[:, (H + KV) * HD :].reshape(row_count, KV, HD)
    query = rotate(rms_scale(query, query_gain), cosine[:, None, :], sine[:, None, :])
    keys = rotate(rms_scale(keys, key_gain), cosine[:, None, :], sine[:, None, :])
    return (query, keys, values)


def gated(gate_up):
    half = gate_up.shape[1] // 2
    return jax.nn.silu(gate_up[:, :half]) * gate_up[:, half:]


def real_places(stretch_list, start, count, half_stretch):
    stored = start + jnp.arange(count, dtype=jnp.int32)
    piece_index = stored // half_stretch
    table = jnp.arange(stretch_list.shape[0], dtype=jnp.int32)
    picked = jnp.sum(
        jnp.where(piece_index[:, None] == table[None, :], stretch_list[None, :], 0), axis=1
    )
    return picked * half_stretch + stored % half_stretch


def by_blocks(block_fn, carry, piece, width):
    count = piece[0].shape[1]

    def advance(state, number):
        sliced = tuple(
            (lax.dynamic_slice_in_dim(member, number * width, width, 1) for member in piece)
        )
        return (block_fn(state, sliced, number * width), None)

    state, unused = lax.scan(advance, carry, jnp.arange(count // width, dtype=jnp.int32))
    return state


def adam_step(weight, moment, square, grad, rate, decay):
    moment_new = BETA_ONE * moment + (1.0 - BETA_ONE) * grad
    square_new = BETA_TWO * square + (1.0 - BETA_TWO) * grad * grad
    ratio = (
        moment_new
        / (1.0 - BETA_ONE**STEP)
        / (jnp.sqrt(square_new / (1.0 - BETA_TWO**STEP)) + ADAM_EPSILON)
    )
    return (weight - rate * (ratio + decay * weight), moment_new, square_new)


def general_shards(
    hidden_in,
    out_grad,
    stretch_order,
    positions,
    qkv_weight,
    qkv_moment,
    qkv_square,
    out_weight,
    out_moment,
    out_square,
    gateup_weight,
    gateup_moment,
    gateup_square,
    down_weight,
    down_moment,
    down_square,
    gain_weight,
    gain_moment,
    gain_square,
):
    groups = lax.axis_size("group")
    sequences, local_len, width = hidden_in.shape
    half_stretch = local_len // 2
    seq_len = local_len * groups
    ratio = H // KV
    row_count = sequences * local_len
    scale = HD ** (-0.5)
    bf16 = jnp.bfloat16
    f32 = jnp.float32
    w_qkv, w_out, w_gateup, w_down, gains_low = (
        lax.all_gather(qkv_weight.astype(bf16), "group", axis=0, tiled=True),
        lax.all_gather(out_weight.astype(bf16), "group", axis=0, tiled=True),
        lax.all_gather(gateup_weight.astype(bf16), "group", axis=0, tiled=True),
        lax.all_gather(down_weight.astype(bf16), "group", axis=0, tiled=True),
        lax.all_gather(gain_weight.astype(bf16), "group", axis=0, tiled=True),
    )
    gains = gains_low.astype(f32)
    gain_one = gains[:D]
    gain_two = gains[D : 2 * D]
    gain_query = gains[2 * D : 2 * D + HD]
    gain_key = gains[2 * D + HD :]
    member = lax.axis_index("group")
    query_places = real_places(stretch_order, member * local_len, local_len, half_stretch)
    cosine, sine = rope_tables(positions.reshape(row_count))
    tokens = hidden_in.reshape(row_count, width).astype(f32)
    normed, pull_one = jax.vjp(rms_scale, tokens, gain_one)
    normed_low = normed.astype(bf16)
    mixed = jnp.dot(normed_low, w_qkv, preferred_element_type=f32)

    def heads_of(mixed_rows, query_gain, key_gain):
        return split_heads(mixed_rows, query_gain, key_gain, cosine, sine)

    (query, keys, values), pull_heads = jax.vjp(heads_of, mixed, gain_query, gain_key)
    query_low = query.astype(bf16).reshape(sequences, local_len, KV, ratio, HD)
    keys_low = keys.astype(bf16).reshape(sequences, local_len, KV, HD)
    values_low = values.astype(bf16).reshape(sequences, local_len, KV, HD)

    def scores_for(keys_piece, start):
        count = keys_piece.shape[1]
        key_places = real_places(stretch_order, start, count, half_stretch)
        allowed = key_places[None, :] <= query_places[:, None]
        raw_scores = (
            jnp.einsum("sqkrd,spkd->skrqp", query_low, keys_piece, preferred_element_type=f32)
            * scale
        )
        return jnp.where(allowed, raw_scores, MASKED)

    def forward_block(carry, piece, start):
        top_old, total_old, accum_old = carry
        scores = scores_for(piece[0], start)
        top_new = jnp.maximum(top_old, jnp.max(scores, axis=-1))
        factor = jnp.exp(top_old - top_new)
        exp_terms = jnp.exp(scores - top_new[..., None])
        total_new = total_old * factor + jnp.sum(exp_terms, axis=-1)
        update = jnp.einsum(
            "skrqp,spkd->skrqd", exp_terms.astype(bf16), piece[1], preferred_element_type=f32
        )
        return (top_new, total_new, accum_old * factor[..., None] + update)

    start_state = (
        jnp.full((sequences, KV, ratio, local_len), START_TOP, f32),
        jnp.zeros((sequences, KV, ratio, local_len), f32),
        jnp.zeros((sequences, KV, ratio, local_len, HD), f32),
    )
    top, total, accum = by_blocks(
        forward_block,
        start_state,
        (
            lax.all_gather(keys_low, "group", axis=1, tiled=True),
            lax.all_gather(values_low, "group", axis=1, tiled=True),
        ),
        local_len,
    )
    attended = accum / total[..., None]
    log_total = top + jnp.log(total)
    attended_low = jnp.transpose(attended, (0, 3, 1, 2, 4)).reshape(row_count, H * HD).astype(bf16)
    middle = tokens + jnp.dot(attended_low, w_out, preferred_element_type=f32)
    second, pull_two = jax.vjp(rms_scale, middle, gain_two)
    second_low = second.astype(bf16)
    gate_up = jnp.dot(second_low, w_gateup, preferred_element_type=f32)
    inner, pull_gate = jax.vjp(gated, gate_up)
    inner_low = inner.astype(bf16)
    result = middle + jnp.dot(inner_low, w_down, preferred_element_type=f32)
    layer_out = result.astype(bf16).reshape(sequences, local_len, width)
    grad_result_low = out_grad.reshape(row_count, width)
    grad_down = jnp.einsum("ti,to->io", inner_low, grad_result_low, preferred_element_type=f32)
    grad_inner = jnp.einsum("to,io->ti", grad_result_low, w_down, preferred_element_type=f32)
    (grad_gate_up,) = pull_gate(grad_inner)
    grad_gate_low = grad_gate_up.astype(bf16)
    grad_gateup = jnp.einsum("td,tf->df", second_low, grad_gate_low, preferred_element_type=f32)
    grad_second = jnp.einsum("tf,df->td", grad_gate_low, w_gateup, preferred_element_type=f32)
    grad_mid_part, grad_gain_two = pull_two(grad_second)
    grad_middle = grad_result_low.astype(f32) + grad_mid_part
    grad_branch_low = grad_middle.astype(bf16)
    grad_out = jnp.einsum("ta,td->ad", attended_low, grad_branch_low, preferred_element_type=f32)
    grad_att = jnp.einsum("td,ad->ta", grad_branch_low, w_out, preferred_element_type=f32).astype(
        bf16
    )
    grad_att_heads = jnp.transpose(
        grad_att.reshape(sequences, local_len, KV, ratio, HD), (0, 2, 3, 1, 4)
    )
    delta = jnp.sum(grad_att_heads.astype(f32) * attended, axis=-1)

    def backward_block(carry, piece, start):
        grad_query, grad_pairs = carry
        keys_piece, values_piece = piece
        count = keys_piece.shape[1]
        scores = scores_for(keys_piece, start)
        probs = jnp.exp(scores - log_total[..., None])
        grad_values = jnp.einsum(
            "skrqp,skrqd->spkd", probs.astype(bf16), grad_att_heads, preferred_element_type=f32
        )
        grad_probs = jnp.einsum(
            "skrqd,spkd->skrqp", grad_att_heads, values_piece, preferred_element_type=f32
        )
        grad_scores = (probs * (grad_probs - delta[..., None])).astype(bf16)
        grad_query = (
            grad_query
            + jnp.einsum("skrqp,spkd->skrqd", grad_scores, keys_piece, preferred_element_type=f32)
            * scale
        )
        grad_keys = (
            jnp.einsum("skrqp,sqkrd->spkd", grad_scores, query_low, preferred_element_type=f32)
            * scale
        )
        current = lax.dynamic_slice_in_dim(grad_pairs, start, count, 1)
        joined = current + jnp.concatenate([grad_keys, grad_values], axis=-1)
        return (grad_query, lax.dynamic_update_slice_in_dim(grad_pairs, joined, start, 1))

    back_state = (
        jnp.zeros((sequences, KV, ratio, local_len, HD), f32),
        jnp.zeros((sequences, seq_len, KV, 2 * HD), f32),
    )
    grad_query, grad_pairs = by_blocks(
        backward_block,
        back_state,
        (
            lax.all_gather(keys_low, "group", axis=1, tiled=True),
            lax.all_gather(values_low, "group", axis=1, tiled=True),
        ),
        local_len,
    )
    grad_local = lax.psum_scatter(
        grad_pairs.astype(jnp.bfloat16), "group", scatter_dimension=1, tiled=True
    ).astype(jnp.float32)
    grad_keys = grad_local[..., :HD].reshape(row_count, KV, HD)
    grad_values = grad_local[..., HD:].reshape(row_count, KV, HD)
    grad_query = jnp.transpose(grad_query, (0, 3, 1, 2, 4)).reshape(row_count, H, HD)
    grad_mixed, grad_gain_query, grad_gain_key = pull_heads((grad_query, grad_keys, grad_values))
    grad_mixed_low = grad_mixed.astype(bf16)
    grad_qkv = jnp.einsum("td,tc->dc", normed_low, grad_mixed_low, preferred_element_type=f32)
    grad_normed = jnp.einsum("tc,dc->td", grad_mixed_low, w_qkv, preferred_element_type=f32)
    grad_token_part, grad_gain_one = pull_one(grad_normed)
    input_grad = (grad_middle + grad_token_part).astype(bf16).reshape(sequences, local_len, width)
    grad_gains = jnp.concatenate([grad_gain_one, grad_gain_two, grad_gain_query, grad_gain_key])
    part_qkv, part_out, part_gateup, part_down, part_gain = (
        lax.psum_scatter(
            grad_qkv.astype(jnp.bfloat16), "group", scatter_dimension=0, tiled=True
        ).astype(jnp.float32),
        lax.psum_scatter(
            grad_out.astype(jnp.bfloat16), "group", scatter_dimension=0, tiled=True
        ).astype(jnp.float32),
        lax.psum_scatter(
            grad_gateup.astype(jnp.bfloat16), "group", scatter_dimension=0, tiled=True
        ).astype(jnp.float32),
        lax.psum_scatter(
            grad_down.astype(jnp.bfloat16), "group", scatter_dimension=0, tiled=True
        ).astype(jnp.float32),
        lax.psum_scatter(
            grad_gains.astype(jnp.bfloat16), "group", scatter_dimension=0, tiled=True
        ).astype(jnp.float32),
    )
    total_qkv, total_out, total_gateup, total_down, total_gain = (
        lax.psum(part_qkv.astype(jnp.bfloat16), "dp").astype(jnp.float32),
        lax.psum(part_out.astype(jnp.bfloat16), "dp").astype(jnp.float32),
        lax.psum(part_gateup.astype(jnp.bfloat16), "dp").astype(jnp.float32),
        lax.psum(part_down.astype(jnp.bfloat16), "dp").astype(jnp.float32),
        lax.psum(part_gain.astype(jnp.bfloat16), "dp").astype(jnp.float32),
    )
    out_fan = H * HD * 8 // seq_len
    qkv_new = adam_step(qkv_weight, qkv_moment, qkv_square, total_qkv, LR_MULT * D ** (-0.5), DECAY)
    out_new = adam_step(
        out_weight, out_moment, out_square, total_out, LR_MULT * out_fan ** (-0.5), DECAY
    )
    gateup_new = adam_step(
        gateup_weight, gateup_moment, gateup_square, total_gateup, LR_MULT * D ** (-0.5), DECAY
    )
    down_new = adam_step(
        down_weight, down_moment, down_square, total_down, LR_MULT * FF ** (-0.5), DECAY
    )
    gain_new = adam_step(gain_weight, gain_moment, gain_square, total_gain, GAIN_RATE, 0.0)
    return (
        layer_out,
        input_grad,
        qkv_new[0],
        qkv_new[1],
        qkv_new[2],
        out_new[0],
        out_new[1],
        out_new[2],
        gateup_new[0],
        gateup_new[1],
        gateup_new[2],
        down_new[0],
        down_new[1],
        down_new[2],
        gain_new[0],
        gain_new[1],
        gain_new[2],
    )


ALL = ("dp", "group")
LOG2E = 1.4426950408889634
SMALL = pl.CostEstimate(flops=1000000, bytes_accessed=100000, transcendentals=0)


def tie(value, *others):
    return lax.optimization_barrier((value, *others))[0]


def split_product(left, right, left_dim, right_dim):
    return lax.dot_general(
        left, right, (((left_dim,), (right_dim,)), ((), ())), preferred_element_type=jnp.float32
    )


def place_rows(mine, theirs, targets, chunk, gain):
    count = targets.shape[0]
    width = mine.shape[1]
    near = mine.shape[0] // chunk
    with_norm = gain is not None

    def kernel(targets_ref, mine_ref, theirs_ref, *refs):
        step = pl.program_id(0)
        rows = jnp.where(step < near, mine_ref[...], theirs_ref[...])
        if with_norm:
            gain_ref, placed, normed = refs
            wide = rows.astype(jnp.float32)
            normed[...] = rms_scale(wide, gain_ref[...]).astype(jnp.bfloat16)
        else:
            (placed,) = refs
        placed[...] = rows

    def target_row(i, targets_ref):
        return (targets_ref[i], 0)

    in_specs = [
        pl.BlockSpec((chunk, width), lambda i, targets_ref: (jnp.minimum(i, near - 1), 0)),
        pl.BlockSpec((chunk, width), lambda i, targets_ref: (jnp.maximum(i - near, 0), 0)),
    ]
    operands = [mine, theirs]
    outputs = 1
    if with_norm:
        in_specs.append(pl.BlockSpec((1, width), lambda i, targets_ref: (0, 0)))
        operands.append(gain.reshape(1, width))
        outputs = 2
    shape = jax.ShapeDtypeStruct((count * chunk, width), mine.dtype)
    return pl.pallas_call(
        kernel,
        out_shape=[shape] * outputs,
        grid_spec=pltpu.PrefetchScalarGridSpec(
            num_scalar_prefetch=1,
            grid=(count,),
            in_specs=in_specs,
            out_specs=[pl.BlockSpec((chunk, width), target_row)] * outputs,
        ),
        cost_estimate=SMALL,
        name="place_rows",
    )(targets, *operands)


def cut_columns(array, rows_array, where_at, kinds, parts):
    lead, total = array.shape
    groups = 4
    kept = total // groups
    rows_lead, rows_width = rows_array.shape

    def kernel(at_ref, *refs):
        sources = refs[: len(kinds)]
        rows_ref = refs[len(kinds)]
        chip, diagonal, core, near, far, rows_out = refs[len(kinds) + 1 :]
        step = pl.program_id(0)
        for number, target in enumerate(
            (chip, diagonal, core.at[0], core.at[1], near, far)
        ):

            @pl.when(step == number)
            def _(target=target):
                low = 0
                for part in range(parts):
                    for source, (first, size) in zip(sources, kinds):
                        width = size // parts
                        target[:, low : low + width] = source[
                            :, part * width : (part + 1) * width
                        ].astype(jnp.bfloat16)
                        low += width

        @pl.when(step == 0)
        def _():
            rows_out[...] = rows_ref[...].astype(jnp.bfloat16)

    def block_at(step, at_ref):
        half, rank, side = at_ref[0], at_ref[1], at_ref[2]
        sent = jnp.where(side == 0, 1 - half, half)
        pair = jnp.where(
            step < 2, sent, jnp.where((step == 2) | (step == 4), half, 1 - half)
        )
        other = (step == 1) | (step == 2) | (step == 3)
        return pair * 2 + jnp.where(other, 1 - rank, rank)

    def source_spec(first, size):
        return pl.BlockSpec(
            (lead, size), lambda i, at_ref: (0, first // size + block_at(i, at_ref))
        )

    flat = pl.BlockSpec((lead, kept), lambda i, at_ref: (0, 0))
    pair = pl.BlockSpec((2, lead, kept), lambda i, at_ref: (0, 0, 0))
    half_rows = (rows_lead // 2, rows_width)
    single = jax.ShapeDtypeStruct((lead, kept), jnp.bfloat16)
    return pl.pallas_call(
        kernel,
        out_shape=[
            single,
            single,
            jax.ShapeDtypeStruct((2, lead, kept), jnp.bfloat16),
            single,
            single,
            jax.ShapeDtypeStruct(half_rows, jnp.bfloat16),
        ],
        grid_spec=pltpu.PrefetchScalarGridSpec(
            num_scalar_prefetch=1,
            grid=(6,),
            in_specs=[source_spec(first, size) for first, size in kinds]
            + [pl.BlockSpec(half_rows, lambda i, at_ref: (at_ref[2], 0))],
            out_specs=[flat, flat, pair, flat, flat]
            + [pl.BlockSpec(half_rows, lambda i, at_ref: (0, 0))],
        ),
        compiler_params=pltpu.CompilerParams(vmem_limit_bytes=48 * 1024 * 1024),
        cost_estimate=SMALL,
        name="cut_columns",
    )(where_at, *([array] * len(kinds)), rows_array)


def join_columns(own_near, own_far, peer, chip, diagonal, chip_side, diagonal_side, where_at, parts):
    lead, cols = own_near.shape
    width = cols // parts

    def kernel(
        at_ref, near_ref, far_ref, peer_ref, chip_ref, diag_ref, chip_x_ref, diag_x_ref, out_ref
    ):
        step = pl.program_id(0)
        same_half = step // 2 == at_ref[0]
        same_rank = step % 2 == at_ref[1]
        even = at_ref[2] == 0

        def put(condition, first, second):
            @pl.when(condition)
            def _():
                for part in range(parts):
                    columns = slice(part * width, (part + 1) * width)
                    low = 2 * part * width
                    out_ref[:, low : low + width] = first[:, columns]
                    out_ref[:, low + width : low + 2 * width] = second[:, columns]

        put(same_half & same_rank, near_ref, far_ref)
        put(same_half & ~same_rank, peer_ref.at[0], peer_ref.at[1])
        put(~same_half & same_rank & even, chip_ref, chip_x_ref)
        put(~same_half & same_rank & ~even, chip_x_ref, chip_ref)
        put(~same_half & ~same_rank & even, diag_ref, diag_x_ref)
        put(~same_half & ~same_rank & ~even, diag_x_ref, diag_ref)

    flat = pl.BlockSpec((lead, cols), lambda i, at_ref: (0, 0))
    pair = pl.BlockSpec((2, lead, cols), lambda i, at_ref: (0, 0, 0))
    return pl.pallas_call(
        kernel,
        out_shape=jax.ShapeDtypeStruct((4 * lead, 2 * cols), own_near.dtype),
        grid_spec=pltpu.PrefetchScalarGridSpec(
            num_scalar_prefetch=1,
            grid=(4,),
            in_specs=[flat, flat, pair, flat, flat, flat, flat],
            out_specs=pl.BlockSpec((lead, 2 * cols), lambda i, at_ref: (i, 0)),
        ),
        compiler_params=pltpu.CompilerParams(vmem_limit_bytes=48 * 1024 * 1024),
        cost_estimate=SMALL,
        name="join_columns",
    )(where_at, own_near, own_far, peer, chip, diagonal, chip_side, diagonal_side)


def take_rows(rows, sources, chunk):
    return jnp.concatenate(
        [
            lax.dynamic_slice_in_dim(rows, sources[number] * chunk, chunk, 0)
            for number in range(sources.shape[0])
        ],
        axis=0,
    )


def normal_rope(raw, gain, cosine, sine):
    inverse = lax.rsqrt(jnp.mean(raw * raw, axis=-1, keepdims=True) + EPSILON)
    scaled = raw * inverse * gain
    return scaled * cosine + pltpu.roll(scaled, HD // 2, 1) * sine, inverse


def normal_rope_back(grad, raw, inverse, gain, cosine, sine):
    grad_scaled = grad * cosine + pltpu.roll(grad * sine, HD // 2, 1)
    unit = raw * inverse
    grad_gain = jnp.sum(grad_scaled * unit, axis=0, keepdims=True)
    weighted = grad_scaled * gain
    shift = jnp.mean(weighted * unit, axis=-1, keepdims=True)
    return inverse * (weighted - unit * shift), grad_gain


def causal_mask(block, ratio):
    row = lax.broadcasted_iota(jnp.int32, (ratio * block, block), 0) % block
    column = lax.broadcasted_iota(jnp.int32, (ratio * block, block), 1)
    return column <= row


def attend_forward(mixed, cosine, sine, gain_query, gain_key, heads, ratio, block):
    rows = mixed.shape[0]
    wide = (ratio + 2) * HD
    factor = HD ** (-0.5) * LOG2E
    bf16 = jnp.bfloat16
    f32 = jnp.float32

    def kernel(mixed_ref, cos_ref, sin_ref, gq_ref, gk_ref, att_ref, total_ref):
        cos = cos_ref[...]
        sin = sin_ref[...]
        query = [
            normal_rope(mixed_ref[:, r * HD : (r + 1) * HD], gq_ref[...], cos, sin)[0].astype(bf16)
            for r in range(ratio)
        ]
        keys = normal_rope(mixed_ref[:, ratio * HD : (ratio + 1) * HD], gk_ref[...], cos, sin)[0]
        keys = keys.astype(bf16)
        values = mixed_ref[:, (ratio + 1) * HD :].astype(bf16)
        values = jnp.concatenate([values, jnp.ones((rows, HD), bf16)], axis=1)
        allowed = causal_mask(block, ratio)
        lane = lax.broadcasted_iota(jnp.int32, (block, HD), 1)
        for number in range(rows // block):
            low, high = number * block, (number + 1) * block
            stacked = jnp.concatenate([part[low:high] for part in query], axis=0)
            scores = split_product(stacked, keys[low:high], 1, 1)
            terms = jnp.where(allowed, jnp.exp2(scores * factor), 0.0).astype(bf16)
            joined = split_product(terms, values[low:high], 1, 0)
            if low:
                scores = split_product(stacked, keys[:low], 1, 1)
                terms = jnp.exp2(scores * factor).astype(bf16)
                joined = joined + split_product(terms, values[:low], 1, 0)
            total = joined[:, HD:]
            result = (joined[:, :HD] / total).astype(bf16)
            kept = total[:block]
            for r in range(ratio):
                att_ref[low:high, r * HD : (r + 1) * HD] = result[r * block : (r + 1) * block]
                if r:
                    kept = jnp.where(
                        lane >= r * (HD // ratio), total[r * block : (r + 1) * block], kept
                    )
            total_ref[low:high, :] = kept

    return pl.pallas_call(
        kernel,
        grid=(heads,),
        in_specs=[
            pl.BlockSpec((rows, wide), lambda i: (0, i)),
            pl.BlockSpec((rows, HD), lambda i: (0, 0)),
            pl.BlockSpec((rows, HD), lambda i: (0, 0)),
            pl.BlockSpec((1, HD), lambda i: (0, 0)),
            pl.BlockSpec((1, HD), lambda i: (0, 0)),
        ],
        out_specs=[
            pl.BlockSpec((rows, ratio * HD), lambda i: (0, i % 2 * (heads // 2) + i // 2)),
            pl.BlockSpec((rows, HD), lambda i: (0, i)),
        ],
        out_shape=[
            jax.ShapeDtypeStruct((rows, heads * ratio * HD), bf16),
            jax.ShapeDtypeStruct((rows, heads * HD), f32),
        ],
        compiler_params=pltpu.CompilerParams(vmem_limit_bytes=48 * 1024 * 1024),
        cost_estimate=SMALL,
        name="attend_forward",
    )(mixed, cosine, sine, gain_query, gain_key)


def attend_backward(
    mixed, cosine, sine, gain_query, gain_key, attended, totals, grad_att, part, parts, ratio, block
):
    heads = 2
    rows = mixed.shape[0]
    wide = (ratio + 2) * HD
    scale = HD ** (-0.5)
    factor = scale * LOG2E
    bf16 = jnp.bfloat16
    f32 = jnp.float32

    def kernel(
        mixed_ref, cos_ref, sin_ref, gq_ref, gk_ref, att_ref, total_ref, grad_ref,
        out_ref, dgq_ref, dgk_ref, key_sum, value_sum,
    ):
        cos = cos_ref[...]
        sin = sin_ref[...]
        gain_q = gq_ref[...]
        query = []
        query_inverse = []
        for r in range(ratio):
            turned, inverse = normal_rope(mixed_ref[:, r * HD : (r + 1) * HD], gain_q, cos, sin)
            query.append(turned.astype(bf16))
            query_inverse.append(inverse)
        raw_keys = mixed_ref[:, ratio * HD : (ratio + 1) * HD]
        keys, key_inverse = normal_rope(raw_keys, gk_ref[...], cos, sin)
        keys = keys.astype(bf16)
        values = mixed_ref[:, (ratio + 1) * HD :].astype(bf16)
        allowed = causal_mask(block, ratio)
        grad_gain = jnp.zeros((1, HD), f32)

        @pl.when(pl.program_id(0) == 0)
        def _():
            dgq_ref[...] = jnp.zeros_like(dgq_ref)
            dgk_ref[...] = jnp.zeros_like(dgk_ref)

        for number in reversed(range(rows // block)):
            low, high = number * block, (number + 1) * block
            stacked = jnp.concatenate([turned[low:high] for turned in query], axis=0)
            grads = []
            deltas = []
            for r in range(ratio):
                lane = r * (HD // ratio)
                inverse = 1.0 / total_ref[low:high, lane : lane + 1]
                columns = slice(r * HD, (r + 1) * HD)
                scaled = (grad_ref[low:high, columns].astype(f32) * inverse).astype(bf16)
                grads.append(scaled)
                deltas.append(
                    jnp.sum(
                        scaled.astype(f32) * att_ref[low:high, columns].astype(f32),
                        axis=-1,
                        keepdims=True,
                    )
                )
            grad = jnp.concatenate(grads, axis=0)
            delta = jnp.concatenate(deltas, axis=0)
            grad_query = None
            for start, end, masked in ((low, high, True), (0, low, False)):
                if end == start:
                    continue
                scores = split_product(stacked, keys[start:end], 1, 1)
                terms = jnp.exp2(scores * factor)
                if masked:
                    terms = jnp.where(allowed, terms, 0.0)
                grad_terms = split_product(grad, values[start:end], 1, 1)
                grad_scores = (terms * (grad_terms - delta)).astype(bf16)
                grad_values = split_product(terms.astype(bf16), grad, 0, 0)
                grad_keys = split_product(grad_scores, stacked, 0, 0)
                added = split_product(grad_scores, keys[start:end], 1, 0)
                grad_query = added if grad_query is None else grad_query + added
                if number == rows // block - 1:
                    value_sum[start:end, :] = grad_values
                    key_sum[start:end, :] = grad_keys
                else:
                    value_sum[start:end, :] += grad_values
                    key_sum[start:end, :] += grad_keys
            for r in range(ratio):
                columns = slice(r * HD, (r + 1) * HD)
                back, gain_part = normal_rope_back(
                    grad_query[r * block : (r + 1) * block] * scale,
                    mixed_ref[low:high, columns],
                    query_inverse[r][low:high],
                    gain_q,
                    cos[low:high],
                    sin[low:high],
                )
                out_ref[low:high, columns] = back.astype(bf16)
                grad_gain = grad_gain + gain_part
        dgq_ref[...] += grad_gain
        back, gain_part = normal_rope_back(
            key_sum[...] * scale, raw_keys, key_inverse, gk_ref[...], cos, sin
        )
        dgk_ref[...] += gain_part
        out_ref[:, ratio * HD : (ratio + 1) * HD] = back.astype(bf16)
        out_ref[:, (ratio + 1) * HD :] = value_sum[...].astype(bf16)

    return pl.pallas_call(
        kernel,
        grid=(heads,),
        in_specs=[
            pl.BlockSpec((rows, wide), lambda i: (0, part * 2 + i)),
            pl.BlockSpec((rows, HD), lambda i: (0, 0)),
            pl.BlockSpec((rows, HD), lambda i: (0, 0)),
            pl.BlockSpec((1, HD), lambda i: (0, 0)),
            pl.BlockSpec((1, HD), lambda i: (0, 0)),
            pl.BlockSpec((rows, ratio * HD), lambda i: (0, i * parts + part)),
            pl.BlockSpec((rows, HD), lambda i: (0, part * 2 + i)),
            pl.BlockSpec((rows, ratio * HD), lambda i: (0, i * parts + part)),
        ],
        out_specs=[
            pl.BlockSpec((rows, wide), lambda i: (0, i)),
            pl.BlockSpec((1, HD), lambda i: (0, 0)),
            pl.BlockSpec((1, HD), lambda i: (0, 0)),
        ],
        out_shape=[
            jax.ShapeDtypeStruct((rows, heads * wide), bf16),
            jax.ShapeDtypeStruct((1, HD), f32),
            jax.ShapeDtypeStruct((1, HD), f32),
        ],
        scratch_shapes=[pltpu.VMEM((rows, HD), f32), pltpu.VMEM((rows, HD), f32)],
        compiler_params=pltpu.CompilerParams(vmem_limit_bytes=48 * 1024 * 1024),
        cost_estimate=SMALL,
        name="attend_backward",
    )(mixed, cosine, sine, gain_query, gain_key, attended, totals, grad_att)


def paired_shards(
    hidden_in,
    out_grad,
    stretch_order,
    positions,
    qkv_weight,
    qkv_moment,
    qkv_square,
    out_weight,
    out_moment,
    out_square,
    gateup_weight,
    gateup_moment,
    gateup_square,
    down_weight,
    down_moment,
    down_square,
    gain_weight,
    gain_moment,
    gain_square,
):
    groups = lax.axis_size("group")
    copies = lax.axis_size("dp")
    sequences, local_len, width = hidden_in.shape
    seq_len = local_len * groups
    pieces = stretch_order.shape[0]
    chunk = seq_len // pieces
    held = pieces // groups
    ratio = H // KV
    heads = 2 * KV // groups
    ff = FF // groups
    bf16 = jnp.bfloat16
    f32 = jnp.float32
    member = lax.axis_index("group")
    copy = lax.axis_index("dp")
    half = member // 2
    rank = member % 2
    side = copy % 2
    depth = copies // 2

    def permute(value, target):
        pairs = []
        for d in range(copies):
            for g in range(groups):
                to_d, to_g = target(d, g)
                pairs.append((d * groups + g, to_d * groups + to_g))
        return lax.ppermute(value, ALL, pairs)

    def over_core(value):
        return permute(value, lambda d, g: (d, g ^ 1))

    def over_chip(value):
        return permute(value, lambda d, g: (d, g ^ 2))

    def over_diagonal(value):
        return permute(value, lambda d, g: (d, g ^ 3))

    def over_side(value):
        return permute(value, lambda d, g: (d ^ 1, g))

    def block_of(far, other_rank):
        at = half if not far else 1 - half
        return at * 2 + (rank if not other_rank else 1 - rank)

    def pick(array, index):
        return lax.dynamic_index_in_dim(array, index, 0, keepdims=False)

    def ordered(first_side, mine, theirs):
        return jnp.concatenate(
            [jnp.where(first_side, mine, theirs), jnp.where(first_side, theirs, mine)]
        )

    table = jnp.arange(pieces, dtype=jnp.int32)

    def places_of(stored):
        return jnp.sum(
            jnp.where(stored[:, None] == table[None, :], stretch_order[None, :], 0), axis=1
        )

    slots = jnp.arange(pieces, dtype=jnp.int32)
    slot_rank = jnp.where(slots < 2 * held, rank, 1 - rank)
    slot_half = jnp.where(slots // held % 2 == 0, half, 1 - half)
    all_targets = places_of((slot_half * 2 + slot_rank) * held + slots % held)
    own_targets, peer_targets = all_targets[: 2 * held], all_targets[2 * held :]
    start = pick(positions, half)[0] - all_targets[0] * chunk
    exponent = jnp.arange(HD // 2, dtype=f32) * (2.0 / HD)
    inverse = jnp.power(jnp.float32(ROPE_BASE), -exponent)
    places = (start + jnp.arange(seq_len, dtype=jnp.int32)).astype(f32)
    angle = places[:, None] * inverse[None, :]
    cosine_half, sine_half = jnp.cos(angle), jnp.sin(angle)
    cosine = jnp.concatenate([cosine_half, cosine_half], axis=-1)
    sine = jnp.concatenate([-sine_half, sine_half], axis=-1)

    parts = 2
    wide = (ratio + 2) * HD
    some = ff // parts
    where_at = jnp.stack([half, rank, side]).astype(jnp.int32)

    class Columns:
        def __init__(self, array, rows_array, kinds):
            self.to_chip, self.to_diagonal, self.to_core, self.near, self.far, self.rows = (
                cut_columns(array, rows_array, where_at, kinds, parts)
            )

        def joined(self):
            return join_columns(
                self.near, self.far, self.peer, self.chip, self.diagonal,
                self.chip_side, self.diagonal_side, where_at, parts,
            )

    def join_rows(own, chip, other_side):
        return jnp.concatenate([own.astype(bf16), ordered(side == 0, chip, other_side)], axis=0)

    gain_rows = gain_weight.shape[0]
    gain_pad = jnp.pad(gain_weight.astype(bf16), (0, 16 * width - gain_rows)).reshape(16, width)
    hidden_sent = jnp.concatenate([pick(hidden_in, 1 - half), gain_pad], axis=0)
    hidden_far = over_chip(hidden_sent)
    block_cols = H * HD // groups
    key_cols = KV * HD // groups
    qkv = Columns(
        tie(qkv_weight, hidden_sent),
        out_weight,
        [(0, block_cols), (H * HD, key_cols), ((H + KV) * HD, key_cols)],
    )
    qkv_chip = over_chip(jnp.stack([qkv.to_chip, qkv.rows]))
    qkv.diagonal = over_diagonal(qkv.to_diagonal)
    qkv.peer = over_core(qkv.to_core)
    gateup = Columns(
        tie(gateup_weight, qkv.to_chip, qkv.to_diagonal), down_weight, [(0, ff), (FF, ff)]
    )
    gateup.chip = over_chip(tie(gateup.to_chip, hidden_far))
    hidden_mine = jnp.concatenate(
        [pick(hidden_in, half), hidden_far[:local_len], gain_pad, hidden_far[local_len:]], axis=0
    )
    hidden_theirs = over_core(hidden_mine)
    gain_low = gain_pad.reshape(-1)[:gain_rows]
    gain_parts = [
        block.reshape(-1)[:gain_rows]
        for block in (
            hidden_theirs[2 * local_len : 2 * local_len + 16],
            hidden_far[local_len:],
            hidden_theirs[2 * local_len + 16 :],
        )
    ]
    gains = ordered(
        half == 0,
        ordered(rank == 0, gain_low, gain_parts[0]),
        ordered(rank == 0, gain_parts[1], gain_parts[2]),
    ).astype(f32)
    gain_one = gains[:D]
    gain_two = gains[D : 2 * D]
    gain_query = gains[2 * D : 2 * D + HD].reshape(1, HD)
    gain_key = gains[2 * D + HD :].reshape(1, HD)

    gateup.peer = over_core(tie(gateup.to_core, qkv.peer))
    qkv_side = over_side(qkv_chip)
    gateup.diagonal = over_diagonal(tie(gateup.to_diagonal, qkv_chip))
    qkv.diagonal_side = over_side(qkv.diagonal)
    qkv.chip, qkv.chip_side = qkv_chip[0], qkv_side[0]
    w_out = join_rows(out_weight, qkv_chip[1], qkv_side[1])
    gateup.chip_side = over_side(gateup.chip)
    down_chip = over_chip(tie(gateup.rows, gateup.chip, qkv_side))
    gateup.diagonal_side = over_side(gateup.diagonal)
    grad_far = over_chip(tie(pick(out_grad, 1 - half), gateup.diagonal, qkv.diagonal_side))
    grad_mine = jnp.concatenate([pick(out_grad, half), grad_far], axis=0)
    grad_theirs = over_core(grad_mine)
    down_side = over_side(tie(down_chip, gateup.chip_side))

    hidden, normed_low = place_rows(hidden_mine, hidden_theirs, all_targets, chunk, gain_one)
    tokens = hidden.astype(f32)
    qkv.near = tie(qkv.near, gateup.chip)
    w_qkv = qkv.joined()
    mixed = split_product(normed_low, w_qkv, 1, 0)
    block = min(256, seq_len)
    attended, totals = attend_forward(
        tie(mixed, gateup.diagonal), cosine, sine, gain_query, gain_key, heads, ratio, block
    )
    branch = split_product(attended, w_out, 1, 0).astype(bf16)
    middle = tokens + (branch.astype(f32) + over_core(branch).astype(f32))
    second, pull_two = jax.vjp(rms_scale, middle, gain_two)
    second_low = second.astype(bf16)
    w_gateup = gateup.joined()
    gate_up = split_product(second_low, w_gateup, 1, 0)

    def gated_part(values, part):
        pieces_here = []
        for far in range(2):
            low = (part * 2 + far) * 2 * some
            pieces_here.append(
                jax.nn.silu(values[:, low : low + some]) * values[:, low + some : low + 2 * some]
            )
        return pieces_here

    def gated_all(values):
        found = [gated_part(values, part) for part in range(parts)]
        return jnp.concatenate(
            [found[part][far] for far in range(2) for part in range(parts)], axis=1
        )

    inner, pull_gate = jax.vjp(gated_all, gate_up)
    inner_low = inner.astype(bf16)
    (grad_result,) = place_rows(grad_mine, grad_theirs, all_targets, chunk, None)

    def half_columns(array, far):
        size = array.shape[1] // 2
        near_side = half == (1 if far else 0)
        return jnp.where(near_side, array[:, :size], array[:, size:])

    def far_columns(array, far):
        size = array.shape[1] // 2
        return array[:, size:] if far else array[:, :size]

    def far_first(array):
        size = array.shape[1] // 2
        return jnp.concatenate([array[:, size:], array[:, :size]], axis=1)

    def exchange(left_far, left_near, right):
        far = split_product(left_far, right, 0, 0).astype(bf16)
        received = over_chip(far)
        near = split_product(left_near, right, 0, 0).astype(bf16)
        return near, received

    def add(first, *others):
        total = first.astype(f32)
        for other in others:
            total = total + other.astype(f32)
        return total.astype(bf16)

    def swap_rows(near, received):
        received = far_first(received)
        lead = near.shape[0] // 2
        near = near.reshape(2, lead, -1)
        received = received.reshape(2, lead, -1)
        theirs = add(pick(near, 1 - rank), pick(received, 1 - rank))
        mine = add(pick(near, rank), pick(received, rank))
        return jnp.stack([mine, over_core(theirs)])

    def side_sum(value):
        value = value.reshape(2, depth, -1, value.shape[-1])
        return add(pick(value, side), over_side(pick(value, 1 - side)))

    token = [None]

    def event(*values):
        if token[0] is None:
            return values
        return lax.optimization_barrier((*values, token[0]))[: len(values)]

    def passed(value):
        token[0] = value

    w_down = join_rows(down_weight, down_chip, down_side)
    down_near, down_received = exchange(
        far_columns(inner_low, True), far_columns(inner_low, False), grad_result
    )
    grad_inner = split_product(tie(grad_result, down_near), w_down, 1, 1)
    (grad_gate_up,) = pull_gate(grad_inner)
    grad_gate_low = grad_gate_up.astype(bf16)
    second_near, second_far = half_columns(second_low, False), half_columns(second_low, True)
    part_cols = grad_gate_low.shape[1] // parts
    gateup_sent = [
        exchange(second_far, second_near, grad_gate_low[:, part * part_cols : (part + 1) * part_cols])
        for part in range(parts)
    ]
    second_part = split_product(grad_gate_low, w_gateup, 1, 1).astype(bf16)
    grad_second = second_part.astype(f32) + over_core(second_part).astype(f32)
    result_part = split_product(inner_low, w_down, 1, 0).astype(bf16)
    grad_mid_part, grad_gain_two = pull_two(grad_second)
    grad_middle = grad_result.astype(f32) + grad_mid_part
    grad_branch_low = grad_middle.astype(bf16)
    out_far = split_product(far_columns(attended, True), grad_branch_low, 0, 0).astype(bf16)
    out_near = split_product(far_columns(attended, False), grad_branch_low, 0, 0).astype(bf16)
    grad_att = split_product(grad_branch_low, w_out, 1, 1).astype(bf16)
    normed_near, normed_far = half_columns(normed_low, False), half_columns(normed_low, True)

    def share_rows(part):
        return take_rows(part, own_targets, chunk).astype(f32) + over_core(
            take_rows(part, peer_targets, chunk)
        ).astype(f32)

    def to_stored(rows_here):
        stored = rows_here.astype(bf16).reshape(2, local_len, width)
        from_far = over_chip(stored[1])
        first = jnp.where(half == 0, stored[0], from_far)
        last = jnp.where(half == 0, from_far, stored[0])
        return jnp.stack([first, last])

    def backward_part(part, grad_att):
        grad_part, grad_query_part, grad_key_part = attend_backward(
            mixed, cosine, sine, gain_query, gain_key, attended, totals, grad_att,
            part, parts, ratio, block,
        )
        return grad_part, grad_query_part[0], grad_key_part[0]

    levels = [(side, over_side)]
    near_step = 1
    while near_step < depth:
        levels.append(
            (
                copy // 2 // near_step % 2,
                lambda value, step=near_step: permute(
                    value, lambda d, g: ((d // 2 ^ step) * 2 + d % 2, g)
                ),
            )
        )
        near_step *= 2

    class Summed:
        def __init__(self, near, received):
            near, received = event(near, received)
            self.value = swap_rows(near, received)
            passed(self.value)
            self.level = 0
            self.down = True
            self.send_half()

        def send_half(self):
            bit, move = levels[self.level]
            halves = self.value.reshape(2, -1, self.value.shape[-1])
            self.kept = pick(halves, bit)
            self.received = move(pick(halves, 1 - bit))

        def send_back(self):
            self.received = levels[self.level][1](self.value)

        def step(self):
            if self.down:
                self.value = add(*event(self.kept, self.received))
                self.level += 1
                passed(self.value)
                if self.level < len(levels):
                    self.send_half()
                    return
                self.down = False
            else:
                value, received = event(self.value, self.received)
                self.value = ordered(levels[self.level][0] == 0, value, received)
                passed(self.value)
            self.level -= 1
            if self.level >= 0:
                self.send_back()

    def all_sum(near, received):
        value = add(*event(near, received))
        passed(value)
        return lax.psum(value, "dp")

    down_sum = all_sum(down_near, tie(down_received, grad_att))
    grad_att = tie(grad_att, token[0])
    back_0 = backward_part(0, grad_att)
    qkv_0 = exchange(normed_far, normed_near, back_0[0])
    back_1 = backward_part(1, tie(grad_att, qkv_0[0]))
    qkv_1 = exchange(normed_far, normed_near, back_1[0])
    out_far = tie(out_far, qkv_1[0])
    out_received = over_chip(tie(out_far, gateup_sent[0][1]))
    gateup_0 = Summed(gateup_sent[0][0], tie(gateup_sent[0][1], qkv_1[0]))
    normed_part = split_product(
        tie(back_0[0], token[0]), w_qkv[:, : 2 * wide], 1, 1
    ) + split_product(tie(back_1[0], token[0]), w_qkv[:, 2 * wide :], 1, 1)
    normed_part = normed_part.astype(bf16)
    gateup_0.received = tie(gateup_0.received, normed_part)
    gateup_0.step()
    gateup_1 = Summed(*gateup_sent[1])
    grad_normed = share_rows(normed_part)
    own_tokens = take_rows(hidden, own_targets, chunk).astype(f32)
    unused, pull_one = jax.vjp(rms_scale, own_tokens, gain_one)
    grad_token_part, grad_gain_one = pull_one(grad_normed)
    input_rows = (take_rows(grad_middle, own_targets, chunk) + grad_token_part).astype(bf16)
    gateup_0.step()
    gateup_1.step()
    gateup_0.step()
    summed_0 = Summed(*qkv_0)
    gateup_0.step()
    gateup_1.step()
    (down_sum,) = event(down_sum)
    passed(down_sum)
    summed_0.step()
    gateup_0.step()
    gateup_1.step()
    summed_1 = Summed(*qkv_1)
    summed_0.step()
    gateup_1.step()
    gateup_0.step()
    summed_1.step()
    out_sum = all_sum(out_near, out_received)
    summed_0.step()
    gateup_1.step()
    summed_1.step()
    summed_0.step()
    gateup_1.step()
    summed_1.step()
    summed_0.step()
    counted = jnp.where(rank == 0, 1.0, 0.0).astype(f32)
    total_gains = jnp.concatenate(
        [
            grad_gain_one,
            grad_gain_two * counted,
            back_0[1] + back_1[1],
            back_0[2] + back_1[2],
        ]
    )
    layer_out = to_stored(
        take_rows(middle, own_targets, chunk) + share_rows(tie(result_part, token[0]))
    )
    input_grad = to_stored(tie(input_rows, token[0]))
    for move in (over_core, over_chip):
        total_gains = total_gains + move(tie(total_gains, token[0]))
    summed_1.step()
    for bit, move in levels:
        total_gains = total_gains + move(tie(total_gains, token[0]))
    summed_0.step()
    summed_1.step()
    for summed in (gateup_0, gateup_1, summed_0, summed_1):
        while summed.level >= 0:
            summed.step()
    gateup_sums = [gateup_0.value, gateup_1.value]
    qkv_sums = [summed_0.value, summed_1.value]
    total_down = down_sum.astype(f32)
    total_out = out_sum.astype(f32)

    def owner_blocks(totals_of_parts):
        blocks = []
        for block_number in range(groups):
            far = (block_number // 2) ^ half
            peer = (block_number % 2) ^ rank
            for total in totals_of_parts:
                lead = total.shape[0] // 2
                cols = total.shape[1] // 2
                stacked = total.reshape(2, lead, 2 * cols)
                rows_here = pick(stacked, peer)
                blocks.append(jnp.where(far == 0, rows_here[:, :cols], rows_here[:, cols:]))
        return blocks

    gateup_blocks = owner_blocks(gateup_sums)
    total_gateup = jnp.concatenate(
        [blocked[:, :some] for blocked in gateup_blocks]
        + [blocked[:, some:] for blocked in gateup_blocks],
        axis=1,
    ).astype(f32)
    head_blocks = owner_blocks(qkv_sums)
    total_qkv = jnp.concatenate(
        [blocked[:, : ratio * HD] for blocked in head_blocks]
        + [blocked[:, ratio * HD : (ratio + 1) * HD] for blocked in head_blocks]
        + [blocked[:, (ratio + 1) * HD :] for blocked in head_blocks],
        axis=1,
    ).astype(f32)
    total_gain = lax.dynamic_slice_in_dim(total_gains, member * gain_rows, gain_rows, 0)

    out_fan = H * HD * 8 // seq_len
    qkv_new = adam_step(qkv_weight, qkv_moment, qkv_square, total_qkv, LR_MULT * D ** (-0.5), DECAY)
    out_new = adam_step(
        out_weight, out_moment, out_square, total_out, LR_MULT * out_fan ** (-0.5), DECAY
    )
    gateup_new = adam_step(
        gateup_weight, gateup_moment, gateup_square, total_gateup, LR_MULT * D ** (-0.5), DECAY
    )
    down_new = adam_step(
        down_weight, down_moment, down_square, total_down, LR_MULT * FF ** (-0.5), DECAY
    )
    gain_new = adam_step(gain_weight, gain_moment, gain_square, total_gain, GAIN_RATE, 0.0)
    return (layer_out, input_grad, *qkv_new, *out_new, *gateup_new, *down_new, *gain_new)


def shards(hidden_in, *others):
    groups = lax.axis_size("group")
    copies = lax.axis_size("dp")
    two_ranks = hidden_in.shape[0] == 2 and groups == 4
    if two_ranks and copies % 2 == 0:
        return paired_shards(hidden_in, *others)
    return general_shards(hidden_in, *others)


def solution(mesh):
    return jax.shard_map(
        shards,
        mesh=mesh,
        in_specs=(
            P("dp", "group", None),
            P("dp", "group", None),
            P(),
            P("dp", "group"),
            P("group", None),
            P("group", None),
            P("group", None),
            P("group", None),
            P("group", None),
            P("group", None),
            P("group", None),
            P("group", None),
            P("group", None),
            P("group", None),
            P("group", None),
            P("group", None),
            P("group"),
            P("group"),
            P("group"),
        ),
        out_specs=(
            P("dp", "group", None),
            P("dp", "group", None),
            P("group", None),
            P("group", None),
            P("group", None),
            P("group", None),
            P("group", None),
            P("group", None),
            P("group", None),
            P("group", None),
            P("group", None),
            P("group", None),
            P("group", None),
            P("group", None),
            P("group"),
            P("group"),
            P("group"),
        ),
        check_vma=False,
    )
```

```python
import jax
import jax.numpy as jnp
from jax import lax
from jax.experimental import pallas as pl
from jax.experimental.pallas import tpu as pltpu
from jax.sharding import PartitionSpec as P

D = 1024
H = 16
KV = 8
HD = 128
FF = 3072
STEP = 10


EPSILON = 1e-06
ROPE_BASE = 1000000.0
BETA_ONE = 0.9
BETA_TWO = 0.95
ADAM_EPSILON = 1e-08
DECAY = 0.1
LR_MULT = 3.0
GAIN_RATE = 0.3
MASKED = -1e30
START_TOP = -1e29


def rms_scale(values, gain):
    mean_square = jnp.mean(values * values, axis=-1, keepdims=True)
    return values * lax.rsqrt(mean_square + EPSILON) * gain


def rotate(values, cosine, sine):
    half = values.shape[-1] // 2
    turned = jnp.concatenate([-values[..., half:], values[..., :half]], axis=-1)
    return values * cosine + turned * sine


def rope_tables(places):
    exponent = jnp.arange(HD // 2, dtype=jnp.float32) * (2.0 / HD)
    inverse = jnp.power(jnp.float32(ROPE_BASE), -exponent)
    angle = places.astype(jnp.float32)[:, None] * inverse[None, :]
    angle = jnp.concatenate([angle, angle], axis=-1)
    return (jnp.cos(angle), jnp.sin(angle))


def split_heads(mixed, query_gain, key_gain, cosine, sine):
    row_count = mixed.shape[0]
    query = mixed[:, : H * HD].reshape(row_count, H, HD)
    keys = mixed[:, H * HD : (H + KV) * HD].reshape(row_count, KV, HD)
    values = mixed[:, (H + KV) * HD :].reshape(row_count, KV, HD)
    query = rotate(rms_scale(query, query_gain), cosine[:, None, :], sine[:, None, :])
    keys = rotate(rms_scale(keys, key_gain), cosine[:, None, :], sine[:, None, :])
    return (query, keys, values)


def gated(gate_up):
    half = gate_up.shape[1] // 2
    return jax.nn.silu(gate_up[:, :half]) * gate_up[:, half:]


def real_places(stretch_list, start, count, half_stretch):
    stored = start + jnp.arange(count, dtype=jnp.int32)
    piece_index = stored // half_stretch
    table = jnp.arange(stretch_list.shape[0], dtype=jnp.int32)
    picked = jnp.sum(
        jnp.where(piece_index[:, None] == table[None, :], stretch_list[None, :], 0), axis=1
    )
    return picked * half_stretch + stored % half_stretch


def by_blocks(block_fn, carry, piece, width):
    count = piece[0].shape[1]

    def advance(state, number):
        sliced = tuple(
            (lax.dynamic_slice_in_dim(member, number * width, width, 1) for member in piece)
        )
        return (block_fn(state, sliced, number * width), None)

    state, unused = lax.scan(advance, carry, jnp.arange(count // width, dtype=jnp.int32))
    return state


def adam_step(weight, moment, square, grad, rate, decay):
    moment_new = BETA_ONE * moment + (1.0 - BETA_ONE) * grad
    square_new = BETA_TWO * square + (1.0 - BETA_TWO) * grad * grad
    ratio = (
        moment_new
        / (1.0 - BETA_ONE**STEP)
        / (jnp.sqrt(square_new / (1.0 - BETA_TWO**STEP)) + ADAM_EPSILON)
    )
    return (weight - rate * (ratio + decay * weight), moment_new, square_new)


def general_shards(
    hidden_in,
    out_grad,
    stretch_order,
    positions,
    qkv_weight,
    qkv_moment,
    qkv_square,
    out_weight,
    out_moment,
    out_square,
    gateup_weight,
    gateup_moment,
    gateup_square,
    down_weight,
    down_moment,
    down_square,
    gain_weight,
    gain_moment,
    gain_square,
):
    groups = lax.axis_size("group")
    sequences, local_len, width = hidden_in.shape
    half_stretch = local_len // 2
    seq_len = local_len * groups
    ratio = H // KV
    row_count = sequences * local_len
    scale = HD ** (-0.5)
    bf16 = jnp.bfloat16
    f32 = jnp.float32
    w_qkv, w_out, w_gateup, w_down, gains_low = (
        lax.all_gather(qkv_weight.astype(bf16), "group", axis=0, tiled=True),
        lax.all_gather(out_weight.astype(bf16), "group", axis=0, tiled=True),
        lax.all_gather(gateup_weight.astype(bf16), "group", axis=0, tiled=True),
        lax.all_gather(down_weight.astype(bf16), "group", axis=0, tiled=True),
        lax.all_gather(gain_weight.astype(bf16), "group", axis=0, tiled=True),
    )
    gains = gains_low.astype(f32)
    gain_one = gains[:D]
    gain_two = gains[D : 2 * D]
    gain_query = gains[2 * D : 2 * D + HD]
    gain_key = gains[2 * D + HD :]
    member = lax.axis_index("group")
    query_places = real_places(stretch_order, member * local_len, local_len, half_stretch)
    cosine, sine = rope_tables(positions.reshape(row_count))
    tokens = hidden_in.reshape(row_count, width).astype(f32)
    normed, pull_one = jax.vjp(rms_scale, tokens, gain_one)
    normed_low = normed.astype(bf16)
    mixed = jnp.dot(normed_low, w_qkv, preferred_element_type=f32)

    def heads_of(mixed_rows, query_gain, key_gain):
        return split_heads(mixed_rows, query_gain, key_gain, cosine, sine)

    (query, keys, values), pull_heads = jax.vjp(heads_of, mixed, gain_query, gain_key)
    query_low = query.astype(bf16).reshape(sequences, local_len, KV, ratio, HD)
    keys_low = keys.astype(bf16).reshape(sequences, local_len, KV, HD)
    values_low = values.astype(bf16).reshape(sequences, local_len, KV, HD)

    def scores_for(keys_piece, start):
        count = keys_piece.shape[1]
        key_places = real_places(stretch_order, start, count, half_stretch)
        allowed = key_places[None, :] <= query_places[:, None]
        raw_scores = (
            jnp.einsum("sqkrd,spkd->skrqp", query_low, keys_piece, preferred_element_type=f32)
            * scale
        )
        return jnp.where(allowed, raw_scores, MASKED)

    def forward_block(carry, piece, start):
        top_old, total_old, accum_old = carry
        scores = scores_for(piece[0], start)
        top_new = jnp.maximum(top_old, jnp.max(scores, axis=-1))
        factor = jnp.exp(top_old - top_new)
        exp_terms = jnp.exp(scores - top_new[..., None])
        total_new = total_old * factor + jnp.sum(exp_terms, axis=-1)
        update = jnp.einsum(
            "skrqp,spkd->skrqd", exp_terms.astype(bf16), piece[1], preferred_element_type=f32
        )
        return (top_new, total_new, accum_old * factor[..., None] + update)

    start_state = (
        jnp.full((sequences, KV, ratio, local_len), START_TOP, f32),
        jnp.zeros((sequences, KV, ratio, local_len), f32),
        jnp.zeros((sequences, KV, ratio, local_len, HD), f32),
    )
    top, total, accum = by_blocks(
        forward_block,
        start_state,
        (
            lax.all_gather(keys_low, "group", axis=1, tiled=True),
            lax.all_gather(values_low, "group", axis=1, tiled=True),
        ),
        local_len,
    )
    attended = accum / total[..., None]
    log_total = top + jnp.log(total)
    attended_low = jnp.transpose(attended, (0, 3, 1, 2, 4)).reshape(row_count, H * HD).astype(bf16)
    middle = tokens + jnp.dot(attended_low, w_out, preferred_element_type=f32)
    second, pull_two = jax.vjp(rms_scale, middle, gain_two)
    second_low = second.astype(bf16)
    gate_up = jnp.dot(second_low, w_gateup, preferred_element_type=f32)
    inner, pull_gate = jax.vjp(gated, gate_up)
    inner_low = inner.astype(bf16)
    result = middle + jnp.dot(inner_low, w_down, preferred_element_type=f32)
    layer_out = result.astype(bf16).reshape(sequences, local_len, width)
    grad_result_low = out_grad.reshape(row_count, width)
    grad_down = jnp.einsum("ti,to->io", inner_low, grad_result_low, preferred_element_type=f32)
    grad_inner = jnp.einsum("to,io->ti", grad_result_low, w_down, preferred_element_type=f32)
    (grad_gate_up,) = pull_gate(grad_inner)
    grad_gate_low = grad_gate_up.astype(bf16)
    grad_gateup = jnp.einsum("td,tf->df", second_low, grad_gate_low, preferred_element_type=f32)
    grad_second = jnp.einsum("tf,df->td", grad_gate_low, w_gateup, preferred_element_type=f32)
    grad_mid_part, grad_gain_two = pull_two(grad_second)
    grad_middle = grad_result_low.astype(f32) + grad_mid_part
    grad_branch_low = grad_middle.astype(bf16)
    grad_out = jnp.einsum("ta,td->ad", attended_low, grad_branch_low, preferred_element_type=f32)
    grad_att = jnp.einsum("td,ad->ta", grad_branch_low, w_out, preferred_element_type=f32).astype(
        bf16
    )
    grad_att_heads = jnp.transpose(
        grad_att.reshape(sequences, local_len, KV, ratio, HD), (0, 2, 3, 1, 4)
    )
    delta = jnp.sum(grad_att_heads.astype(f32) * attended, axis=-1)

    def backward_block(carry, piece, start):
        grad_query, grad_pairs = carry
        keys_piece, values_piece = piece
        count = keys_piece.shape[1]
        scores = scores_for(keys_piece, start)
        probs = jnp.exp(scores - log_total[..., None])
        grad_values = jnp.einsum(
            "skrqp,skrqd->spkd", probs.astype(bf16), grad_att_heads, preferred_element_type=f32
        )
        grad_probs = jnp.einsum(
            "skrqd,spkd->skrqp", grad_att_heads, values_piece, preferred_element_type=f32
        )
        grad_scores = (probs * (grad_probs - delta[..., None])).astype(bf16)
        grad_query = (
            grad_query
            + jnp.einsum("skrqp,spkd->skrqd", grad_scores, keys_piece, preferred_element_type=f32)
            * scale
        )
        grad_keys = (
            jnp.einsum("skrqp,sqkrd->spkd", grad_scores, query_low, preferred_element_type=f32)
            * scale
        )
        current = lax.dynamic_slice_in_dim(grad_pairs, start, count, 1)
        joined = current + jnp.concatenate([grad_keys, grad_values], axis=-1)
        return (grad_query, lax.dynamic_update_slice_in_dim(grad_pairs, joined, start, 1))

    back_state = (
        jnp.zeros((sequences, KV, ratio, local_len, HD), f32),
        jnp.zeros((sequences, seq_len, KV, 2 * HD), f32),
    )
    grad_query, grad_pairs = by_blocks(
        backward_block,
        back_state,
        (
            lax.all_gather(keys_low, "group", axis=1, tiled=True),
            lax.all_gather(values_low, "group", axis=1, tiled=True),
        ),
        local_len,
    )
    grad_local = lax.psum_scatter(
        grad_pairs.astype(jnp.bfloat16), "group", scatter_dimension=1, tiled=True
    ).astype(jnp.float32)
    grad_keys = grad_local[..., :HD].reshape(row_count, KV, HD)
    grad_values = grad_local[..., HD:].reshape(row_count, KV, HD)
    grad_query = jnp.transpose(grad_query, (0, 3, 1, 2, 4)).reshape(row_count, H, HD)
    grad_mixed, grad_gain_query, grad_gain_key = pull_heads((grad_query, grad_keys, grad_values))
    grad_mixed_low = grad_mixed.astype(bf16)
    grad_qkv = jnp.einsum("td,tc->dc", normed_low, grad_mixed_low, preferred_element_type=f32)
    grad_normed = jnp.einsum("tc,dc->td", grad_mixed_low, w_qkv, preferred_element_type=f32)
    grad_token_part, grad_gain_one = pull_one(grad_normed)
    input_grad = (grad_middle + grad_token_part).astype(bf16).reshape(sequences, local_len, width)
    grad_gains = jnp.concatenate([grad_gain_one, grad_gain_two, grad_gain_query, grad_gain_key])
    part_qkv, part_out, part_gateup, part_down, part_gain = (
        lax.psum_scatter(
            grad_qkv.astype(jnp.bfloat16), "group", scatter_dimension=0, tiled=True
        ).astype(jnp.float32),
        lax.psum_scatter(
            grad_out.astype(jnp.bfloat16), "group", scatter_dimension=0, tiled=True
        ).astype(jnp.float32),
        lax.psum_scatter(
            grad_gateup.astype(jnp.bfloat16), "group", scatter_dimension=0, tiled=True
        ).astype(jnp.float32),
        lax.psum_scatter(
            grad_down.astype(jnp.bfloat16), "group", scatter_dimension=0, tiled=True
        ).astype(jnp.float32),
        lax.psum_scatter(
            grad_gains.astype(jnp.bfloat16), "group", scatter_dimension=0, tiled=True
        ).astype(jnp.float32),
    )
    total_qkv, total_out, total_gateup, total_down, total_gain = (
        lax.psum(part_qkv.astype(jnp.bfloat16), "dp").astype(jnp.float32),
        lax.psum(part_out.astype(jnp.bfloat16), "dp").astype(jnp.float32),
        lax.psum(part_gateup.astype(jnp.bfloat16), "dp").astype(jnp.float32),
        lax.psum(part_down.astype(jnp.bfloat16), "dp").astype(jnp.float32),
        lax.psum(part_gain.astype(jnp.bfloat16), "dp").astype(jnp.float32),
    )
    out_fan = H * HD * 8 // seq_len
    qkv_new = adam_step(qkv_weight, qkv_moment, qkv_square, total_qkv, LR_MULT * D ** (-0.5), DECAY)
    out_new = adam_step(
        out_weight, out_moment, out_square, total_out, LR_MULT * out_fan ** (-0.5), DECAY
    )
    gateup_new = adam_step(
        gateup_weight, gateup_moment, gateup_square, total_gateup, LR_MULT * D ** (-0.5), DECAY
    )
    down_new = adam_step(
        down_weight, down_moment, down_square, total_down, LR_MULT * FF ** (-0.5), DECAY
    )
    gain_new = adam_step(gain_weight, gain_moment, gain_square, total_gain, GAIN_RATE, 0.0)
    return (
        layer_out,
        input_grad,
        qkv_new[0],
        qkv_new[1],
        qkv_new[2],
        out_new[0],
        out_new[1],
        out_new[2],
        gateup_new[0],
        gateup_new[1],
        gateup_new[2],
        down_new[0],
        down_new[1],
        down_new[2],
        gain_new[0],
        gain_new[1],
        gain_new[2],
    )


ALL = ("dp", "group")
LOG2E = 1.4426950408889634
SMALL = pl.CostEstimate(flops=1000000, bytes_accessed=100000, transcendentals=0)


def tie(value, *others):
    return lax.optimization_barrier((value, *others))[0]


def split_product(left, right, left_dim, right_dim):
    return lax.dot_general(
        left, right, (((left_dim,), (right_dim,)), ((), ())), preferred_element_type=jnp.float32
    )


def place_rows(mine, theirs, targets, chunk, gain):
    count = targets.shape[0]
    width = mine.shape[1]
    near = mine.shape[0] // chunk
    with_norm = gain is not None

    def kernel(targets_ref, mine_ref, theirs_ref, *refs):
        step = pl.program_id(0)
        rows = jnp.where(step < near, mine_ref[...], theirs_ref[...])
        if with_norm:
            gain_ref, placed, normed = refs
            wide = rows.astype(jnp.float32)
            normed[...] = rms_scale(wide, gain_ref[...]).astype(jnp.bfloat16)
        else:
            (placed,) = refs
        placed[...] = rows

    def target_row(i, targets_ref):
        return (targets_ref[i], 0)

    in_specs = [
        pl.BlockSpec((chunk, width), lambda i, targets_ref: (jnp.minimum(i, near - 1), 0)),
        pl.BlockSpec((chunk, width), lambda i, targets_ref: (jnp.maximum(i - near, 0), 0)),
    ]
    operands = [mine, theirs]
    outputs = 1
    if with_norm:
        in_specs.append(pl.BlockSpec((1, width), lambda i, targets_ref: (0, 0)))
        operands.append(gain.reshape(1, width))
        outputs = 2
    shape = jax.ShapeDtypeStruct((count * chunk, width), mine.dtype)
    return pl.pallas_call(
        kernel,
        out_shape=[shape] * outputs,
        grid_spec=pltpu.PrefetchScalarGridSpec(
            num_scalar_prefetch=1,
            grid=(count,),
            in_specs=in_specs,
            out_specs=[pl.BlockSpec((chunk, width), target_row)] * outputs,
        ),
        cost_estimate=SMALL,
        name="place_rows",
    )(targets, *operands)


def cut_columns(array, rows_array, where_at, kinds, parts):
    lead, total = array.shape
    groups = 4
    kept = total // groups
    rows_lead, rows_width = rows_array.shape

    def kernel(at_ref, *refs):
        sources = refs[: len(kinds)]
        rows_ref = refs[len(kinds)]
        chip, diagonal, core, near, far, rows_out = refs[len(kinds) + 1 :]
        step = pl.program_id(0)
        for number, target in enumerate(
            (chip, diagonal, core.at[0], core.at[1], near, far)
        ):

            @pl.when(step == number)
            def _(target=target):
                low = 0
                for part in range(parts):
                    for source, (first, size) in zip(sources, kinds):
                        width = size // parts
                        target[:, low : low + width] = source[
                            :, part * width : (part + 1) * width
                        ].astype(jnp.bfloat16)
                        low += width

        @pl.when(step == 0)
        def _():
            rows_out[...] = rows_ref[...].astype(jnp.bfloat16)

    def block_at(step, at_ref):
        half, rank, side = at_ref[0], at_ref[1], at_ref[2]
        sent = jnp.where(side == 0, 1 - half, half)
        pair = jnp.where(
            step < 2, sent, jnp.where((step == 2) | (step == 4), half, 1 - half)
        )
        other = (step == 1) | (step == 2) | (step == 3)
        return pair * 2 + jnp.where(other, 1 - rank, rank)

    def source_spec(first, size):
        return pl.BlockSpec(
            (lead, size), lambda i, at_ref: (0, first // size + block_at(i, at_ref))
        )

    flat = pl.BlockSpec((lead, kept), lambda i, at_ref: (0, 0))
    pair = pl.BlockSpec((2, lead, kept), lambda i, at_ref: (0, 0, 0))
    half_rows = (rows_lead // 2, rows_width)
    single = jax.ShapeDtypeStruct((lead, kept), jnp.bfloat16)
    return pl.pallas_call(
        kernel,
        out_shape=[
            single,
            single,
            jax.ShapeDtypeStruct((2, lead, kept), jnp.bfloat16),
            single,
            single,
            jax.ShapeDtypeStruct(half_rows, jnp.bfloat16),
        ],
        grid_spec=pltpu.PrefetchScalarGridSpec(
            num_scalar_prefetch=1,
            grid=(6,),
            in_specs=[source_spec(first, size) for first, size in kinds]
            + [pl.BlockSpec(half_rows, lambda i, at_ref: (at_ref[2], 0))],
            out_specs=[flat, flat, pair, flat, flat]
            + [pl.BlockSpec(half_rows, lambda i, at_ref: (0, 0))],
        ),
        compiler_params=pltpu.CompilerParams(vmem_limit_bytes=48 * 1024 * 1024),
        cost_estimate=SMALL,
        name="cut_columns",
    )(where_at, *([array] * len(kinds)), rows_array)


def join_columns(own_near, own_far, peer, chip, diagonal, chip_side, diagonal_side, where_at, parts):
    lead, cols = own_near.shape
    width = cols // parts

    def kernel(
        at_ref, near_ref, far_ref, peer_ref, chip_ref, diag_ref, chip_x_ref, diag_x_ref, out_ref
    ):
        step = pl.program_id(0)
        same_half = step // 2 == at_ref[0]
        same_rank = step % 2 == at_ref[1]
        even = at_ref[2] == 0

        def put(condition, first, second):
            @pl.when(condition)
            def _():
                for part in range(parts):
                    columns = slice(part * width, (part + 1) * width)
                    low = 2 * part * width
                    out_ref[:, low : low + width] = first[:, columns]
                    out_ref[:, low + width : low + 2 * width] = second[:, columns]

        put(same_half & same_rank, near_ref, far_ref)
        put(same_half & ~same_rank, peer_ref.at[0], peer_ref.at[1])
        put(~same_half & same_rank & even, chip_ref, chip_x_ref)
        put(~same_half & same_rank & ~even, chip_x_ref, chip_ref)
        put(~same_half & ~same_rank & even, diag_ref, diag_x_ref)
        put(~same_half & ~same_rank & ~even, diag_x_ref, diag_ref)

    flat = pl.BlockSpec((lead, cols), lambda i, at_ref: (0, 0))
    pair = pl.BlockSpec((2, lead, cols), lambda i, at_ref: (0, 0, 0))
    return pl.pallas_call(
        kernel,
        out_shape=jax.ShapeDtypeStruct((4 * lead, 2 * cols), own_near.dtype),
        grid_spec=pltpu.PrefetchScalarGridSpec(
            num_scalar_prefetch=1,
            grid=(4,),
            in_specs=[flat, flat, pair, flat, flat, flat, flat],
            out_specs=pl.BlockSpec((lead, 2 * cols), lambda i, at_ref: (i, 0)),
        ),
        compiler_params=pltpu.CompilerParams(vmem_limit_bytes=48 * 1024 * 1024),
        cost_estimate=SMALL,
        name="join_columns",
    )(where_at, own_near, own_far, peer, chip, diagonal, chip_side, diagonal_side)


def take_rows(rows, sources, chunk):
    return jnp.concatenate(
        [
            lax.dynamic_slice_in_dim(rows, sources[number] * chunk, chunk, 0)
            for number in range(sources.shape[0])
        ],
        axis=0,
    )


def normal_rope(raw, gain, cosine, sine):
    inverse = lax.rsqrt(jnp.mean(raw * raw, axis=-1, keepdims=True) + EPSILON)
    scaled = raw * inverse * gain
    return scaled * cosine + pltpu.roll(scaled, HD // 2, 1) * sine, inverse


def normal_rope_back(grad, raw, inverse, gain, cosine, sine):
    grad_scaled = grad * cosine + pltpu.roll(grad * sine, HD // 2, 1)
    unit = raw * inverse
    grad_gain = jnp.sum(grad_scaled * unit, axis=0, keepdims=True)
    weighted = grad_scaled * gain
    shift = jnp.mean(weighted * unit, axis=-1, keepdims=True)
    return inverse * (weighted - unit * shift), grad_gain


def causal_mask(block, ratio):
    row = lax.broadcasted_iota(jnp.int32, (ratio * block, block), 0) % block
    column = lax.broadcasted_iota(jnp.int32, (ratio * block, block), 1)
    return column <= row


def attend_forward(mixed, cosine, sine, gain_query, gain_key, heads, ratio, block):
    rows = mixed.shape[0]
    wide = (ratio + 2) * HD
    factor = HD ** (-0.5) * LOG2E
    bf16 = jnp.bfloat16
    f32 = jnp.float32

    def kernel(mixed_ref, cos_ref, sin_ref, gq_ref, gk_ref, att_ref, total_ref):
        cos = cos_ref[...]
        sin = sin_ref[...]
        query = [
            normal_rope(mixed_ref[:, r * HD : (r + 1) * HD], gq_ref[...], cos, sin)[0].astype(bf16)
            for r in range(ratio)
        ]
        keys = normal_rope(mixed_ref[:, ratio * HD : (ratio + 1) * HD], gk_ref[...], cos, sin)[0]
        keys = keys.astype(bf16)
        values = mixed_ref[:, (ratio + 1) * HD :].astype(bf16)
        values = jnp.concatenate([values, jnp.ones((rows, HD), bf16)], axis=1)
        allowed = causal_mask(block, ratio)
        lane = lax.broadcasted_iota(jnp.int32, (block, HD), 1)
        for number in range(rows // block):
            low, high = number * block, (number + 1) * block
            stacked = jnp.concatenate([part[low:high] for part in query], axis=0)
            scores = split_product(stacked, keys[low:high], 1, 1)
            terms = jnp.where(allowed, jnp.exp2(scores * factor), 0.0).astype(bf16)
            joined = split_product(terms, values[low:high], 1, 0)
            if low:
                scores = split_product(stacked, keys[:low], 1, 1)
                terms = jnp.exp2(scores * factor).astype(bf16)
                joined = joined + split_product(terms, values[:low], 1, 0)
            total = joined[:, HD:]
            result = (joined[:, :HD] / total).astype(bf16)
            kept = total[:block]
            for r in range(ratio):
                att_ref[low:high, r * HD : (r + 1) * HD] = result[r * block : (r + 1) * block]
                if r:
                    kept = jnp.where(
                        lane >= r * (HD // ratio), total[r * block : (r + 1) * block], kept
                    )
            total_ref[low:high, :] = kept

    return pl.pallas_call(
        kernel,
        grid=(heads,),
        in_specs=[
            pl.BlockSpec((rows, wide), lambda i: (0, i)),
            pl.BlockSpec((rows, HD), lambda i: (0, 0)),
            pl.BlockSpec((rows, HD), lambda i: (0, 0)),
            pl.BlockSpec((1, HD), lambda i: (0, 0)),
            pl.BlockSpec((1, HD), lambda i: (0, 0)),
        ],
        out_specs=[
            pl.BlockSpec((rows, ratio * HD), lambda i: (0, i % 2 * (heads // 2) + i // 2)),
            pl.BlockSpec((rows, HD), lambda i: (0, i)),
        ],
        out_shape=[
            jax.ShapeDtypeStruct((rows, heads * ratio * HD), bf16),
            jax.ShapeDtypeStruct((rows, heads * HD), f32),
        ],
        compiler_params=pltpu.CompilerParams(vmem_limit_bytes=48 * 1024 * 1024),
        cost_estimate=SMALL,
        name="attend_forward",
    )(mixed, cosine, sine, gain_query, gain_key)


def attend_backward(
    mixed, cosine, sine, gain_query, gain_key, attended, totals, grad_att, part, parts, ratio, block
):
    heads = 2
    rows = mixed.shape[0]
    wide = (ratio + 2) * HD
    scale = HD ** (-0.5)
    factor = scale * LOG2E
    bf16 = jnp.bfloat16
    f32 = jnp.float32

    def kernel(
        mixed_ref, cos_ref, sin_ref, gq_ref, gk_ref, att_ref, total_ref, grad_ref,
        out_ref, dgq_ref, dgk_ref, key_sum, value_sum,
    ):
        cos = cos_ref[...]
        sin = sin_ref[...]
        gain_q = gq_ref[...]
        query = []
        query_inverse = []
        for r in range(ratio):
            turned, inverse = normal_rope(mixed_ref[:, r * HD : (r + 1) * HD], gain_q, cos, sin)
            query.append(turned.astype(bf16))
            query_inverse.append(inverse)
        raw_keys = mixed_ref[:, ratio * HD : (ratio + 1) * HD]
        keys, key_inverse = normal_rope(raw_keys, gk_ref[...], cos, sin)
        keys = keys.astype(bf16)
        values = mixed_ref[:, (ratio + 1) * HD :].astype(bf16)
        allowed = causal_mask(block, ratio)
        grad_gain = jnp.zeros((1, HD), f32)

        @pl.when(pl.program_id(0) == 0)
        def _():
            dgq_ref[...] = jnp.zeros_like(dgq_ref)
            dgk_ref[...] = jnp.zeros_like(dgk_ref)

        for number in reversed(range(rows // block)):
            low, high = number * block, (number + 1) * block
            stacked = jnp.concatenate([turned[low:high] for turned in query], axis=0)
            grads = []
            deltas = []
            for r in range(ratio):
                lane = r * (HD // ratio)
                inverse = 1.0 / total_ref[low:high, lane : lane + 1]
                columns = slice(r * HD, (r + 1) * HD)
                scaled = (grad_ref[low:high, columns].astype(f32) * inverse).astype(bf16)
                grads.append(scaled)
                deltas.append(
                    jnp.sum(
                        scaled.astype(f32) * att_ref[low:high, columns].astype(f32),
                        axis=-1,
                        keepdims=True,
                    )
                )
            grad = jnp.concatenate(grads, axis=0)
            delta = jnp.concatenate(deltas, axis=0)
            grad_query = None
            for start, end, masked in ((low, high, True), (0, low, False)):
                if end == start:
                    continue
                scores = split_product(stacked, keys[start:end], 1, 1)
                terms = jnp.exp2(scores * factor)
                if masked:
                    terms = jnp.where(allowed, terms, 0.0)
                grad_terms = split_product(grad, values[start:end], 1, 1)
                grad_scores = (terms * (grad_terms - delta)).astype(bf16)
                grad_values = split_product(terms.astype(bf16), grad, 0, 0)
                grad_keys = split_product(grad_scores, stacked, 0, 0)
                added = split_product(grad_scores, keys[start:end], 1, 0)
                grad_query = added if grad_query is None else grad_query + added
                if number == rows // block - 1:
                    value_sum[start:end, :] = grad_values
                    key_sum[start:end, :] = grad_keys
                else:
                    value_sum[start:end, :] += grad_values
                    key_sum[start:end, :] += grad_keys
            for r in range(ratio):
                columns = slice(r * HD, (r + 1) * HD)
                back, gain_part = normal_rope_back(
                    grad_query[r * block : (r + 1) * block] * scale,
                    mixed_ref[low:high, columns],
                    query_inverse[r][low:high],
                    gain_q,
                    cos[low:high],
                    sin[low:high],
                )
                out_ref[low:high, columns] = back.astype(bf16)
                grad_gain = grad_gain + gain_part
        dgq_ref[...] += grad_gain
        back, gain_part = normal_rope_back(
            key_sum[...] * scale, raw_keys, key_inverse, gk_ref[...], cos, sin
        )
        dgk_ref[...] += gain_part
        out_ref[:, ratio * HD : (ratio + 1) * HD] = back.astype(bf16)
        out_ref[:, (ratio + 1) * HD :] = value_sum[...].astype(bf16)

    return pl.pallas_call(
        kernel,
        grid=(heads,),
        in_specs=[
            pl.BlockSpec((rows, wide), lambda i: (0, part * 2 + i)),
            pl.BlockSpec((rows, HD), lambda i: (0, 0)),
            pl.BlockSpec((rows, HD), lambda i: (0, 0)),
            pl.BlockSpec((1, HD), lambda i: (0, 0)),
            pl.BlockSpec((1, HD), lambda i: (0, 0)),
            pl.BlockSpec((rows, ratio * HD), lambda i: (0, i * parts + part)),
            pl.BlockSpec((rows, HD), lambda i: (0, part * 2 + i)),
            pl.BlockSpec((rows, ratio * HD), lambda i: (0, i * parts + part)),
        ],
        out_specs=[
            pl.BlockSpec((rows, wide), lambda i: (0, i)),
            pl.BlockSpec((1, HD), lambda i: (0, 0)),
            pl.BlockSpec((1, HD), lambda i: (0, 0)),
        ],
        out_shape=[
            jax.ShapeDtypeStruct((rows, heads * wide), bf16),
            jax.ShapeDtypeStruct((1, HD), f32),
            jax.ShapeDtypeStruct((1, HD), f32),
        ],
        scratch_shapes=[pltpu.VMEM((rows, HD), f32), pltpu.VMEM((rows, HD), f32)],
        compiler_params=pltpu.CompilerParams(vmem_limit_bytes=48 * 1024 * 1024),
        cost_estimate=SMALL,
        name="attend_backward",
    )(mixed, cosine, sine, gain_query, gain_key, attended, totals, grad_att)


def paired_shards(
    hidden_in,
    out_grad,
    stretch_order,
    positions,
    qkv_weight,
    qkv_moment,
    qkv_square,
    out_weight,
    out_moment,
    out_square,
    gateup_weight,
    gateup_moment,
    gateup_square,
    down_weight,
    down_moment,
    down_square,
    gain_weight,
    gain_moment,
    gain_square,
):
    groups = lax.axis_size("group")
    copies = lax.axis_size("dp")
    sequences, local_len, width = hidden_in.shape
    seq_len = local_len * groups
    pieces = stretch_order.shape[0]
    chunk = seq_len // pieces
    held = pieces // groups
    ratio = H // KV
    heads = 2 * KV // groups
    ff = FF // groups
    bf16 = jnp.bfloat16
    f32 = jnp.float32
    member = lax.axis_index("group")
    copy = lax.axis_index("dp")
    half = member // 2
    rank = member % 2
    side = copy % 2
    depth = copies // 2

    def permute(value, target):
        pairs = []
        for d in range(copies):
            for g in range(groups):
                to_d, to_g = target(d, g)
                pairs.append((d * groups + g, to_d * groups + to_g))
        return lax.ppermute(value, ALL, pairs)

    def over_core(value):
        return permute(value, lambda d, g: (d, g ^ 1))

    def over_chip(value):
        return permute(value, lambda d, g: (d, g ^ 2))

    def over_diagonal(value):
        return permute(value, lambda d, g: (d, g ^ 3))

    def over_side(value):
        return permute(value, lambda d, g: (d ^ 1, g))

    def block_of(far, other_rank):
        at = half if not far else 1 - half
        return at * 2 + (rank if not other_rank else 1 - rank)

    def pick(array, index):
        return lax.dynamic_index_in_dim(array, index, 0, keepdims=False)

    def ordered(first_side, mine, theirs):
        return jnp.concatenate(
            [jnp.where(first_side, mine, theirs), jnp.where(first_side, theirs, mine)]
        )

    table = jnp.arange(pieces, dtype=jnp.int32)

    def places_of(stored):
        return jnp.sum(
            jnp.where(stored[:, None] == table[None, :], stretch_order[None, :], 0), axis=1
        )

    slots = jnp.arange(pieces, dtype=jnp.int32)
    slot_rank = jnp.where(slots < 2 * held, rank, 1 - rank)
    slot_half = jnp.where(slots // held % 2 == 0, half, 1 - half)
    all_targets = places_of((slot_half * 2 + slot_rank) * held + slots % held)
    own_targets, peer_targets = all_targets[: 2 * held], all_targets[2 * held :]
    start = pick(positions, half)[0] - all_targets[0] * chunk
    exponent = jnp.arange(HD // 2, dtype=f32) * (2.0 / HD)
    inverse = jnp.power(jnp.float32(ROPE_BASE), -exponent)
    places = (start + jnp.arange(seq_len, dtype=jnp.int32)).astype(f32)
    angle = places[:, None] * inverse[None, :]
    cosine_half, sine_half = jnp.cos(angle), jnp.sin(angle)
    cosine = jnp.concatenate([cosine_half, cosine_half], axis=-1)
    sine = jnp.concatenate([-sine_half, sine_half], axis=-1)

    parts = 2
    wide = (ratio + 2) * HD
    some = ff // parts
    where_at = jnp.stack([half, rank, side]).astype(jnp.int32)

    class Columns:
        def __init__(self, array, rows_array, kinds):
            self.to_chip, self.to_diagonal, self.to_core, self.near, self.far, self.rows = (
                cut_columns(array, rows_array, where_at, kinds, parts)
            )

        def joined(self):
            return join_columns(
                self.near, self.far, self.peer, self.chip, self.diagonal,
                self.chip_side, self.diagonal_side, where_at, parts,
            )

    def join_rows(own, chip, other_side):
        return jnp.concatenate([own.astype(bf16), ordered(side == 0, chip, other_side)], axis=0)

    gain_rows = gain_weight.shape[0]
    gain_pad = jnp.pad(gain_weight.astype(bf16), (0, 16 * width - gain_rows)).reshape(16, width)
    hidden_sent = jnp.concatenate([pick(hidden_in, 1 - half), gain_pad], axis=0)
    hidden_far = over_chip(hidden_sent)
    block_cols = H * HD // groups
    key_cols = KV * HD // groups
    qkv = Columns(
        tie(qkv_weight, hidden_sent),
        out_weight,
        [(0, block_cols), (H * HD, key_cols), ((H + KV) * HD, key_cols)],
    )
    qkv_chip = over_chip(jnp.stack([qkv.to_chip, qkv.rows]))
    qkv.diagonal = over_diagonal(qkv.to_diagonal)
    qkv.peer = over_core(qkv.to_core)
    gateup = Columns(
        tie(gateup_weight, qkv.to_chip, qkv.to_diagonal), down_weight, [(0, ff), (FF, ff)]
    )
    gateup.chip = over_chip(tie(gateup.to_chip, hidden_far))
    hidden_mine = jnp.concatenate(
        [pick(hidden_in, half), hidden_far[:local_len], gain_pad, hidden_far[local_len:]], axis=0
    )
    hidden_theirs = over_core(hidden_mine)
    gain_low = gain_pad.reshape(-1)[:gain_rows]
    gain_parts = [
        block.reshape(-1)[:gain_rows]
        for block in (
            hidden_theirs[2 * local_len : 2 * local_len + 16],
            hidden_far[local_len:],
            hidden_theirs[2 * local_len + 16 :],
        )
    ]
    gains = ordered(
        half == 0,
        ordered(rank == 0, gain_low, gain_parts[0]),
        ordered(rank == 0, gain_parts[1], gain_parts[2]),
    ).astype(f32)
    gain_one = gains[:D]
    gain_two = gains[D : 2 * D]
    gain_query = gains[2 * D : 2 * D + HD].reshape(1, HD)
    gain_key = gains[2 * D + HD :].reshape(1, HD)

    gateup.peer = over_core(tie(gateup.to_core, qkv.peer))
    qkv_side = over_side(qkv_chip)
    gateup.diagonal = over_diagonal(tie(gateup.to_diagonal, qkv_chip))
    qkv.diagonal_side = over_side(qkv.diagonal)
    qkv.chip, qkv.chip_side = qkv_chip[0], qkv_side[0]
    w_out = join_rows(out_weight, qkv_chip[1], qkv_side[1])
    gateup.chip_side = over_side(gateup.chip)
    down_chip = over_chip(tie(gateup.rows, gateup.chip, qkv_side))
    gateup.diagonal_side = over_side(gateup.diagonal)
    grad_far = over_chip(tie(pick(out_grad, 1 - half), gateup.diagonal, qkv.diagonal_side))
    grad_mine = jnp.concatenate([pick(out_grad, half), grad_far], axis=0)
    grad_theirs = over_core(grad_mine)
    down_side = over_side(tie(down_chip, gateup.chip_side))

    hidden, normed_low = place_rows(hidden_mine, hidden_theirs, all_targets, chunk, gain_one)
    tokens = hidden.astype(f32)
    qkv.near = tie(qkv.near, gateup.chip)
    w_qkv = qkv.joined()
    mixed = split_product(tie(normed_low, gateup.peer), w_qkv, 1, 0)
    block = min(256, seq_len)
    attended, totals = attend_forward(
        tie(mixed, gateup.diagonal, gateup.chip_side), cosine, sine, gain_query, gain_key, heads, ratio, block
    )
    pinned = tie(attended, gateup.diagonal_side, down_chip)
    branch = split_product(pinned, w_out, 1, 0).astype(bf16)
    middle = tokens + (branch.astype(f32) + over_core(branch).astype(f32))
    second, pull_two = jax.vjp(rms_scale, middle, gain_two)
    second_low = second.astype(bf16)
    gateup.near = tie(gateup.near, grad_far)
    w_gateup = gateup.joined()
    gate_up = split_product(tie(second_low, down_side), w_gateup, 1, 0)

    def gated_part(values, part):
        pieces_here = []
        for far in range(2):
            low = (part * 2 + far) * 2 * some
            pieces_here.append(
                jax.nn.silu(values[:, low : low + some]) * values[:, low + some : low + 2 * some]
            )
        return pieces_here

    def gated_all(values):
        found = [gated_part(values, part) for part in range(parts)]
        return jnp.concatenate(
            [found[part][far] for far in range(2) for part in range(parts)], axis=1
        )

    inner, pull_gate = jax.vjp(gated_all, gate_up)
    inner_low = inner.astype(bf16)
    (grad_result,) = place_rows(grad_mine, grad_theirs, all_targets, chunk, None)

    def half_columns(array, far):
        size = array.shape[1] // 2
        near_side = half == (1 if far else 0)
        return jnp.where(near_side, array[:, :size], array[:, size:])

    def far_columns(array, far):
        size = array.shape[1] // 2
        return array[:, size:] if far else array[:, :size]

    def far_first(array):
        size = array.shape[1] // 2
        return jnp.concatenate([array[:, size:], array[:, :size]], axis=1)

    def exchange(left_far, left_near, right):
        far = split_product(left_far, right, 0, 0).astype(bf16)
        received = over_chip(far)
        near = split_product(left_near, right, 0, 0).astype(bf16)
        return near, received

    def add(first, *others):
        total = first.astype(f32)
        for other in others:
            total = total + other.astype(f32)
        return total.astype(bf16)

    def swap_rows(near, received):
        received = far_first(received)
        lead = near.shape[0] // 2
        near = near.reshape(2, lead, -1)
        received = received.reshape(2, lead, -1)
        theirs = add(pick(near, 1 - rank), pick(received, 1 - rank))
        mine = add(pick(near, rank), pick(received, rank))
        return jnp.stack([mine, over_core(theirs)])

    def side_sum(value):
        value = value.reshape(2, depth, -1, value.shape[-1])
        return add(pick(value, side), over_side(pick(value, 1 - side)))

    token = [None]

    def event(*values):
        if token[0] is None:
            return values
        return lax.optimization_barrier((*values, token[0]))[: len(values)]

    def passed(value):
        token[0] = value

    def all_sum(near, received):
        value = add(*event(near, received))
        passed(value)
        return lax.psum(value, "dp")

    w_down = join_rows(down_weight, down_chip, down_side)
    down_near, down_received = exchange(
        far_columns(inner_low, True), far_columns(inner_low, False), grad_result
    )
    grad_inner = split_product(tie(grad_result, down_near), w_down, 1, 1)
    (grad_gate_up,) = pull_gate(grad_inner)
    grad_gate_low = grad_gate_up.astype(bf16)
    down_sum = all_sum(down_near, down_received)
    sent_low = tie(grad_gate_low, token[0])
    second_near, second_far = half_columns(second_low, False), half_columns(second_low, True)
    part_cols = grad_gate_low.shape[1] // parts
    gateup_sent = [
        exchange(second_far, second_near, sent_low[:, part * part_cols : (part + 1) * part_cols])
        for part in range(parts)
    ]
    second_part = split_product(grad_gate_low, w_gateup, 1, 1).astype(bf16)
    grad_second = second_part.astype(f32) + over_core(second_part).astype(f32)
    result_part = split_product(inner_low, w_down, 1, 0).astype(bf16)
    grad_mid_part, grad_gain_two = pull_two(grad_second)
    grad_middle = grad_result.astype(f32) + grad_mid_part
    grad_branch_low = grad_middle.astype(bf16)
    out_far = split_product(far_columns(attended, True), grad_branch_low, 0, 0).astype(bf16)
    out_near = split_product(far_columns(attended, False), grad_branch_low, 0, 0).astype(bf16)
    grad_att = split_product(grad_branch_low, w_out, 1, 1).astype(bf16)
    normed_near, normed_far = half_columns(normed_low, False), half_columns(normed_low, True)

    def share_rows(part):
        return take_rows(part, own_targets, chunk).astype(f32) + over_core(
            take_rows(part, peer_targets, chunk)
        ).astype(f32)

    def to_stored(rows_here):
        stored = rows_here.astype(bf16).reshape(2, local_len, width)
        from_far = over_chip(stored[1])
        first = jnp.where(half == 0, stored[0], from_far)
        last = jnp.where(half == 0, from_far, stored[0])
        return jnp.stack([first, last])

    def backward_part(part, grad_att):
        grad_part, grad_query_part, grad_key_part = attend_backward(
            mixed, cosine, sine, gain_query, gain_key, attended, totals, grad_att,
            part, parts, ratio, block,
        )
        return grad_part, grad_query_part[0], grad_key_part[0]

    levels = [(side, over_side)]
    near_step = 1
    while near_step < depth:
        levels.append(
            (
                copy // 2 // near_step % 2,
                lambda value, step=near_step: permute(
                    value, lambda d, g: ((d // 2 ^ step) * 2 + d % 2, g)
                ),
            )
        )
        near_step *= 2

    class Summed:
        def __init__(self, near, received):
            near, received = event(near, received)
            self.value = swap_rows(near, received)
            passed(self.value)
            self.level = 0
            self.down = True
            self.send_half()

        def send_half(self):
            bit, move = levels[self.level]
            halves = self.value.reshape(2, -1, self.value.shape[-1])
            self.kept = pick(halves, bit)
            self.received = move(pick(halves, 1 - bit))

        def send_back(self):
            self.received = levels[self.level][1](self.value)

        def step(self):
            if self.down:
                self.value = add(*event(self.kept, self.received))
                self.level += 1
                passed(self.value)
                if self.level < len(levels):
                    self.send_half()
                    return
                self.down = False
            else:
                value, received = event(self.value, self.received)
                self.value = ordered(levels[self.level][0] == 0, value, received)
                passed(self.value)
            self.level -= 1
            if self.level >= 0:
                self.send_back()

    out_received = over_chip(out_far)
    back_0 = backward_part(0, grad_att)
    qkv_0 = exchange(normed_far, normed_near, back_0[0])
    back_1 = backward_part(1, tie(grad_att, qkv_0[0]))
    far_1 = split_product(normed_far, back_1[0], 0, 0).astype(bf16)
    near_1 = split_product(normed_near, back_1[0], 0, 0).astype(bf16)
    gateup_0 = Summed(gateup_sent[0][0], tie(gateup_sent[0][1], near_1))
    qkv_1 = (near_1, over_chip(tie(far_1, token[0])))
    normed_part = split_product(
        tie(back_0[0], token[0]), w_qkv[:, : 2 * wide], 1, 1
    ) + split_product(tie(back_1[0], token[0]), w_qkv[:, 2 * wide :], 1, 1)
    normed_part = normed_part.astype(bf16)
    gateup_0.received = tie(gateup_0.received, normed_part)
    gateup_0.step()
    gateup_1 = Summed(*gateup_sent[1])
    grad_normed = share_rows(normed_part)
    own_tokens = take_rows(hidden, own_targets, chunk).astype(f32)
    unused, pull_one = jax.vjp(rms_scale, own_tokens, gain_one)
    grad_token_part, grad_gain_one = pull_one(grad_normed)
    input_rows = (take_rows(grad_middle, own_targets, chunk) + grad_token_part).astype(bf16)
    counted = jnp.where(rank == 0, 1.0, 0.0).astype(f32)
    gain_state = [
        jnp.concatenate(
            [
                grad_gain_one,
                grad_gain_two * counted,
                back_0[1] + back_1[1],
                back_0[2] + back_1[2],
            ]
        )
    ]
    gain_moves = [over_core, over_chip] + [move for bit, move in levels]

    def gain_step():
        if len(gain_state) > 1:
            value, received = event(*gain_state)
            gain_state[:] = [value + received]
            passed(gain_state[0])
        if gain_moves:
            gain_state.append(gain_moves.pop(0)(gain_state[0]))

    gateup_0.step()
    gateup_1.step()
    gateup_0.step()
    gain_step()
    gateup_0.step()
    gateup_1.step()
    (down_sum,) = event(down_sum)
    passed(down_sum)
    out_sum = all_sum(out_near, out_received)
    summed_0 = Summed(*qkv_0)
    gain_step()
    gateup_0.step()
    gateup_1.step()
    summed_0.step()
    gain_step()
    gateup_1.step()
    summed_1 = Summed(*qkv_1)
    layer_out = to_stored(
        take_rows(middle, own_targets, chunk) + share_rows(tie(result_part, back_0[0]))
    )
    input_grad = to_stored(tie(input_rows, token[0]))
    gateup_0.step()
    gateup_1.step()
    summed_0.step()
    gain_step()
    summed_1.step()
    summed_0.step()
    gateup_1.step()
    summed_1.step()
    gain_step()
    summed_0.step()
    summed_1.step()
    gain_step()
    summed_0.step()
    summed_1.step()
    summed_1.step()
    summed_0.step()
    for summed in (gateup_0, gateup_1, summed_0, summed_1):
        while summed.level >= 0:
            summed.step()
    while len(gain_state) > 1:
        gain_step()
    total_gains = gain_state[0]
    gateup_sums = [gateup_0.value, gateup_1.value]
    qkv_sums = [summed_0.value, summed_1.value]
    total_down = down_sum.astype(f32)
    total_out = out_sum.astype(f32)

    def owner_blocks(totals_of_parts):
        blocks = []
        for block_number in range(groups):
            far = (block_number // 2) ^ half
            peer = (block_number % 2) ^ rank
            for total in totals_of_parts:
                lead = total.shape[0] // 2
                cols = total.shape[1] // 2
                stacked = total.reshape(2, lead, 2 * cols)
                rows_here = pick(stacked, peer)
                blocks.append(jnp.where(far == 0, rows_here[:, :cols], rows_here[:, cols:]))
        return blocks

    gateup_blocks = owner_blocks(gateup_sums)
    total_gateup = jnp.concatenate(
        [blocked[:, :some] for blocked in gateup_blocks]
        + [blocked[:, some:] for blocked in gateup_blocks],
        axis=1,
    ).astype(f32)
    head_blocks = owner_blocks(qkv_sums)
    total_qkv = jnp.concatenate(
        [blocked[:, : ratio * HD] for blocked in head_blocks]
        + [blocked[:, ratio * HD : (ratio + 1) * HD] for blocked in head_blocks]
        + [blocked[:, (ratio + 1) * HD :] for blocked in head_blocks],
        axis=1,
    ).astype(f32)
    total_gain = lax.dynamic_slice_in_dim(total_gains, member * gain_rows, gain_rows, 0)

    out_fan = H * HD * 8 // seq_len
    qkv_new = adam_step(qkv_weight, qkv_moment, qkv_square, total_qkv, LR_MULT * D ** (-0.5), DECAY)
    out_new = adam_step(
        out_weight, out_moment, out_square, total_out, LR_MULT * out_fan ** (-0.5), DECAY
    )
    gateup_new = adam_step(
        gateup_weight, gateup_moment, gateup_square, total_gateup, LR_MULT * D ** (-0.5), DECAY
    )
    down_new = adam_step(
        down_weight, down_moment, down_square, total_down, LR_MULT * FF ** (-0.5), DECAY
    )
    gain_new = adam_step(gain_weight, gain_moment, gain_square, total_gain, GAIN_RATE, 0.0)
    return (layer_out, input_grad, *qkv_new, *out_new, *gateup_new, *down_new, *gain_new)


def shards(hidden_in, *others):
    groups = lax.axis_size("group")
    copies = lax.axis_size("dp")
    two_ranks = hidden_in.shape[0] == 2 and groups == 4
    if two_ranks and copies % 2 == 0:
        return paired_shards(hidden_in, *others)
    return general_shards(hidden_in, *others)


def solution(mesh):
    return jax.shard_map(
        shards,
        mesh=mesh,
        in_specs=(
            P("dp", "group", None),
            P("dp", "group", None),
            P(),
            P("dp", "group"),
            P("group", None),
            P("group", None),
            P("group", None),
            P("group", None),
            P("group", None),
            P("group", None),
            P("group", None),
            P("group", None),
            P("group", None),
            P("group", None),
            P("group", None),
            P("group", None),
            P("group"),
            P("group"),
            P("group"),
        ),
        out_specs=(
            P("dp", "group", None),
            P("dp", "group", None),
            P("group", None),
            P("group", None),
            P("group", None),
            P("group", None),
            P("group", None),
            P("group", None),
            P("group", None),
            P("group", None),
            P("group", None),
            P("group", None),
            P("group", None),
            P("group", None),
            P("group"),
            P("group"),
            P("group"),
        ),
        check_vma=False,
    )
```
